32 devices in a mesh: grp: 2 (over y), slc: 4 (over z), coil: 2 (over x), vol: 2 (over core).
Axes of the slice: x: 2, y: 2, z: 4, core: 2. Of those that a mesh axis runs over, the one named last changes fastest.
Arguments:
- images: bfloat16 [4, 32, 2, 220, 220], P(('grp', 'vol'), 'slc'), parts along dimension 0, may hold values from -6 to 6
- coil_maps: bfloat16 [8, 32, 2, 220, 220], P(('grp', 'coil'), 'slc'), parts along dimension 0, may hold values from -3 to 3
- kspace: bfloat16 [4, 4, 4, 2, 220, 220], P(('grp', 'vol'), 'slc', 'coil'), parts along dimension 0, may hold values from -12 to 12
- shift_index: int32 [32], P('slc'), may hold values from 0 to 7
- phase_offset: float32 [32, 220], P('slc'), may hold values from -3.140625 to 3.140625
- group_order: int32 [4], replicated, may hold values from 0 to 3, each once
Outputs:
- grad_phase: float32 [64, 220], P(('grp', 'slc')), parts along dimension 0
The draws below stay inside these ranges and needn't reach their ends.
There are 2 independent parts, one for each index of `grp`. The reference program is written for one: setup_inputs(seed, part) draws one part's arguments, and reference() takes and returns one part's arrays. A program takes and returns all parts, laid end to end along the dimension named above; an argument that names none is the same for every part. Nothing has to cross between parts.
Inputs may be any that keep to these rules, and one draw needn't show every extreme that they name: group_order names each of the 4 measured rows exactly once.
All inputs are finite; a program needn't handle non-finite values.
Results may differ from the reference program's by a relative error of at most 0.0096.
Values may be sent and summed in bfloat16 or wider, within the bound.
No kernel may reach another device: no remote copies, remote signals or barrier semaphores. Data moves between devices by JAX's collectives and lax.ppermute only.
A program may use at most 64 MiB of HBM per device.

```python
import math
import jax
import jax.numpy as jnp
from jax import lax

MATRIX = 220
MB = 8
COILS = 4
VOLS = 2
SLICES = 32
GROUPS = 4


def set_ends(drawn, key, low, largest):
    extent = drawn.shape
    place = [jax.random.randint(jax.random.fold_in(key, axis), (), 0, extent[axis]) for axis in range(len(extent))]
    drawn = drawn.at[tuple(place)].set(low)
    longest = extent.index(max(extent))
    place[longest] = (place[longest] + 1) % extent[longest]
    return drawn.at[tuple(place)].set(largest)


def level_of(rng, extent, split, low, largest):
    factor_of, own = 1.0, jax.random.fold_in(rng, 6)
    for position, blocks in split:
        steps = jnp.exp(jax.random.uniform(jax.random.fold_in(own, position), (blocks,), jnp.float32, low / len(split), largest / len(split)))
        factor_of = factor_of * jnp.repeat(steps, extent[position] // blocks).reshape([-1 if axis == position else 1 for axis in range(len(extent))])
    return factor_of


def centred(stream_key, shape, spread, bound, pieces=(), held_as=jnp.bfloat16):
    drawn = jax.random.normal(stream_key, shape, jnp.float32) * spread
    if len(pieces) > 0:
        drawn = level_of(stream_key, shape, pieces, -0.22, 0.18) * drawn
    return jnp.clip(drawn, min=-bound, max=bound).astype(held_as)


def setup_inputs(seed: int = 0, part: int = 0) -> dict:
    seeds = jax.random.split(jax.random.key(seed), 7)
    own_keys = jax.random.split(jax.random.fold_in(seeds[6], part), 7)
    return {
        "images": centred(own_keys[0], (VOLS, SLICES, 2, MATRIX, MATRIX), 1.0, 6.0, ((0, 2), (1, 4))),
        "coil_maps": centred(own_keys[1], (COILS, SLICES, 2, MATRIX, MATRIX), 0.5, 3.0, ((0, 2), (1, 4))),
        "kspace": centred(own_keys[2], (VOLS, GROUPS, COILS, 2, MATRIX, MATRIX), 2.0, 12.0, ((0, 2), (1, 4), (2, 2))),
        "shift_index": set_ends(jax.random.randint(seeds[3], (SLICES,), 0, MB), jax.random.fold_in(seeds[3], 1), 0, MB - 1).astype(jnp.int32),
        "phase_offset": jnp.clip(jax.random.uniform(seeds[4], (SLICES, MATRIX), jnp.float32, -3.140625, 3.140625), -3.140625, 3.140625),
        "group_order": jax.random.permutation(seeds[5], GROUPS).astype(jnp.int32),
    }


def to_half(values):
    return lax.optimization_barrier(values.astype(jnp.bfloat16)).astype(jnp.float32)

def fourier_tables(length):
    positions = jnp.arange(length, dtype=jnp.int32)
    product = positions[:, None] * positions[None, :] % length
    radians = 2.0 * math.pi / length * product.astype(jnp.float32)
    factor = 1.0 / math.sqrt(length)
    return ((jnp.cos(radians) * factor).astype(jnp.bfloat16), (-jnp.sin(radians) * factor).astype(jnp.bfloat16))

def slice_phases(shift_index, phase_offset, length):
    lines = (jnp.arange(length, dtype=jnp.int32) - length // 2).astype(jnp.float32)
    return 2.0 * math.pi / MB * (shift_index.astype(jnp.float32)[:, None] * lines[None, :]) + phase_offset

def reference(images, coil_maps, kspace, shift_index, phase_offset, group_order):
    hp = lax.Precision.HIGHEST
    cos_table, sin_table = fourier_tables(MATRIX)
    cos_full = cos_table.astype(jnp.float32)
    sin_full = sin_table.astype(jnp.float32)
    phase_angle = slice_phases(shift_index, phase_offset, MATRIX)
    cosine = jnp.cos(phase_angle)[None, :, :, None]
    sine = jnp.sin(phase_angle)[None, :, :, None]
    classes = jnp.arange(SLICES, dtype=jnp.int32) % GROUPS
    target = group_order[classes]
    onehot = (target[None, :] == jnp.arange(GROUPS, dtype=jnp.int32)[:, None]).astype(jnp.float32)
    image_re = images[:, :, 0].astype(jnp.float32)
    image_im = images[:, :, 1].astype(jnp.float32)

    def per_coil(packed):
        coil_map, measured = packed
        map_re = coil_map[:, 0].astype(jnp.float32)[None]
        map_im = coil_map[:, 1].astype(jnp.float32)[None]
        coil_re = to_half(map_re * image_re - map_im * image_im)
        coil_im = to_half(map_re * image_im + map_im * image_re)
        half_re = to_half(jnp.einsum('ky,vsyx->vskx', cos_full, coil_re, precision=hp) - jnp.einsum('ky,vsyx->vskx', sin_full, coil_im, precision=hp))
        half_im = to_half(jnp.einsum('ky,vsyx->vskx', cos_full, coil_im, precision=hp) + jnp.einsum('ky,vsyx->vskx', sin_full, coil_re, precision=hp))
        spec_re = jnp.einsum('vsyx,kx->vsyk', half_re, cos_full, precision=hp) - jnp.einsum('vsyx,kx->vsyk', half_im, sin_full, precision=hp)
        spec_im = jnp.einsum('vsyx,kx->vsyk', half_re, sin_full, precision=hp) + jnp.einsum('vsyx,kx->vsyk', half_im, cos_full, precision=hp)
        shift_re = to_half(spec_re * cosine - spec_im * sine)
        shift_im = to_half(spec_re * sine + spec_im * cosine)
        alias_re = jnp.einsum('gs,vsyx->vgyx', onehot, shift_re, precision=hp)
        alias_im = jnp.einsum('gs,vsyx->vgyx', onehot, shift_im, precision=hp)
        resid_re = to_half(alias_re - measured[:, :, 0].astype(jnp.float32))
        resid_im = to_half(alias_im - measured[:, :, 1].astype(jnp.float32))
        chosen_re = resid_re[:, target]
        chosen_im = resid_im[:, target]
        return lax.optimization_barrier(jnp.sum(chosen_im * shift_re - chosen_re * shift_im, axis=(0, 3)))
    per_coil_grad = lax.map(per_coil, (coil_maps, jnp.moveaxis(kspace, 2, 0)))
    return lax.optimization_barrier(jnp.sum(per_coil_grad, axis=0)) * (1.0 / (COILS * VOLS))
```

```python
import functools
import math

import jax
import jax.numpy as jnp
import ml_dtypes
import numpy as np
from jax import lax
from jax.experimental import pallas as pl
from jax.experimental.pallas import tpu as pltpu
from jax.sharding import PartitionSpec as P

MB = 8
ROW_TILE = 16
LANE_TILE = 128
ROW_PARTS = 2


def round_up(value, multiple):
    return -(-value // multiple) * multiple


def fourier_tables(length):
    positions = np.arange(length, dtype=np.int32)
    product = positions[:, None] * positions[None, :] % length
    radians = np.float32(2.0 * math.pi / length) * product.astype(np.float32)
    factor = np.float32(1.0 / math.sqrt(length))
    return (
        (np.cos(radians) * factor).astype(ml_dtypes.bfloat16),
        (-np.sin(radians) * factor).astype(ml_dtypes.bfloat16),
    )


def dft_matrices(length, rows):
    cos_table, sin_table = fourier_tables(length)
    cosine, sine = cos_table.astype(np.float64), sin_table.astype(np.float64)
    left_re = np.zeros((2 * rows, length), np.float64)
    left_im = np.zeros((2 * rows, length), np.float64)
    left_re[:length], left_re[rows : rows + length] = cosine, sine
    left_im[:length], left_im[rows : rows + length] = -sine, cosine
    gram_re = cosine.T @ cosine + sine.T @ sine
    gram_im = sine.T @ cosine - cosine.T @ sine
    gram = np.stack(
        [np.concatenate([gram_re, gram_im], 1), np.concatenate([-gram_im, gram_re], 1)]
    )
    adjoint = np.stack(
        [np.concatenate([cosine, -sine], 1), np.concatenate([sine, cosine], 1)]
    )
    left = np.stack([left_re, left_im])
    return tuple(part.astype(ml_dtypes.bfloat16) for part in (left, gram, adjoint))


def slice_phases(shift_index, phase_offset, length):
    lines = (jnp.arange(length, dtype=jnp.int32) - length // 2).astype(jnp.float32)
    return (
        2.0 * math.pi / MB * (shift_index.astype(jnp.float32)[:, None] * lines[None, :])
        + phase_offset
    )


def dot(left, right):
    return jnp.dot(left, right, preferred_element_type=jnp.float32)


def encode_kernel(slots, columns, masked, scalars, *refs):
    image_refs, refs = refs[:slots], refs[slots:]
    map_refs, refs = refs[:slots], refs[slots:]
    kspace_ref, phase_ref, left_ref, gram_ref, adjoint_ref = refs[:5]
    shifted_ref = refs[5]
    out_refs = refs[6:-1]
    total = refs[-1]
    vols, coils = image_refs[0].shape[0], map_refs[0].shape[0]
    length = image_refs[0].shape[-1]
    rows = shifted_ref.shape[-2]
    half = phase_ref.shape[1] // 2
    part = rows // len(out_refs)
    if total.shape[1] > vols * coils * 2 * length:
        total[...] = jnp.zeros_like(total)
    for vol in range(vols):
        for coil in range(coils):
            place = vol * coils + coil
            sum_re = sum_im = None
            for slot in range(slots):
                image_re = image_refs[slot][vol, 0, 0].astype(jnp.float32)
                image_im = image_refs[slot][vol, 0, 1].astype(jnp.float32)
                map_re = map_refs[slot][coil, 0, 0].astype(jnp.float32)
                map_im = map_refs[slot][coil, 0, 1].astype(jnp.float32)
                coil_re = (map_re * image_re - map_im * image_im).astype(jnp.bfloat16)
                coil_im = (map_re * image_im + map_im * image_re).astype(jnp.bfloat16)
                partly = dot(left_ref[0], coil_re) + dot(left_ref[1], coil_im)
                column = columns[slot]
                cosine = phase_ref[:, column : column + 1]
                sine = phase_ref[:, half + column : half + column + 1]
                part_re, part_im = partly[:rows], partly[rows:]
                shift_re = part_re * cosine - part_im * sine
                shift_im = part_re * sine + part_im * cosine
                shifted_ref[slot, place, 0] = shift_re.astype(jnp.bfloat16)
                shifted_ref[slot, place, 1] = shift_im.astype(jnp.bfloat16)
                sum_re = shift_re if slot == 0 else sum_re + shift_re
                sum_im = shift_im if slot == 0 else sum_im + shift_im
            mixed = dot(sum_re.astype(jnp.bfloat16), gram_ref[0]) + dot(
                sum_im.astype(jnp.bfloat16), gram_ref[1]
            )
            if masked:
                mixed = jnp.where(scalars[1] > 0, mixed, 0.0)
            total[:, place * 2 * length : (place + 1) * 2 * length] = mixed

    @pl.when(scalars[0] > 0)
    def _():
        for vol in range(vols):
            for coil in range(coils):
                place = vol * coils + coil
                measured = dot(kspace_ref[vol, 0, coil, 0], adjoint_ref[0]) + dot(
                    kspace_ref[vol, 0, coil, 1], adjoint_ref[1]
                )
                total[:length, place * 2 * length : (place + 1) * 2 * length] -= measured

    for index, out_ref in enumerate(out_refs):
        out_ref[...] = total[index * part : (index + 1) * part, :].astype(jnp.bfloat16)


def gradient_kernel(parts, terms, *refs):
    term_refs, shifted_ref, out_ref = refs[:-2], refs[-2], refs[-1]
    slots, places, _, rows, length = shifted_ref.shape
    part = rows // parts
    for index in range(parts):
        residual = None
        for ref in term_refs[index * terms : (index + 1) * terms]:
            value = ref[...].astype(jnp.float32)
            residual = value if residual is None else residual + value
        sums = [None] * slots
        for place in range(places):
            base = place * 2 * length
            resid_re = residual[:, base : base + length]
            resid_im = residual[:, base + length : base + 2 * length]
            for slot in range(slots):
                span = slice(index * part, (index + 1) * part)
                shift_re = shifted_ref[slot, place, 0, span, :].astype(jnp.float32)
                shift_im = shifted_ref[slot, place, 1, span, :].astype(jnp.float32)
                term = resid_im * shift_re - resid_re * shift_im
                sums[slot] = term if place == 0 else sums[slot] + term
        for slot in range(slots):
            out_ref[index, slot : slot + 1, :] = jnp.sum(sums[slot].T, axis=0, keepdims=True)


def chain_steps(count):
    for step in range(1, count):
        up, down = (step - 1, step), (count - step, count - step - 1)
        yield ([up, down],) if up[0] != down[0] else ([up], [down])


def chain_terms(value, axis):
    terms, payload = [value], value
    for rounds in chain_steps(lax.axis_size(axis)):
        arrived = [lax.ppermute(payload, axis, pairs) for pairs in rounds]
        received = functools.reduce(lambda a, b: a + b, arrived)
        terms.append(received)
        payload = value + received
    return terms


def body(images, coil_maps, kspace, shift_index, phase_offset, group_order):
    vols, per_device, _, _, length = images.shape
    coils = coil_maps.shape[0]
    groups = lax.axis_size("slc")
    position = lax.axis_index("slc")
    rows = round_up(length, ROW_TILE * ROW_PARTS)
    part = rows // ROW_PARTS
    places = vols * coils
    lanes = round_up(places * 2 * length, LANE_TILE)
    whole_classes = per_device % groups == 0
    slots = max(1, per_device // groups)
    left, gram, adjoint = dft_matrices(length, rows)

    phase_angle = jnp.pad(
        slice_phases(shift_index, phase_offset, length), ((0, 0), (0, rows - length))
    )
    phases = jnp.concatenate([jnp.cos(phase_angle), jnp.sin(phase_angle)], axis=0).T
    owned = (group_order == position).astype(jnp.int32)

    encoded, pieces = [], []
    for group in range(groups):
        if whole_classes:
            columns = [slot * groups + group for slot in range(slots)]
            scalars = jnp.stack([owned[group], jnp.int32(1)])
            places_of = [lambda i, scalars, w=w: (0, w, 0, 0, 0) for w in columns]
            group_phases = phases
        else:
            within = group - (position * per_device) % groups
            held = (within >= 0) & (within < per_device)
            within = jnp.where(held, within, 0).astype(jnp.int32)
            scalars = jnp.stack([owned[group], held.astype(jnp.int32), within])
            columns = [0]
            places_of = [lambda i, scalars: (0, scalars[2], 0, 0, 0)]
            group_phases = jnp.take(
                phases, jnp.stack([within, within + per_device]), axis=1
            )
        constant = lambda ndim: (lambda i, scalars: (0,) * ndim)
        whole = lambda array: pl.BlockSpec(array.shape, constant(array.ndim))
        outputs = pl.pallas_call(
            functools.partial(encode_kernel, slots, columns, not whole_classes),
            grid_spec=pltpu.PrefetchScalarGridSpec(
                num_scalar_prefetch=1,
                grid=(1,),
                in_specs=[
                    pl.BlockSpec((vols, 1, 2, length, length), place) for place in places_of
                ]
                + [pl.BlockSpec((coils, 1, 2, length, length), place) for place in places_of]
                + [whole(kspace), whole(group_phases), whole(left), whole(gram), whole(adjoint)],
                out_specs=[
                    pl.BlockSpec((slots, places, 2, rows, length), constant(5)),
                ]
                + [pl.BlockSpec((part, lanes), constant(2))] * ROW_PARTS,
                scratch_shapes=[pltpu.VMEM((rows, lanes), jnp.float32)],
            ),
            out_shape=[
                jax.ShapeDtypeStruct((slots, places, 2, rows, length), jnp.bfloat16),
            ]
            + [jax.ShapeDtypeStruct((part, lanes), jnp.bfloat16)] * ROW_PARTS,
            compiler_params=pltpu.CompilerParams(vmem_limit_bytes=40 * 1024 * 1024),
            cost_estimate=pl.CostEstimate(
                flops=places * (slots + 1) * 16 * length**3,
                bytes_accessed=6_000_000,
                transcendentals=0,
            ),
            name="encode",
        )(
            scalars,
            *([images] * slots),
            *([coil_maps] * slots),
            kspace,
            group_phases,
            left,
            gram,
            adjoint,
        )
        encoded.append(outputs[0])
        pieces.append(outputs[1:])

    gradients = []
    for group in range(groups):
        if whole_classes:
            terms = [chain_terms(piece, "slc") for piece in pieces[group]]
        else:
            terms = [[lax.psum(piece, "slc")] for piece in pieces[group]]
        flat = [term for piece in terms for term in piece]
        gradient = pl.pallas_call(
            functools.partial(gradient_kernel, ROW_PARTS, len(terms[0])),
            out_shape=jax.ShapeDtypeStruct((ROW_PARTS, slots, part), jnp.float32),
            compiler_params=pltpu.CompilerParams(vmem_limit_bytes=40 * 1024 * 1024),
            cost_estimate=pl.CostEstimate(
                flops=places * slots * 4 * length**2, bytes_accessed=3_000_000, transcendentals=0
            ),
            name="gradient",
        )(*flat, encoded[group])
        gradients.append(jnp.moveaxis(gradient, 0, 1).reshape(slots, rows)[:, :length])
    by_class = jnp.stack(gradients, axis=1)
    if whole_classes:
        local = by_class.reshape(per_device, length)
    else:
        first = (position * per_device) % groups
        local = lax.dynamic_slice_in_dim(by_class[0], first, per_device, axis=0)
    summed = lax.psum(local, ("coil", "vol"))
    factor = 1.0 / (coils * lax.axis_size("coil") * vols * lax.axis_size("vol"))
    return summed * factor


def solution(mesh):
    placed = (
        P(("grp", "vol"), "slc", None, None, None),
        P(("grp", "coil"), "slc", None, None, None),
        P(("grp", "vol"), "slc", "coil", None, None, None),
        P("slc"),
        P("slc", None),
        P(),
    )
    return jax.shard_map(
        body, mesh=mesh, in_specs=placed, out_specs=P(("grp", "slc"), None), check_vma=False
    )
```

```python
import functools
import math

import jax
import jax.numpy as jnp
import ml_dtypes
import numpy as np
from jax import lax
from jax.experimental import pallas as pl
from jax.experimental.pallas import tpu as pltpu
from jax.sharding import PartitionSpec as P

MB = 8
ROW_TILE = 16
LANE_TILE = 128
ROW_PARTS = 1


def round_up(value, multiple):
    return -(-value // multiple) * multiple


def fourier_tables(length):
    positions = np.arange(length, dtype=np.int32)
    product = positions[:, None] * positions[None, :] % length
    radians = np.float32(2.0 * math.pi / length) * product.astype(np.float32)
    factor = np.float32(1.0 / math.sqrt(length))
    return (
        (np.cos(radians) * factor).astype(ml_dtypes.bfloat16),
        (-np.sin(radians) * factor).astype(ml_dtypes.bfloat16),
    )


def dft_matrices(length, rows):
    cos_table, sin_table = fourier_tables(length)
    cosine, sine = cos_table.astype(np.float64), sin_table.astype(np.float64)
    left_re = np.zeros((2 * rows, length), np.float64)
    left_im = np.zeros((2 * rows, length), np.float64)
    left_re[:length], left_re[rows : rows + length] = cosine, sine
    left_im[:length], left_im[rows : rows + length] = -sine, cosine
    gram_re = cosine.T @ cosine + sine.T @ sine
    gram_im = sine.T @ cosine - cosine.T @ sine
    gram = np.stack(
        [np.concatenate([gram_re, gram_im], 1), np.concatenate([-gram_im, gram_re], 1)]
    )
    adjoint = np.stack(
        [np.concatenate([cosine, -sine], 1), np.concatenate([sine, cosine], 1)]
    )
    left = np.stack([left_re, left_im])
    return tuple(part.astype(ml_dtypes.bfloat16) for part in (left, gram, adjoint))


def slice_phases(shift_index, phase_offset, length):
    lines = (jnp.arange(length, dtype=jnp.int32) - length // 2).astype(jnp.float32)
    return (
        2.0 * math.pi / MB * (shift_index.astype(jnp.float32)[:, None] * lines[None, :])
        + phase_offset
    )


def dot(left, right):
    return jnp.dot(left, right, preferred_element_type=jnp.float32)


def encode_kernel(slots, columns, masked, scalars, *refs):
    image_refs, refs = refs[:slots], refs[slots:]
    map_refs, refs = refs[:slots], refs[slots:]
    kspace_ref, phase_ref, left_ref, gram_ref, adjoint_ref = refs[:5]
    shifted_ref = refs[5]
    out_refs = refs[6:-1]
    total = refs[-1]
    vols, coils = image_refs[0].shape[0], map_refs[0].shape[0]
    length = image_refs[0].shape[-1]
    rows = shifted_ref.shape[-2]
    half = phase_ref.shape[1] // 2
    part = rows // len(out_refs)
    if total.shape[1] > vols * coils * 2 * length:
        total[...] = jnp.zeros_like(total)
    for vol in range(vols):
        for coil in range(coils):
            place = vol * coils + coil
            sum_re = sum_im = None
            for slot in range(slots):
                image_re = image_refs[slot][vol, 0, 0].astype(jnp.float32)
                image_im = image_refs[slot][vol, 0, 1].astype(jnp.float32)
                map_re = map_refs[slot][coil, 0, 0].astype(jnp.float32)
                map_im = map_refs[slot][coil, 0, 1].astype(jnp.float32)
                coil_re = (map_re * image_re - map_im * image_im).astype(jnp.bfloat16)
                coil_im = (map_re * image_im + map_im * image_re).astype(jnp.bfloat16)
                partly = dot(left_ref[0], coil_re) + dot(left_ref[1], coil_im)
                column = columns[slot]
                cosine = phase_ref[:, column : column + 1]
                sine = phase_ref[:, half + column : half + column + 1]
                part_re, part_im = partly[:rows], partly[rows:]
                shift_re = part_re * cosine - part_im * sine
                shift_im = part_re * sine + part_im * cosine
                shifted_ref[slot, place, 0] = shift_re.astype(jnp.bfloat16)
                shifted_ref[slot, place, 1] = shift_im.astype(jnp.bfloat16)
                sum_re = shift_re if slot == 0 else sum_re + shift_re
                sum_im = shift_im if slot == 0 else sum_im + shift_im
            mixed = dot(sum_re.astype(jnp.bfloat16), gram_ref[0]) + dot(
                sum_im.astype(jnp.bfloat16), gram_ref[1]
            )
            if masked:
                mixed = jnp.where(scalars[1] > 0, mixed, 0.0)
            total[:, place * 2 * length : (place + 1) * 2 * length] = mixed

    @pl.when(scalars[0] > 0)
    def _():
        for vol in range(vols):
            for coil in range(coils):
                place = vol * coils + coil
                measured = dot(kspace_ref[vol, 0, coil, 0], adjoint_ref[0]) + dot(
                    kspace_ref[vol, 0, coil, 1], adjoint_ref[1]
                )
                total[:length, place * 2 * length : (place + 1) * 2 * length] -= measured

    for index, out_ref in enumerate(out_refs):
        out_ref[...] = total[index * part : (index + 1) * part, :].astype(jnp.bfloat16)


def gradient_kernel(parts, terms, *refs):
    term_refs, shifted_ref, out_ref = refs[:-2], refs[-2], refs[-1]
    slots, places, _, rows, length = shifted_ref.shape
    part = rows // parts
    for index in range(parts):
        residual = None
        for ref in term_refs[index * terms : (index + 1) * terms]:
            value = ref[...].astype(jnp.float32)
            residual = value if residual is None else residual + value
        sums = [None] * slots
        for place in range(places):
            base = place * 2 * length
            resid_re = residual[:, base : base + length]
            resid_im = residual[:, base + length : base + 2 * length]
            for slot in range(slots):
                span = slice(index * part, (index + 1) * part)
                shift_re = shifted_ref[slot, place, 0, span, :].astype(jnp.float32)
                shift_im = shifted_ref[slot, place, 1, span, :].astype(jnp.float32)
                term = resid_im * shift_re - resid_re * shift_im
                sums[slot] = term if place == 0 else sums[slot] + term
        for slot in range(slots):
            out_ref[index, slot : slot + 1, :] = jnp.sum(sums[slot].T, axis=0, keepdims=True)


def body(images, coil_maps, kspace, shift_index, phase_offset, group_order):
    vols, per_device, _, _, length = images.shape
    coils = coil_maps.shape[0]
    groups = lax.axis_size("slc")
    position = lax.axis_index("slc")
    rows = round_up(length, ROW_TILE * ROW_PARTS)
    part = rows // ROW_PARTS
    places = vols * coils
    lanes = round_up(places * 2 * length, LANE_TILE)
    whole_classes = per_device % groups == 0
    slots = max(1, per_device // groups)
    left, gram, adjoint = dft_matrices(length, rows)

    phase_angle = jnp.pad(
        slice_phases(shift_index, phase_offset, length), ((0, 0), (0, rows - length))
    )
    phases = jnp.concatenate([jnp.cos(phase_angle), jnp.sin(phase_angle)], axis=0).T
    owned = (group_order == position).astype(jnp.int32)

    encoded, pieces = [], []
    for group in range(groups):
        if whole_classes:
            columns = [slot * groups + group for slot in range(slots)]
            scalars = jnp.stack([owned[group], jnp.int32(1)])
            places_of = [lambda i, scalars, w=w: (0, w, 0, 0, 0) for w in columns]
            group_phases = phases
        else:
            within = group - (position * per_device) % groups
            held = (within >= 0) & (within < per_device)
            within = jnp.where(held, within, 0).astype(jnp.int32)
            scalars = jnp.stack([owned[group], held.astype(jnp.int32), within])
            columns = [0]
            places_of = [lambda i, scalars: (0, scalars[2], 0, 0, 0)]
            group_phases = jnp.take(
                phases, jnp.stack([within, within + per_device]), axis=1
            )
        constant = lambda ndim: (lambda i, scalars: (0,) * ndim)
        whole = lambda array: pl.BlockSpec(array.shape, constant(array.ndim))
        outputs = pl.pallas_call(
            functools.partial(encode_kernel, slots, columns, not whole_classes),
            grid_spec=pltpu.PrefetchScalarGridSpec(
                num_scalar_prefetch=1,
                grid=(1,),
                in_specs=[
                    pl.BlockSpec((vols, 1, 2, length, length), place) for place in places_of
                ]
                + [pl.BlockSpec((coils, 1, 2, length, length), place) for place in places_of]
                + [whole(kspace), whole(group_phases), whole(left), whole(gram), whole(adjoint)],
                out_specs=[
                    pl.BlockSpec((slots, places, 2, rows, length), constant(5)),
                ]
                + [pl.BlockSpec((part, lanes), constant(2))] * ROW_PARTS,
                scratch_shapes=[pltpu.VMEM((rows, lanes), jnp.float32)],
            ),
            out_shape=[
                jax.ShapeDtypeStruct((slots, places, 2, rows, length), jnp.bfloat16),
            ]
            + [jax.ShapeDtypeStruct((part, lanes), jnp.bfloat16)] * ROW_PARTS,
            compiler_params=pltpu.CompilerParams(vmem_limit_bytes=40 * 1024 * 1024),
            cost_estimate=pl.CostEstimate(
                flops=places * (slots + 1) * 16 * length**3,
                bytes_accessed=6_000_000,
                transcendentals=0,
            ),
            name="encode",
        )(
            scalars,
            *([images] * slots),
            *([coil_maps] * slots),
            kspace,
            group_phases,
            left,
            gram,
            adjoint,
        )
        encoded.append(outputs[0])
        pieces.append(outputs[1:])

    reduced = lax.psum(pieces, "slc")
    gradients = []
    for group in range(groups):
        terms = [[piece] for piece in reduced[group]]
        flat = [term for piece in terms for term in piece]
        gradient = pl.pallas_call(
            functools.partial(gradient_kernel, ROW_PARTS, len(terms[0])),
            out_shape=jax.ShapeDtypeStruct((ROW_PARTS, slots, part), jnp.float32),
            compiler_params=pltpu.CompilerParams(vmem_limit_bytes=40 * 1024 * 1024),
            cost_estimate=pl.CostEstimate(
                flops=places * slots * 4 * length**2, bytes_accessed=3_000_000, transcendentals=0
            ),
            name="gradient",
        )(*flat, encoded[group])
        gradients.append(jnp.moveaxis(gradient, 0, 1).reshape(slots, rows)[:, :length])
    by_class = jnp.stack(gradients, axis=1)
    if whole_classes:
        local = by_class.reshape(per_device, length)
    else:
        first = (position * per_device) % groups
        local = lax.dynamic_slice_in_dim(by_class[0], first, per_device, axis=0)
    summed = lax.psum(local, ("coil", "vol"))
    factor = 1.0 / (coils * lax.axis_size("coil") * vols * lax.axis_size("vol"))
    return summed * factor


def solution(mesh):
    placed = (
        P(("grp", "vol"), "slc", None, None, None),
        P(("grp", "coil"), "slc", None, None, None),
        P(("grp", "vol"), "slc", "coil", None, None, None),
        P("slc"),
        P("slc", None),
        P(),
    )
    return jax.shard_map(
        body, mesh=mesh, in_specs=placed, out_specs=P(("grp", "slc"), None), check_vma=False
    )
```

```python
import functools
import math

import jax
import jax.numpy as jnp
import ml_dtypes
import numpy as np
from jax import lax
from jax.experimental import pallas as pl
from jax.experimental.pallas import tpu as pltpu
from jax.sharding import PartitionSpec as P

MB = 8
ROW_TILE = 16
LANE_TILE = 128
ROW_PARTS = 2
LAG = 3
VMEM_BYTES = 24 * 1024 * 1024


def round_up(value, multiple):
    return -(-value // multiple) * multiple


def fourier_tables(length):
    positions = np.arange(length, dtype=np.int32)
    product = positions[:, None] * positions[None, :] % length
    radians = np.float32(2.0 * math.pi / length) * product.astype(np.float32)
    factor = np.float32(1.0 / math.sqrt(length))
    return (
        (np.cos(radians) * factor).astype(ml_dtypes.bfloat16),
        (-np.sin(radians) * factor).astype(ml_dtypes.bfloat16),
    )


def dft_matrices(length, rows):
    cos_table, sin_table = fourier_tables(length)
    cosine, sine = cos_table.astype(np.float64), sin_table.astype(np.float64)
    left_re = np.zeros((2 * rows, length), np.float64)
    left_im = np.zeros((2 * rows, length), np.float64)
    left_re[:length], left_re[rows : rows + length] = cosine, sine
    left_im[:length], left_im[rows : rows + length] = -sine, cosine
    gram_re = cosine.T @ cosine + sine.T @ sine
    gram_im = sine.T @ cosine - cosine.T @ sine
    gram = np.stack(
        [np.concatenate([gram_re, gram_im], 1), np.concatenate([-gram_im, gram_re], 1)]
    )
    adjoint = np.stack(
        [np.concatenate([cosine, -sine], 1), np.concatenate([sine, cosine], 1)]
    )
    left = np.stack([left_re, left_im])
    return tuple(part.astype(ml_dtypes.bfloat16) for part in (left, gram, adjoint))


def dot(left, right):
    return jnp.dot(left, right, preferred_element_type=jnp.float32)


def phase_columns(shift_ref, offset_ref, angle, rows_of, length):
    lines = lax.broadcasted_iota(jnp.int32, (1, length), 1) - length // 2
    angle[...] = jnp.zeros_like(angle)
    for slot, row in enumerate(rows_of):
        turns = (shift_ref[row] * lines) & (MB - 1)
        angle[slot : slot + 1, :length] = (
            2.0 * math.pi / MB * turns.astype(jnp.float32) + offset_ref[pl.ds(row, 1), :]
        )
    return jnp.cos(angle[...]).T, jnp.sin(angle[...]).T


def encode_kernel(slots, group, whole_classes, *refs):
    shift_ref, order_ref, place_ref = refs[:3]
    image_refs, refs = refs[3 : 3 + slots], refs[3 + slots :]
    map_refs, refs = refs[:slots], refs[slots:]
    kspace_ref, offset_ref, left_ref, gram_ref, adjoint_ref, shifted_ref = refs[:6]
    out_refs = refs[6:-2]
    total, angle = refs[-2:]
    vols, coils = image_refs[0].shape[0], map_refs[0].shape[0]
    length = image_refs[0].shape[-1]
    rows = shifted_ref.shape[-2]
    part = rows // len(out_refs)
    groups = order_ref.shape[0]
    if whole_classes:
        rows_of = [slot * groups + group for slot in range(slots)]
    else:
        rows_of = [place_ref[1]]
    cosines, sines = phase_columns(shift_ref, offset_ref, angle, rows_of, length)
    if total.shape[1] > vols * coils * 2 * length:
        total[...] = jnp.zeros_like(total)
    for vol in range(vols):
        for coil in range(coils):
            place = vol * coils + coil
            sum_re = sum_im = None
            for slot in range(slots):
                image_re = image_refs[slot][vol, 0, 0].astype(jnp.float32)
                image_im = image_refs[slot][vol, 0, 1].astype(jnp.float32)
                map_re = map_refs[slot][coil, 0, 0].astype(jnp.float32)
                map_im = map_refs[slot][coil, 0, 1].astype(jnp.float32)
                coil_re = (map_re * image_re - map_im * image_im).astype(jnp.bfloat16)
                coil_im = (map_re * image_im + map_im * image_re).astype(jnp.bfloat16)
                partly = dot(left_ref[0], coil_re) + dot(left_ref[1], coil_im)
                cosine = cosines[:rows, slot : slot + 1]
                sine = sines[:rows, slot : slot + 1]
                part_re, part_im = partly[:rows], partly[rows:]
                shift_re = part_re * cosine - part_im * sine
                shift_im = part_re * sine + part_im * cosine
                shifted_ref[slot, place, 0] = shift_re.astype(jnp.bfloat16)
                shifted_ref[slot, place, 1] = shift_im.astype(jnp.bfloat16)
                sum_re = shift_re if slot == 0 else sum_re + shift_re
                sum_im = shift_im if slot == 0 else sum_im + shift_im
            mixed = dot(sum_re.astype(jnp.bfloat16), gram_ref[0]) + dot(
                sum_im.astype(jnp.bfloat16), gram_ref[1]
            )
            if not whole_classes:
                mixed = jnp.where(place_ref[0] > 0, mixed, 0.0)
            total[:, place * 2 * length : (place + 1) * 2 * length] = mixed

    @pl.when(order_ref[group] == lax.axis_index("slc"))
    def _():
        for vol in range(vols):
            for coil in range(coils):
                place = vol * coils + coil
                measured = dot(kspace_ref[vol, 0, coil, 0], adjoint_ref[0]) + dot(
                    kspace_ref[vol, 0, coil, 1], adjoint_ref[1]
                )
                total[:length, place * 2 * length : (place + 1) * 2 * length] -= measured

    for index, out_ref in enumerate(out_refs):
        out_ref[...] = total[index * part : (index + 1) * part, :].astype(jnp.bfloat16)


def gradient_kernel(index, factor, on_line, *refs):
    term_refs, shifted_ref, out_ref = refs[:-2], refs[-2], refs[-1]
    slots, places, _, _, length = shifted_ref.shape
    part = out_ref.shape[1]
    terms = [ref[...].astype(jnp.float32) for ref in term_refs]
    if on_line:
        own, near, across, rest = terms
        position = lax.axis_index("slc")
        edge = (position == 0) | (position == lax.axis_size("slc") - 1)
        residual = own + jnp.where(edge, rest, near + across)
    else:
        residual = terms[0]
    sums = [None] * slots
    for place in range(places):
        base = place * 2 * length
        resid_re = residual[:, base : base + length]
        resid_im = residual[:, base + length : base + 2 * length]
        for slot in range(slots):
            span = slice(index * part, (index + 1) * part)
            shift_re = shifted_ref[slot, place, 0, span, :].astype(jnp.float32)
            shift_im = shifted_ref[slot, place, 1, span, :].astype(jnp.float32)
            term = resid_im * shift_re - resid_re * shift_im
            sums[slot] = term if place == 0 else sums[slot] + term
    for slot in range(slots):
        out_ref[slot : slot + 1, :] = factor * jnp.sum(sums[slot].T, axis=0, keepdims=True)


def line_of_four(pieces):
    position = lax.axis_index("slc")
    edge = (position == 0) | (position == 3)
    outer_pairs = [(0, 1), (1, 0), (2, 3), (3, 2)]
    inner_pairs = [(0, 0), (1, 2), (2, 1), (3, 3)]
    count = len(pieces)
    outer, inner = [], []
    for step in range(count + LAG):
        back = step - LAG
        payload = pieces[step] if step < count else None
        if back >= 0:
            others = pieces[back] + inner[back]
            payload = others if payload is None else jnp.where(edge, payload, others)
        outer.append(lax.ppermute(payload, "slc", outer_pairs))
        if step < count:
            inner.append(lax.ppermute(pieces[step] + outer[step], "slc", inner_pairs))
    return [
        (pieces[step], outer[step], inner[step], outer[step + LAG]) for step in range(count)
    ]


def body(images, coil_maps, kspace, shift_index, phase_offset, group_order):
    vols, per_device, _, _, length = images.shape
    coils = coil_maps.shape[0]
    groups = lax.axis_size("slc")
    rows = round_up(length, ROW_TILE * ROW_PARTS)
    part = rows // ROW_PARTS
    places = vols * coils
    lanes = round_up(places * 2 * length, LANE_TILE)
    whole_classes = per_device % groups == 0
    slots = max(1, per_device // groups)
    tables = dft_matrices(length, rows)
    factor = 1.0 / (coils * lax.axis_size("coil") * vols * lax.axis_size("vol"))
    first = (lax.axis_index("slc") * per_device) % groups

    def whole(array):
        return pl.BlockSpec(array.shape, lambda i, *_: (0,) * array.ndim)

    encoded, pieces = [], []
    for group in range(groups):
        if whole_classes:
            place = np.zeros((2,), np.int32)
            picks = [lambda i, *_, w=slot * groups + group: (0, w, 0, 0, 0) for slot in range(slots)]
        else:
            within = group - first
            held = (within >= 0) & (within < per_device)
            place = jnp.stack([held, jnp.where(held, within, 0)]).astype(jnp.int32)
            picks = [lambda i, shift, order, place: (0, place[1], 0, 0, 0)]
        outputs = pl.pallas_call(
            functools.partial(encode_kernel, slots, group, whole_classes),
            grid_spec=pltpu.PrefetchScalarGridSpec(
                num_scalar_prefetch=3,
                grid=(1,),
                in_specs=[pl.BlockSpec((vols, 1, 2, length, length), pick) for pick in picks]
                + [pl.BlockSpec((coils, 1, 2, length, length), pick) for pick in picks]
                + [whole(array) for array in (kspace, phase_offset, *tables)],
                out_specs=[
                    pl.BlockSpec((slots, places, 2, rows, length), lambda i, *_: (0,) * 5),
                ]
                + [pl.BlockSpec((part, lanes), lambda i, *_: (0, 0))] * ROW_PARTS,
                scratch_shapes=[
                    pltpu.VMEM((rows, lanes), jnp.float32),
                    pltpu.VMEM((round_up(slots, 8), round_up(rows, LANE_TILE)), jnp.float32),
                ],
            ),
            out_shape=[
                jax.ShapeDtypeStruct((slots, places, 2, rows, length), jnp.bfloat16),
            ]
            + [jax.ShapeDtypeStruct((part, lanes), jnp.bfloat16)] * ROW_PARTS,
            compiler_params=pltpu.CompilerParams(vmem_limit_bytes=VMEM_BYTES),
            cost_estimate=pl.CostEstimate(
                flops=places * (slots + 1) * 16 * length**3,
                bytes_accessed=6_000_000,
                transcendentals=0,
            ),
            name="encode",
        )(
            shift_index,
            group_order,
            place,
            *([images] * slots),
            *([coil_maps] * slots),
            kspace,
            phase_offset,
            *tables,
        )
        encoded.append(outputs[0])
        pieces.extend(outputs[1:])

    on_line = whole_classes and groups == 4
    if on_line:
        terms = line_of_four(pieces)
    else:
        terms = [(piece,) for piece in lax.psum(pieces, "slc")]
    gradients = []
    for step, term in enumerate(terms):
        group, index = divmod(step, ROW_PARTS)
        gradient = pl.pallas_call(
            functools.partial(gradient_kernel, index, factor, on_line),
            out_shape=jax.ShapeDtypeStruct((slots, part), jnp.float32),
            compiler_params=pltpu.CompilerParams(vmem_limit_bytes=VMEM_BYTES),
            cost_estimate=pl.CostEstimate(
                flops=places * slots * 4 * length**2, bytes_accessed=1_500_000, transcendentals=0
            ),
            name="gradient",
        )(*term, encoded[group])
        gradients.append(gradient)
    by_class = jnp.stack(
        [
            jnp.concatenate(gradients[group * ROW_PARTS : (group + 1) * ROW_PARTS], axis=1)
            for group in range(groups)
        ],
        axis=1,
    )[:, :, :length]
    if whole_classes:
        local = by_class.reshape(per_device, length)
    else:
        local = lax.dynamic_slice_in_dim(by_class[0], first, per_device, axis=0)
    return lax.psum(local, ("coil", "vol"))


def solution(mesh):
    placed = (
        P(("grp", "vol"), "slc", None, None, None),
        P(("grp", "coil"), "slc", None, None, None),
        P(("grp", "vol"), "slc", "coil", None, None, None),
        P("slc"),
        P("slc", None),
        P(),
    )
    return jax.shard_map(
        body, mesh=mesh, in_specs=placed, out_specs=P(("grp", "slc"), None), check_vma=False
    )
```

```python
import functools
import math

import jax
import jax.numpy as jnp
import ml_dtypes
import numpy as np
from jax import lax
from jax.experimental import pallas as pl
from jax.experimental.pallas import tpu as pltpu
from jax.sharding import PartitionSpec as P

MB = 8
ROW_TILE = 16
LANE_TILE = 128
ROW_PARTS = 2
LAG = 3
VMEM_BYTES = 24 * 1024 * 1024


def round_up(value, multiple):
    return -(-value // multiple) * multiple


def fourier_tables(length):
    positions = np.arange(length, dtype=np.int32)
    product = positions[:, None] * positions[None, :] % length
    radians = np.float32(2.0 * math.pi / length) * product.astype(np.float32)
    factor = np.float32(1.0 / math.sqrt(length))
    return (
        (np.cos(radians) * factor).astype(ml_dtypes.bfloat16),
        (-np.sin(radians) * factor).astype(ml_dtypes.bfloat16),
    )


def dft_matrices(length, rows):
    cos_table, sin_table = fourier_tables(length)
    cosine, sine = cos_table.astype(np.float64), sin_table.astype(np.float64)
    left_re = np.zeros((2 * rows, length), np.float64)
    left_im = np.zeros((2 * rows, length), np.float64)
    left_re[:length], left_re[rows : rows + length] = cosine, sine
    left_im[:length], left_im[rows : rows + length] = -sine, cosine
    gram_re = cosine.T @ cosine + sine.T @ sine
    gram_im = sine.T @ cosine - cosine.T @ sine
    gram = np.stack(
        [np.concatenate([gram_re, gram_im], 1), np.concatenate([-gram_im, gram_re], 1)]
    )
    adjoint = np.stack(
        [np.concatenate([cosine, -sine], 1), np.concatenate([sine, cosine], 1)]
    )
    left = np.stack([left_re, left_im])
    return tuple(part.astype(ml_dtypes.bfloat16) for part in (left, gram, adjoint))


def dot(left, right):
    return jnp.dot(left, right, preferred_element_type=jnp.float32)


def phase_columns(shift_ref, offset_ref, angle, rows_of, length):
    lines = lax.broadcasted_iota(jnp.int32, (1, length), 1) - length // 2
    angle[...] = jnp.zeros_like(angle)
    for slot, row in enumerate(rows_of):
        turns = (shift_ref[row] * lines) & (MB - 1)
        angle[slot : slot + 1, :length] = (
            2.0 * math.pi / MB * turns.astype(jnp.float32) + offset_ref[pl.ds(row, 1), :]
        )
    return jnp.cos(angle[...]).T, jnp.sin(angle[...]).T


def encode_kernel(slots, group, whole_classes, *refs):
    shift_ref, order_ref, place_ref, image_ref, map_ref, kspace_ref, offset_ref = refs[:7]
    left_ref, gram_ref, adjoint_ref, shifted_ref = refs[7:11]
    out_refs = refs[11:-2]
    total, angle = refs[-2:]
    vols, coils, length = image_ref.shape[0], map_ref.shape[0], image_ref.shape[-1]
    rows = shifted_ref.shape[-2]
    part = rows // len(out_refs)
    groups = order_ref.shape[0]
    if whole_classes:
        rows_of = [slot * groups + group for slot in range(slots)]
    else:
        rows_of = [place_ref[1]]
    cosines, sines = phase_columns(shift_ref, offset_ref, angle, rows_of, length)
    if total.shape[1] > vols * coils * 2 * length:
        total[...] = jnp.zeros_like(total)
    for vol in range(vols):
        for coil in range(coils):
            place = vol * coils + coil
            sum_re = sum_im = None
            for slot in range(slots):
                image_re = image_ref[vol, slot, 0].astype(jnp.float32)
                image_im = image_ref[vol, slot, 1].astype(jnp.float32)
                map_re = map_ref[coil, slot, 0].astype(jnp.float32)
                map_im = map_ref[coil, slot, 1].astype(jnp.float32)
                coil_re = (map_re * image_re - map_im * image_im).astype(jnp.bfloat16)
                coil_im = (map_re * image_im + map_im * image_re).astype(jnp.bfloat16)
                partly = dot(left_ref[0], coil_re) + dot(left_ref[1], coil_im)
                cosine = cosines[:rows, slot : slot + 1]
                sine = sines[:rows, slot : slot + 1]
                part_re, part_im = partly[:rows], partly[rows:]
                shift_re = part_re * cosine - part_im * sine
                shift_im = part_re * sine + part_im * cosine
                shifted_ref[slot, place, 0] = shift_re.astype(jnp.bfloat16)
                shifted_ref[slot, place, 1] = shift_im.astype(jnp.bfloat16)
                sum_re = shift_re if slot == 0 else sum_re + shift_re
                sum_im = shift_im if slot == 0 else sum_im + shift_im
            mixed = dot(sum_re.astype(jnp.bfloat16), gram_ref[0]) + dot(
                sum_im.astype(jnp.bfloat16), gram_ref[1]
            )
            if not whole_classes:
                mixed = jnp.where(place_ref[0] > 0, mixed, 0.0)
            total[:, place * 2 * length : (place + 1) * 2 * length] = mixed

    @pl.when(order_ref[group] == lax.axis_index("slc"))
    def _():
        for vol in range(vols):
            for coil in range(coils):
                place = vol * coils + coil
                measured = dot(kspace_ref[vol, 0, coil, 0], adjoint_ref[0]) + dot(
                    kspace_ref[vol, 0, coil, 1], adjoint_ref[1]
                )
                total[:length, place * 2 * length : (place + 1) * 2 * length] -= measured

    for index, out_ref in enumerate(out_refs):
        out_ref[...] = total[index * part : (index + 1) * part, :].astype(jnp.bfloat16)


def gradient_kernel(index, factor, on_line, *refs):
    term_refs, shifted_ref, out_ref = refs[:-2], refs[-2], refs[-1]
    slots, places, _, _, length = shifted_ref.shape
    part = out_ref.shape[1]
    terms = [ref[...].astype(jnp.float32) for ref in term_refs]
    if on_line:
        own, near, across, rest = terms
        position = lax.axis_index("slc")
        edge = (position == 0) | (position == lax.axis_size("slc") - 1)
        residual = own + jnp.where(edge, rest, near + across)
    else:
        residual = terms[0]
    sums = [None] * slots
    for place in range(places):
        base = place * 2 * length
        resid_re = residual[:, base : base + length]
        resid_im = residual[:, base + length : base + 2 * length]
        for slot in range(slots):
            span = slice(index * part, (index + 1) * part)
            shift_re = shifted_ref[slot, place, 0, span, :].astype(jnp.float32)
            shift_im = shifted_ref[slot, place, 1, span, :].astype(jnp.float32)
            term = resid_im * shift_re - resid_re * shift_im
            sums[slot] = term if place == 0 else sums[slot] + term
    for slot in range(slots):
        out_ref[slot : slot + 1, :] = factor * jnp.sum(sums[slot].T, axis=0, keepdims=True)


def after(value, *earlier):
    return lax.optimization_barrier((value, *earlier))[0]


def select_slices(array, group, slots, groups, within):
    lead, per_device = array.shape[:2]
    if within is None:
        return array.reshape(lead, slots, groups, *array.shape[2:])[:, :, group]
    return lax.dynamic_slice_in_dim(array, within, 1, axis=1)


def sum_over_replicas(value):
    axes = ("coil", "vol")
    if any(lax.axis_size(axis) != 2 for axis in axes):
        return lax.psum(value, axes)
    swapped = [
        lax.ppermute(value, axes, [(index, index ^ mask) for index in range(4)])
        for mask in (1, 2, 3)
    ]
    return (value + swapped[0]) + (swapped[1] + swapped[2])


def line_of_four(encode, gradient, count):
    position = lax.axis_index("slc")
    edge = (position == 0) | (position == 3)
    outer_pairs = [(0, 1), (1, 0), (2, 3), (3, 2)]
    inner_pairs = [(0, 0), (1, 2), (2, 1), (3, 3)]
    parts = ROW_PARTS
    pieces, shifted, outer, inner, gradients = [], [], [], [], []

    def encode_next(*earlier):
        group = len(shifted)
        if group * parts < count:
            encoded = encode(group, *earlier)
            shifted.append(encoded[0])
            pieces.extend(encoded[1:])

    def outer_next(*earlier):
        step = len(outer)
        back = step - LAG
        payload = pieces[step] if step < count else None
        if back >= 0:
            others = pieces[back] + inner[back]
            payload = others if payload is None else jnp.where(edge, payload, others)
        if earlier:
            payload = after(payload, *earlier)
        outer.append(lax.ppermute(payload, "slc", outer_pairs))
        return payload

    def gradient_next(*earlier):
        step = len(gradients)
        terms = (pieces[step], outer[step], inner[step], outer[step + LAG])
        own = after(terms[0], *earlier) if earlier else terms[0]
        gradients.append(gradient(step, (own, *terms[1:]), shifted[step // parts]))

    encode_next()
    for _ in range(parts):
        outer_next()
    while len(pieces) < LAG:
        encode_next()
    while len(outer) < LAG:
        outer_next()
    latest = ()
    for step in range(count):
        half = pieces[step] + after(outer[step], *latest)
        inner.append(lax.ppermute(half, "slc", inner_pairs))
        if len(pieces) < min(count, step + LAG + 1):
            encode_next(half)
        latest = ()
        if step >= 1:
            latest = (outer_next(half),)
        if step >= LAG + 1:
            gradient_next(*latest)
            latest = (*latest, gradients[-1])
    last = outer_next(*latest)
    while len(gradients) < count:
        gradient_next(last)
    return gradients


def body(images, coil_maps, kspace, shift_index, phase_offset, group_order):
    vols, per_device, _, _, length = images.shape
    coils = coil_maps.shape[0]
    groups = lax.axis_size("slc")
    rows = round_up(length, ROW_TILE * ROW_PARTS)
    part = rows // ROW_PARTS
    places = vols * coils
    lanes = round_up(places * 2 * length, LANE_TILE)
    whole_classes = per_device % groups == 0
    slots = max(1, per_device // groups)
    tables = dft_matrices(length, rows)
    factor = 1.0 / (coils * lax.axis_size("coil") * vols * lax.axis_size("vol"))
    first = (lax.axis_index("slc") * per_device) % groups
    on_line = whole_classes and groups == 4
    in_vmem = pl.BlockSpec(memory_space=pltpu.VMEM)
    in_smem = pl.BlockSpec(memory_space=pltpu.SMEM)

    def encode(group, *earlier):
        if whole_classes:
            within, place = None, np.zeros((2,), np.int32)
        else:
            within = group - first
            held = (within >= 0) & (within < per_device)
            within = jnp.where(held, within, 0)
            place = jnp.stack([held, within]).astype(jnp.int32)
        image, coil_map = images, coil_maps
        if earlier:
            image, coil_map, _ = lax.optimization_barrier((image, coil_map, earlier[0]))
        return pl.pallas_call(
            functools.partial(encode_kernel, slots, group, whole_classes),
            in_specs=[in_smem] * 3 + [in_vmem] * 7,
            out_shape=[
                jax.ShapeDtypeStruct((slots, places, 2, rows, length), jnp.bfloat16),
            ]
            + [jax.ShapeDtypeStruct((part, lanes), jnp.bfloat16)] * ROW_PARTS,
            scratch_shapes=[
                pltpu.VMEM((rows, lanes), jnp.float32),
                pltpu.VMEM((round_up(slots, 8), round_up(rows, LANE_TILE)), jnp.float32),
            ],
            compiler_params=pltpu.CompilerParams(vmem_limit_bytes=VMEM_BYTES),
            cost_estimate=pl.CostEstimate(
                flops=places * (slots + 1) * 16 * length**3,
                bytes_accessed=6_000_000,
                transcendentals=0,
            ),
            name="encode",
        )(
            shift_index,
            group_order,
            place,
            select_slices(image, group, slots, groups, within),
            select_slices(coil_map, group, slots, groups, within),
            kspace,
            phase_offset,
            *tables,
        )

    def gradient(step, terms, encoded):
        return pl.pallas_call(
            functools.partial(gradient_kernel, step % ROW_PARTS, factor, on_line),
            out_shape=jax.ShapeDtypeStruct((slots, part), jnp.float32),
            compiler_params=pltpu.CompilerParams(vmem_limit_bytes=VMEM_BYTES),
            cost_estimate=pl.CostEstimate(
                flops=places * slots * 4 * length**2, bytes_accessed=1_500_000, transcendentals=0
            ),
            name="gradient",
        )(*terms, encoded)

    if on_line:
        gradients = line_of_four(encode, gradient, groups * ROW_PARTS)
    else:
        encoded = [encode(group) for group in range(groups)]
        reduced = lax.psum([list(outputs[1:]) for outputs in encoded], "slc")
        gradients = [
            gradient(index, (piece,), encoded[group][0])
            for group in range(groups)
            for index, piece in enumerate(reduced[group])
        ]
    by_class = jnp.stack(
        [
            jnp.concatenate(gradients[group * ROW_PARTS : (group + 1) * ROW_PARTS], axis=1)
            for group in range(groups)
        ],
        axis=1,
    )[:, :, :length]
    if whole_classes:
        local = by_class.reshape(per_device, length)
    else:
        local = lax.dynamic_slice_in_dim(by_class[0], first, per_device, axis=0)
    return sum_over_replicas(local)


def solution(mesh):
    placed = (
        P(("grp", "vol"), "slc", None, None, None),
        P(("grp", "coil"), "slc", None, None, None),
        P(("grp", "vol"), "slc", "coil", None, None, None),
        P("slc"),
        P("slc", None),
        P(),
    )
    return jax.shard_map(
        body, mesh=mesh, in_specs=placed, out_specs=P(("grp", "slc"), None), check_vma=False
    )
```

```python
import functools
import math

import jax
import jax.numpy as jnp
import ml_dtypes
import numpy as np
from jax import lax
from jax.experimental import pallas as pl
from jax.experimental.pallas import tpu as pltpu
from jax.sharding import PartitionSpec as P

MB = 8
ROW_TILE = 16
LANE_TILE = 128
ROW_PARTS = 2
LAG = 3
VMEM_BYTES = 24 * 1024 * 1024


def round_up(value, multiple):
    return -(-value // multiple) * multiple


def fourier_tables(length):
    positions = np.arange(length, dtype=np.int32)
    product = positions[:, None] * positions[None, :] % length
    radians = np.float32(2.0 * math.pi / length) * product.astype(np.float32)
    factor = np.float32(1.0 / math.sqrt(length))
    return (
        (np.cos(radians) * factor).astype(ml_dtypes.bfloat16),
        (-np.sin(radians) * factor).astype(ml_dtypes.bfloat16),
    )


def dft_matrices(length, rows):
    cos_table, sin_table = fourier_tables(length)
    cosine, sine = cos_table.astype(np.float64), sin_table.astype(np.float64)
    left_re = np.zeros((2 * rows, length), np.float64)
    left_im = np.zeros((2 * rows, length), np.float64)
    left_re[:length], left_re[rows : rows + length] = cosine, sine
    left_im[:length], left_im[rows : rows + length] = -sine, cosine
    gram_re = cosine.T @ cosine + sine.T @ sine
    gram_im = sine.T @ cosine - cosine.T @ sine
    gram = np.stack(
        [np.concatenate([gram_re, gram_im], 1), np.concatenate([-gram_im, gram_re], 1)]
    )
    adjoint = np.stack(
        [np.concatenate([cosine, -sine], 1), np.concatenate([sine, cosine], 1)]
    )
    left = np.stack([left_re, left_im])
    return tuple(part.astype(ml_dtypes.bfloat16) for part in (left, gram, adjoint))


def dot(left, right):
    return jnp.dot(left, right, preferred_element_type=jnp.float32)


def phase_columns(shift_ref, offset_ref, angle, rows_of, length):
    lines = lax.broadcasted_iota(jnp.int32, (1, length), 1) - length // 2
    angle[...] = jnp.zeros_like(angle)
    for slot, row in enumerate(rows_of):
        turns = (shift_ref[row] * lines) & (MB - 1)
        angle[slot : slot + 1, :length] = (
            2.0 * math.pi / MB * turns.astype(jnp.float32) + offset_ref[pl.ds(row, 1), :]
        )
    return jnp.cos(angle[...]).T, jnp.sin(angle[...]).T


def encode_kernel(slots, group, whole_classes, *refs):
    shift_ref, order_ref, place_ref, image_ref, map_ref, kspace_ref, offset_ref = refs[:7]
    left_ref, gram_ref, adjoint_ref, kept_ref = refs[7:11]
    out_refs = refs[11:-4]
    total, angle, shifted_ref, copied = refs[-4:]
    vols, coils, length = image_ref.shape[0], map_ref.shape[0], image_ref.shape[-1]
    rows = shifted_ref.shape[-2]
    copies = []
    part = rows // len(out_refs)
    groups = order_ref.shape[0]
    if whole_classes:
        rows_of = [slot * groups + group for slot in range(slots)]
    else:
        rows_of = [place_ref[1]]
    cosines, sines = phase_columns(shift_ref, offset_ref, angle, rows_of, length)
    if total.shape[1] > vols * coils * 2 * length:
        total[...] = jnp.zeros_like(total)
    for vol in range(vols):
        for coil in range(coils):
            place = vol * coils + coil
            sum_re = sum_im = None
            for slot, pick in enumerate(rows_of):
                image_re = image_ref[vol, pick, 0].astype(jnp.float32)
                image_im = image_ref[vol, pick, 1].astype(jnp.float32)
                map_re = map_ref[coil, pick, 0].astype(jnp.float32)
                map_im = map_ref[coil, pick, 1].astype(jnp.float32)
                coil_re = (map_re * image_re - map_im * image_im).astype(jnp.bfloat16)
                coil_im = (map_re * image_im + map_im * image_re).astype(jnp.bfloat16)
                partly = dot(left_ref[0], coil_re) + dot(left_ref[1], coil_im)
                cosine = cosines[:rows, slot : slot + 1]
                sine = sines[:rows, slot : slot + 1]
                part_re, part_im = partly[:rows], partly[rows:]
                shift_re = part_re * cosine - part_im * sine
                shift_im = part_re * sine + part_im * cosine
                shifted_ref[slot, place, 0] = shift_re.astype(jnp.bfloat16)
                shifted_ref[slot, place, 1] = shift_im.astype(jnp.bfloat16)
                copy = pltpu.make_async_copy(
                    shifted_ref.at[slot, place], kept_ref.at[slot, place], copied.at[slot, place]
                )
                copy.start()
                copies.append(copy)
                sum_re = shift_re if slot == 0 else sum_re + shift_re
                sum_im = shift_im if slot == 0 else sum_im + shift_im
            mixed = dot(sum_re.astype(jnp.bfloat16), gram_ref[0]) + dot(
                sum_im.astype(jnp.bfloat16), gram_ref[1]
            )
            if not whole_classes:
                mixed = jnp.where(place_ref[0] > 0, mixed, 0.0)
            total[:, place * 2 * length : (place + 1) * 2 * length] = mixed

    @pl.when(order_ref[group] == lax.axis_index("slc"))
    def _():
        for vol in range(vols):
            for coil in range(coils):
                place = vol * coils + coil
                measured = dot(kspace_ref[vol, 0, coil, 0], adjoint_ref[0]) + dot(
                    kspace_ref[vol, 0, coil, 1], adjoint_ref[1]
                )
                total[:length, place * 2 * length : (place + 1) * 2 * length] -= measured

    for index, out_ref in enumerate(out_refs):
        out_ref[...] = total[index * part : (index + 1) * part, :].astype(jnp.bfloat16)
    for copy in copies:
        copy.wait()


def gradient_kernel(index, factor, on_line, *refs):
    term_refs, shifted_ref, out_ref = refs[:-2], refs[-2], refs[-1]
    slots, places, _, _, length = shifted_ref.shape
    part = out_ref.shape[1]
    terms = [ref[...].astype(jnp.float32) for ref in term_refs]
    if on_line:
        own, near, across, rest = terms
        position = lax.axis_index("slc")
        edge = (position == 0) | (position == lax.axis_size("slc") - 1)
        residual = own + jnp.where(edge, rest, near + across)
    else:
        residual = terms[0]
    sums = [None] * slots
    for place in range(places):
        base = place * 2 * length
        resid_re = residual[:, base : base + length]
        resid_im = residual[:, base + length : base + 2 * length]
        for slot in range(slots):
            span = slice(index * part, (index + 1) * part)
            shift_re = shifted_ref[slot, place, 0, span, :].astype(jnp.float32)
            shift_im = shifted_ref[slot, place, 1, span, :].astype(jnp.float32)
            term = resid_im * shift_re - resid_re * shift_im
            sums[slot] = term if place == 0 else sums[slot] + term
    for slot in range(slots):
        out_ref[slot : slot + 1, :] = factor * jnp.sum(sums[slot].T, axis=0, keepdims=True)


def after(value, *earlier):
    return lax.optimization_barrier((value, *earlier))[0]


def sum_over_replicas(value):
    axes = ("coil", "vol")
    if any(lax.axis_size(axis) != 2 for axis in axes):
        return lax.psum(value, axes)
    swapped = [
        lax.ppermute(value, axes, [(index, index ^ mask) for index in range(4)])
        for mask in (1, 2, 3)
    ]
    return (value + swapped[0]) + (swapped[1] + swapped[2])


def line_of_four(encode, gradient, count):
    position = lax.axis_index("slc")
    edge = (position == 0) | (position == 3)
    outer_pairs = [(0, 1), (1, 0), (2, 3), (3, 2)]
    inner_pairs = [(0, 0), (1, 2), (2, 1), (3, 3)]
    parts = ROW_PARTS
    pieces, shifted, outer, inner, gradients = [], [], [], [], []

    def encode_next(*earlier):
        group = len(shifted)
        if group * parts < count:
            encoded = encode(group, *earlier)
            shifted.append(encoded[0])
            pieces.extend(encoded[1:])

    def outer_next(*earlier):
        step = len(outer)
        back = step - LAG
        payload = pieces[step] if step < count else None
        if back >= 0:
            others = pieces[back] + inner[back]
            payload = others if payload is None else jnp.where(edge, payload, others)
        if earlier:
            payload = after(payload, *earlier)
        outer.append(lax.ppermute(payload, "slc", outer_pairs))
        return payload

    def gradient_next(*earlier):
        step = len(gradients)
        terms = (pieces[step], outer[step], inner[step], outer[step + LAG])
        own = after(terms[0], *earlier) if earlier else terms[0]
        gradients.append(gradient(step, (own, *terms[1:]), shifted[step // parts]))

    encode_next()
    for _ in range(parts):
        outer_next()
    while len(pieces) < LAG:
        encode_next()
    while len(outer) < LAG:
        outer_next()
    latest = (pieces[-1],)
    for step in range(count):
        half = pieces[step] + after(outer[step], *latest)
        inner.append(lax.ppermute(half, "slc", inner_pairs))
        if len(pieces) < min(count, step + LAG + 1):
            encode_next(half)
        latest = ()
        if step >= 1:
            latest = (outer_next(half),)
        if step >= LAG + 1:
            gradient_next(*latest)
            latest = (*latest, gradients[-1])
    last = outer_next(*latest)
    while len(gradients) < count:
        gradient_next(last)
    return gradients


def body(images, coil_maps, kspace, shift_index, phase_offset, group_order):
    vols, per_device, _, _, length = images.shape
    coils = coil_maps.shape[0]
    groups = lax.axis_size("slc")
    rows = round_up(length, ROW_TILE * ROW_PARTS)
    part = rows // ROW_PARTS
    places = vols * coils
    lanes = round_up(places * 2 * length, LANE_TILE)
    whole_classes = per_device % groups == 0
    slots = max(1, per_device // groups)
    tables = dft_matrices(length, rows)
    factor = 1.0 / (coils * lax.axis_size("coil") * vols * lax.axis_size("vol"))
    first = (lax.axis_index("slc") * per_device) % groups
    on_line = whole_classes and groups == 4
    in_vmem = pl.BlockSpec(memory_space=pltpu.VMEM)
    in_smem = pl.BlockSpec(memory_space=pltpu.SMEM)

    def encode(group, *earlier):
        if whole_classes:
            place = np.zeros((2,), np.int32)
        else:
            within = group - first
            held = (within >= 0) & (within < per_device)
            within = jnp.where(held, within, 0)
            place = jnp.stack([held, within]).astype(jnp.int32)
        offset = after(phase_offset, *earlier) if earlier else phase_offset
        return pl.pallas_call(
            functools.partial(encode_kernel, slots, group, whole_classes),
            in_specs=[in_smem] * 3 + [in_vmem] * 7,
            out_specs=[pl.BlockSpec(memory_space=pl.ANY)] + [in_vmem] * ROW_PARTS,
            out_shape=[
                jax.ShapeDtypeStruct((slots, places, 2, rows, length), jnp.bfloat16),
            ]
            + [jax.ShapeDtypeStruct((part, lanes), jnp.bfloat16)] * ROW_PARTS,
            scratch_shapes=[
                pltpu.VMEM((rows, lanes), jnp.float32),
                pltpu.VMEM((round_up(slots, 8), round_up(rows, LANE_TILE)), jnp.float32),
                pltpu.VMEM((slots, places, 2, rows, length), jnp.bfloat16),
                pltpu.SemaphoreType.DMA((slots, places)),
            ],
            compiler_params=pltpu.CompilerParams(vmem_limit_bytes=VMEM_BYTES),
            cost_estimate=pl.CostEstimate(
                flops=places * (slots + 1) * 16 * length**3,
                bytes_accessed=6_000_000,
                transcendentals=0,
            ),
            name="encode",
        )(
            shift_index,
            group_order,
            place,
            images,
            coil_maps,
            kspace,
            offset,
            *tables,
        )

    def gradient(step, terms, encoded):
        return pl.pallas_call(
            functools.partial(gradient_kernel, step % ROW_PARTS, factor, on_line),
            out_shape=jax.ShapeDtypeStruct((slots, part), jnp.float32),
            compiler_params=pltpu.CompilerParams(vmem_limit_bytes=VMEM_BYTES),
            cost_estimate=pl.CostEstimate(
                flops=places * slots * 4 * length**2, bytes_accessed=1_500_000, transcendentals=0
            ),
            name="gradient",
        )(*terms, encoded)

    if on_line:
        gradients = line_of_four(encode, gradient, groups * ROW_PARTS)
    else:
        encoded = [encode(group) for group in range(groups)]
        reduced = lax.psum([list(outputs[1:]) for outputs in encoded], "slc")
        gradients = [
            gradient(index, (piece,), encoded[group][0])
            for group in range(groups)
            for index, piece in enumerate(reduced[group])
        ]
    by_class = jnp.stack(
        [
            jnp.concatenate(gradients[group * ROW_PARTS : (group + 1) * ROW_PARTS], axis=1)
            for group in range(groups)
        ],
        axis=1,
    )[:, :, :length]
    if whole_classes:
        local = by_class.reshape(per_device, length)
    else:
        local = lax.dynamic_slice_in_dim(by_class[0], first, per_device, axis=0)
    return sum_over_replicas(local)


def solution(mesh):
    placed = (
        P(("grp", "vol"), "slc", None, None, None),
        P(("grp", "coil"), "slc", None, None, None),
        P(("grp", "vol"), "slc", "coil", None, None, None),
        P("slc"),
        P("slc", None),
        P(),
    )
    return jax.shard_map(
        body, mesh=mesh, in_specs=placed, out_specs=P(("grp", "slc"), None), check_vma=False
    )
```

```python
import functools
import math

import jax
import jax.numpy as jnp
import ml_dtypes
import numpy as np
from jax import lax
from jax.experimental import pallas as pl
from jax.experimental.pallas import tpu as pltpu
from jax.sharding import PartitionSpec as P

MB = 8
ROW_TILE = 16
LANE_TILE = 128
ROW_PARTS = 1
LAG = 2
VMEM_BYTES = 24 * 1024 * 1024


def round_up(value, multiple):
    return -(-value // multiple) * multiple


def fourier_tables(length):
    positions = np.arange(length, dtype=np.int32)
    product = positions[:, None] * positions[None, :] % length
    radians = np.float32(2.0 * math.pi / length) * product.astype(np.float32)
    factor = np.float32(1.0 / math.sqrt(length))
    return (
        (np.cos(radians) * factor).astype(ml_dtypes.bfloat16),
        (-np.sin(radians) * factor).astype(ml_dtypes.bfloat16),
    )


def dft_matrices(length, rows):
    cos_table, sin_table = fourier_tables(length)
    cosine, sine = cos_table.astype(np.float64), sin_table.astype(np.float64)
    left_re = np.zeros((2 * rows, length), np.float64)
    left_im = np.zeros((2 * rows, length), np.float64)
    left_re[:length], left_re[rows : rows + length] = cosine, sine
    left_im[:length], left_im[rows : rows + length] = -sine, cosine
    gram_re = cosine.T @ cosine + sine.T @ sine
    gram_im = sine.T @ cosine - cosine.T @ sine
    gram = np.stack(
        [np.concatenate([gram_re, gram_im], 1), np.concatenate([-gram_im, gram_re], 1)]
    )
    adjoint = np.stack(
        [np.concatenate([cosine, -sine], 1), np.concatenate([sine, cosine], 1)]
    )
    left = np.stack([left_re, left_im])
    return tuple(part.astype(ml_dtypes.bfloat16) for part in (left, gram, adjoint))


def dot(left, right):
    return jnp.dot(left, right, preferred_element_type=jnp.float32)


def phase_columns(shift_ref, offset_ref, angle, rows_of, length):
    lines = lax.broadcasted_iota(jnp.int32, (1, length), 1) - length // 2
    angle[...] = jnp.zeros_like(angle)
    for slot, row in enumerate(rows_of):
        turns = (shift_ref[row] * lines) & (MB - 1)
        angle[slot : slot + 1, :length] = (
            2.0 * math.pi / MB * turns.astype(jnp.float32) + offset_ref[pl.ds(row, 1), :]
        )
    return jnp.cos(angle[...]).T, jnp.sin(angle[...]).T


def encode_kernel(slots, group, whole_classes, *refs):
    shift_ref, order_ref, place_ref, image_ref, map_ref, kspace_ref, offset_ref = refs[:7]
    left_ref, gram_ref, adjoint_ref, shifted_ref = refs[7:11]
    out_refs = refs[11:-2]
    total, angle = refs[-2:]
    vols, coils, length = image_ref.shape[0], map_ref.shape[0], image_ref.shape[-1]
    rows = shifted_ref.shape[-2]
    part = rows // len(out_refs)
    groups = order_ref.shape[0]
    if whole_classes:
        rows_of = [slot * groups + group for slot in range(slots)]
    else:
        rows_of = [place_ref[1]]
    cosines, sines = phase_columns(shift_ref, offset_ref, angle, rows_of, length)
    if total.shape[1] > vols * coils * 2 * length:
        total[...] = jnp.zeros_like(total)
    for vol in range(vols):
        for coil in range(coils):
            place = vol * coils + coil
            sum_re = sum_im = None
            for slot in range(slots):
                image_re = image_ref[vol, slot, 0].astype(jnp.float32)
                image_im = image_ref[vol, slot, 1].astype(jnp.float32)
                map_re = map_ref[coil, slot, 0].astype(jnp.float32)
                map_im = map_ref[coil, slot, 1].astype(jnp.float32)
                coil_re = (map_re * image_re - map_im * image_im).astype(jnp.bfloat16)
                coil_im = (map_re * image_im + map_im * image_re).astype(jnp.bfloat16)
                partly = dot(left_ref[0], coil_re) + dot(left_ref[1], coil_im)
                cosine = cosines[:rows, slot : slot + 1]
                sine = sines[:rows, slot : slot + 1]
                part_re, part_im = partly[:rows], partly[rows:]
                shift_re = part_re * cosine - part_im * sine
                shift_im = part_re * sine + part_im * cosine
                shifted_ref[slot, place, 0] = shift_re.astype(jnp.bfloat16)
                shifted_ref[slot, place, 1] = shift_im.astype(jnp.bfloat16)
                sum_re = shift_re if slot == 0 else sum_re + shift_re
                sum_im = shift_im if slot == 0 else sum_im + shift_im
            mixed = dot(sum_re.astype(jnp.bfloat16), gram_ref[0]) + dot(
                sum_im.astype(jnp.bfloat16), gram_ref[1]
            )
            if not whole_classes:
                mixed = jnp.where(place_ref[0] > 0, mixed, 0.0)
            total[:, place * 2 * length : (place + 1) * 2 * length] = mixed

    @pl.when(order_ref[group] == lax.axis_index("slc"))
    def _():
        for vol in range(vols):
            for coil in range(coils):
                place = vol * coils + coil
                measured = dot(kspace_ref[vol, 0, coil, 0], adjoint_ref[0]) + dot(
                    kspace_ref[vol, 0, coil, 1], adjoint_ref[1]
                )
                total[:length, place * 2 * length : (place + 1) * 2 * length] -= measured

    for index, out_ref in enumerate(out_refs):
        out_ref[...] = total[index * part : (index + 1) * part, :].astype(jnp.bfloat16)


def gradient_kernel(index, factor, on_line, *refs):
    term_refs, shifted_ref, out_ref = refs[:-2], refs[-2], refs[-1]
    slots, places, _, _, length = shifted_ref.shape
    part = out_ref.shape[1]
    terms = [ref[...].astype(jnp.float32) for ref in term_refs]
    if on_line:
        own, near, across, rest = terms
        position = lax.axis_index("slc")
        edge = (position == 0) | (position == lax.axis_size("slc") - 1)
        residual = own + jnp.where(edge, rest, near + across)
    else:
        residual = terms[0]
    sums = [None] * slots
    for place in range(places):
        base = place * 2 * length
        resid_re = residual[:, base : base + length]
        resid_im = residual[:, base + length : base + 2 * length]
        for slot in range(slots):
            span = slice(index * part, (index + 1) * part)
            shift_re = shifted_ref[slot, place, 0, span, :].astype(jnp.float32)
            shift_im = shifted_ref[slot, place, 1, span, :].astype(jnp.float32)
            term = resid_im * shift_re - resid_re * shift_im
            sums[slot] = term if place == 0 else sums[slot] + term
    for slot in range(slots):
        out_ref[slot : slot + 1, :] = factor * jnp.sum(sums[slot].T, axis=0, keepdims=True)


def after(value, *earlier):
    return lax.optimization_barrier((value, *earlier))[0]


def select_slices(array, group, slots, groups, within):
    lead, per_device = array.shape[:2]
    if within is None:
        return array.reshape(lead, slots, groups, *array.shape[2:])[:, :, group]
    return lax.dynamic_slice_in_dim(array, within, 1, axis=1)


def sum_over_replicas(value):
    axes = ("coil", "vol")
    if any(lax.axis_size(axis) != 2 for axis in axes):
        return lax.psum(value, axes)
    swapped = [
        lax.ppermute(value, axes, [(index, index ^ mask) for index in range(4)])
        for mask in (1, 2, 3)
    ]
    return (value + swapped[0]) + (swapped[1] + swapped[2])


def line_of_four(encode, gradient, count):
    position = lax.axis_index("slc")
    edge = (position == 0) | (position == 3)
    outer_pairs = [(0, 1), (1, 0), (2, 3), (3, 2)]
    inner_pairs = [(0, 0), (1, 2), (2, 1), (3, 3)]
    parts = ROW_PARTS
    pieces, shifted, outer, inner, gradients = [], [], [], [], []

    def encode_next(*earlier):
        group = len(shifted)
        if group * parts < count:
            encoded = encode(group, *earlier)
            shifted.append(encoded[0])
            pieces.extend(encoded[1:])

    def outer_next(*earlier):
        step = len(outer)
        back = step - LAG
        payload = pieces[step] if step < count else None
        if back >= 0:
            others = pieces[back] + inner[back]
            payload = others if payload is None else jnp.where(edge, payload, others)
        if earlier:
            payload = after(payload, *earlier)
        outer.append(lax.ppermute(payload, "slc", outer_pairs))
        return payload

    def gradient_next(*earlier):
        step = len(gradients)
        terms = (pieces[step], outer[step], inner[step], outer[step + LAG])
        own = after(terms[0], *earlier) if earlier else terms[0]
        gradients.append(gradient(step, (own, *terms[1:]), shifted[step // parts]))

    while len(outer) < LAG:
        encode_next()
        while len(outer) < min(LAG, len(pieces)):
            outer_next()
    encode_next()
    latest = (pieces[-1],)
    for step in range(count):
        half = pieces[step] + after(outer[step], *latest)
        inner.append(lax.ppermute(half, "slc", inner_pairs))
        if len(pieces) < min(count, step + LAG + 2):
            encode_next(half)
        latest = ()
        if step >= 1:
            latest = (outer_next(half),)
        if step >= LAG + 1:
            gradient_next(*latest)
            latest = (*latest, gradients[-1])
    last = outer_next(*latest)
    while len(gradients) < count:
        gradient_next(last)
    return gradients


def body(images, coil_maps, kspace, shift_index, phase_offset, group_order):
    vols, per_device, _, _, length = images.shape
    coils = coil_maps.shape[0]
    groups = lax.axis_size("slc")
    rows = round_up(length, ROW_TILE * ROW_PARTS)
    part = rows // ROW_PARTS
    places = vols * coils
    lanes = round_up(places * 2 * length, LANE_TILE)
    whole_classes = per_device % groups == 0
    slots = max(1, per_device // groups)
    tables = dft_matrices(length, rows)
    factor = 1.0 / (coils * lax.axis_size("coil") * vols * lax.axis_size("vol"))
    first = (lax.axis_index("slc") * per_device) % groups
    on_line = whole_classes and groups == 4
    in_vmem = pl.BlockSpec(memory_space=pltpu.VMEM)
    in_smem = pl.BlockSpec(memory_space=pltpu.SMEM)

    def encode(group, *earlier):
        if whole_classes:
            within, place = None, np.zeros((2,), np.int32)
        else:
            within = group - first
            held = (within >= 0) & (within < per_device)
            within = jnp.where(held, within, 0)
            place = jnp.stack([held, within]).astype(jnp.int32)
        image, coil_map = images, coil_maps
        if earlier:
            image, coil_map, _ = lax.optimization_barrier((image, coil_map, earlier[0]))
        return pl.pallas_call(
            functools.partial(encode_kernel, slots, group, whole_classes),
            in_specs=[in_smem] * 3 + [in_vmem] * 7,
            out_shape=[
                jax.ShapeDtypeStruct((slots, places, 2, rows, length), jnp.bfloat16),
            ]
            + [jax.ShapeDtypeStruct((part, lanes), jnp.bfloat16)] * ROW_PARTS,
            scratch_shapes=[
                pltpu.VMEM((rows, lanes), jnp.float32),
                pltpu.VMEM((round_up(slots, 8), round_up(rows, LANE_TILE)), jnp.float32),
            ],
            compiler_params=pltpu.CompilerParams(vmem_limit_bytes=VMEM_BYTES),
            cost_estimate=pl.CostEstimate(
                flops=places * (slots + 1) * 16 * length**3,
                bytes_accessed=6_000_000,
                transcendentals=0,
            ),
            name="encode",
        )(
            shift_index,
            group_order,
            place,
            select_slices(image, group, slots, groups, within),
            select_slices(coil_map, group, slots, groups, within),
            kspace,
            phase_offset,
            *tables,
        )

    def gradient(step, terms, encoded):
        return pl.pallas_call(
            functools.partial(gradient_kernel, step % ROW_PARTS, factor, on_line),
            out_shape=jax.ShapeDtypeStruct((slots, part), jnp.float32),
            compiler_params=pltpu.CompilerParams(vmem_limit_bytes=VMEM_BYTES),
            cost_estimate=pl.CostEstimate(
                flops=places * slots * 4 * length**2, bytes_accessed=1_500_000, transcendentals=0
            ),
            name="gradient",
        )(*terms, encoded)

    if on_line:
        gradients = line_of_four(encode, gradient, groups * ROW_PARTS)
    else:
        encoded = [encode(group) for group in range(groups)]
        reduced = lax.psum([list(outputs[1:]) for outputs in encoded], "slc")
        gradients = [
            gradient(index, (piece,), encoded[group][0])
            for group in range(groups)
            for index, piece in enumerate(reduced[group])
        ]
    by_class = jnp.stack(
        [
            jnp.concatenate(gradients[group * ROW_PARTS : (group + 1) * ROW_PARTS], axis=1)
            for group in range(groups)
        ],
        axis=1,
    )[:, :, :length]
    if whole_classes:
        local = by_class.reshape(per_device, length)
    else:
        local = lax.dynamic_slice_in_dim(by_class[0], first, per_device, axis=0)
    return sum_over_replicas(local)


def solution(mesh):
    placed = (
        P(("grp", "vol"), "slc", None, None, None),
        P(("grp", "coil"), "slc", None, None, None),
        P(("grp", "vol"), "slc", "coil", None, None, None),
        P("slc"),
        P("slc", None),
        P(),
    )
    return jax.shard_map(
        body, mesh=mesh, in_specs=placed, out_specs=P(("grp", "slc"), None), check_vma=False
    )
```

```python
import functools
import math

import jax
import jax.numpy as jnp
import ml_dtypes
import numpy as np
from jax import lax
from jax.experimental import pallas as pl
from jax.experimental.pallas import tpu as pltpu
from jax.sharding import PartitionSpec as P

MB = 8
ROW_TILE = 16
LANE_TILE = 128
ROW_PARTS = 2
LAG = 3
HALVES = 2
VMEM_BYTES = 24 * 1024 * 1024


def round_up(value, multiple):
    return -(-value // multiple) * multiple


def fourier_tables(length):
    positions = np.arange(length, dtype=np.int32)
    product = positions[:, None] * positions[None, :] % length
    radians = np.float32(2.0 * math.pi / length) * product.astype(np.float32)
    factor = np.float32(1.0 / math.sqrt(length))
    return (
        (np.cos(radians) * factor).astype(ml_dtypes.bfloat16),
        (-np.sin(radians) * factor).astype(ml_dtypes.bfloat16),
    )


def dft_matrices(length, rows):
    cos_table, sin_table = fourier_tables(length)
    cosine, sine = cos_table.astype(np.float64), sin_table.astype(np.float64)
    left_re = np.zeros((2 * rows, length), np.float64)
    left_im = np.zeros((2 * rows, length), np.float64)
    left_re[:length], left_re[rows : rows + length] = cosine, sine
    left_im[:length], left_im[rows : rows + length] = -sine, cosine
    gram_re = cosine.T @ cosine + sine.T @ sine
    gram_im = sine.T @ cosine - cosine.T @ sine
    gram = np.stack(
        [np.concatenate([gram_im, -gram_re], 1), np.concatenate([gram_re, gram_im], 1)]
    )
    adjoint = np.stack(
        [np.concatenate([-sine, -cosine], 1), np.concatenate([cosine, -sine], 1)]
    )
    left = np.stack([left_re, left_im])
    return tuple(part.astype(ml_dtypes.bfloat16) for part in (left, gram, adjoint))


def dot(left, right):
    return jnp.dot(left, right, preferred_element_type=jnp.float32)


def phase_columns(shift_ref, offset_ref, angle, rows_of, length):
    lines = lax.broadcasted_iota(jnp.int32, (1, length), 1) - length // 2
    angle[...] = jnp.zeros_like(angle)
    for slot, row in enumerate(rows_of):
        turns = (shift_ref[row] * lines) & (MB - 1)
        angle[slot : slot + 1, :length] = (
            2.0 * math.pi / MB * turns.astype(jnp.float32) + offset_ref[pl.ds(row, 1), :]
        )
    return jnp.cos(angle[...]).T, jnp.sin(angle[...]).T


def encode_kernel(slots, group, picks, *refs):
    shift_ref, order_ref, place_ref, image_ref, map_ref, kspace_ref, offset_ref = refs[:7]
    left_ref, gram_ref, adjoint_ref, kept_ref = refs[7:11]
    out_refs = refs[11:-4]
    total, angle, shifted, copied = refs[-4:]
    vols, coils, length = image_ref.shape[0], map_ref.shape[0], image_ref.shape[-1]
    _, rows, lanes = shifted.shape
    part = rows // len(out_refs)
    groups = order_ref.shape[0]
    whole_classes = picks is not None
    if whole_classes:
        rows_of = [slot * groups + group for slot in range(slots)]
    else:
        rows_of = picks = [place_ref[1]]
    cosines, sines = phase_columns(shift_ref, offset_ref, angle, rows_of, length)
    if lanes > vols * coils * 2 * length:
        last = slice(lanes - LANE_TILE, lanes)
        total[:, last] = jnp.zeros((rows, LANE_TILE), jnp.float32)
        for slot in range(slots):
            shifted[slot, :, last] = jnp.zeros((rows, LANE_TILE), jnp.bfloat16)
    sums, copies = [None] * (vols * coils), []
    for slot, pick in enumerate(picks):
        cosine = cosines[:rows, slot : slot + 1]
        sine = sines[:rows, slot : slot + 1]
        for vol in range(vols):
            image_re = image_ref[vol, pick, 0].astype(jnp.float32)
            image_im = image_ref[vol, pick, 1].astype(jnp.float32)
            for coil in range(coils):
                place = vol * coils + coil
                base = place * 2 * length
                map_re = map_ref[coil, pick, 0].astype(jnp.float32)
                map_im = map_ref[coil, pick, 1].astype(jnp.float32)
                coil_re = (map_re * image_re - map_im * image_im).astype(jnp.bfloat16)
                coil_im = (map_re * image_im + map_im * image_re).astype(jnp.bfloat16)
                partly = dot(left_ref[0], coil_re) + dot(left_ref[1], coil_im)
                part_re, part_im = partly[:rows], partly[rows:]
                shift_re = part_re * cosine - part_im * sine
                shift_im = part_re * sine + part_im * cosine
                shifted[slot, :, base : base + length] = shift_re.astype(jnp.bfloat16)
                shifted[slot, :, base + length : base + 2 * length] = shift_im.astype(
                    jnp.bfloat16
                )
                if slot > 0:
                    shift_re, shift_im = sums[place][0] + shift_re, sums[place][1] + shift_im
                sums[place] = (shift_re, shift_im)
        copy = pltpu.make_async_copy(shifted.at[slot], kept_ref.at[slot], copied.at[slot])
        copy.start()
        copies.append(copy)
    for place, (sum_re, sum_im) in enumerate(sums):
        mixed = dot(sum_re.astype(jnp.bfloat16), gram_ref[0]) + dot(
            sum_im.astype(jnp.bfloat16), gram_ref[1]
        )
        if not whole_classes:
            mixed = jnp.where(place_ref[0] > 0, mixed, 0.0)
        total[:, place * 2 * length : (place + 1) * 2 * length] = mixed

    @pl.when(order_ref[group] == lax.axis_index("slc"))
    def _():
        for vol in range(vols):
            for coil in range(coils):
                place = vol * coils + coil
                measured = dot(kspace_ref[vol, 0, coil, 0], adjoint_ref[0]) + dot(
                    kspace_ref[vol, 0, coil, 1], adjoint_ref[1]
                )
                total[:length, place * 2 * length : (place + 1) * 2 * length] -= measured

    for index, out_ref in enumerate(out_refs):
        out_ref[...] = total[index * part : (index + 1) * part, :].astype(jnp.bfloat16)
    for copy in copies:
        copy.wait()


def gradient_kernel(index, factor, on_line, *refs):
    term_refs, shifted_ref, out_ref = refs[:-2], refs[-2], refs[-1]
    slots, _, lanes = shifted_ref.shape
    part = out_ref.shape[1]
    terms = [ref[...].astype(jnp.float32) for ref in term_refs]
    if on_line:
        own, near, across, rest = terms
        position = lax.axis_index("slc")
        edge = (position == 0) | (position == lax.axis_size("slc") - 1)
        residual = own + jnp.where(edge, rest, near + across)
    else:
        residual = terms[0]
    for slot in range(slots):
        shifted = shifted_ref[slot, index * part : (index + 1) * part, :].astype(jnp.float32)
        product = residual * shifted
        tiles = [product[:, at : at + LANE_TILE] for at in range(0, lanes, LANE_TILE)]
        folded = functools.reduce(lambda a, b: a + b, tiles)
        out_ref[slot : slot + 1, :] = factor * jnp.sum(folded.T, axis=0, keepdims=True)


def after(value, *earlier):
    return lax.optimization_barrier((value, *earlier))[0]


def sum_over_replicas(value):
    axes = ("coil", "vol")
    if any(lax.axis_size(axis) != 2 for axis in axes):
        return lax.psum(value, axes)
    swapped = [
        lax.ppermute(value, axes, [(index, index ^ mask) for index in range(4)])
        for mask in (1, 2, 3)
    ]
    return (value + swapped[0]) + (swapped[1] + swapped[2])


def line_of_four(encode, gradient, count):
    position = lax.axis_index("slc")
    edge = (position == 0) | (position == 3)
    outer_pairs = [(0, 1), (1, 0), (2, 3), (3, 2)]
    inner_pairs = [(0, 0), (1, 2), (2, 1), (3, 3)]
    parts = ROW_PARTS
    pieces, shifted, outer, inner, gradients = [], [], [], [], []

    def encode_next(*earlier):
        group = len(shifted)
        if group * parts < count:
            encoded = encode(group, *earlier)
            shifted.append(encoded[0])
            pieces.extend(encoded[1:])

    def outer_next(*earlier):
        step = len(outer)
        back = step - LAG
        payload = pieces[step] if step < count else None
        if back >= 0:
            others = pieces[back] + inner[back]
            payload = others if payload is None else jnp.where(edge, payload, others)
        if earlier:
            payload = after(payload, *earlier)
        outer.append(lax.ppermute(payload, "slc", outer_pairs))
        return payload

    def gradient_next(*earlier):
        step = len(gradients)
        terms = (pieces[step], outer[step], inner[step], outer[step + LAG])
        own = after(terms[0], *earlier) if earlier else terms[0]
        gradients.append(gradient(step, (own, *terms[1:]), shifted[step // parts]))

    while len(outer) < LAG:
        encode_next()
        while len(outer) < min(LAG, len(pieces)):
            outer_next()
    latest = (pieces[-1],)
    for step in range(count):
        half = pieces[step] + after(outer[step], *latest)
        inner.append(lax.ppermute(half, "slc", inner_pairs))
        latest = ()
        if step >= 1:
            latest = (outer_next(half),)
        if len(pieces) < min(count, step + LAG + 2):
            encode_next(*(latest or (half,)))
        if step >= LAG + 1:
            gradient_next(*latest)
            latest = (*latest, gradients[-1])
    last = outer_next(*latest)
    while len(gradients) < count:
        gradient_next(last)
    return gradients


def body(images, coil_maps, kspace, shift_index, phase_offset, group_order):
    vols, per_device, _, _, length = images.shape
    coils = coil_maps.shape[0]
    groups = lax.axis_size("slc")
    rows = round_up(length, ROW_TILE * ROW_PARTS)
    part = rows // ROW_PARTS
    places = vols * coils
    lanes = round_up(places * 2 * length, LANE_TILE)
    whole_classes = per_device % groups == 0
    slots = max(1, per_device // groups)
    tables = dft_matrices(length, rows)
    factor = 1.0 / (coils * lax.axis_size("coil") * vols * lax.axis_size("vol"))
    first = (lax.axis_index("slc") * per_device) % groups
    on_line = whole_classes and groups == 4
    in_vmem = pl.BlockSpec(memory_space=pltpu.VMEM)
    in_smem = pl.BlockSpec(memory_space=pltpu.SMEM)

    per_half = groups // HALVES

    @functools.cache
    def halves(half):
        lead = lambda array: array.reshape(
            array.shape[0], slots, groups, *array.shape[2:]
        )[:, :, half * per_half : (half + 1) * per_half].reshape(
            array.shape[0], slots * per_half, *array.shape[2:]
        )
        pair = (images, coil_maps)
        if half > 0:
            pair = lax.optimization_barrier((*pair, *held_back))[:2]
        return tuple(lead(array) for array in pair)

    held_back = []

    def encode(group, *earlier):
        if whole_classes:
            place = np.zeros((2,), np.int32)
            image, coil_map = halves(group // per_half)
            picks = [slot * per_half + group % per_half for slot in range(slots)]
        else:
            within = group - first
            held = (within >= 0) & (within < per_device)
            within = jnp.where(held, within, 0)
            place = jnp.stack([held, within]).astype(jnp.int32)
            image, coil_map, picks = images, coil_maps, None
        offset = after(phase_offset, *earlier) if earlier else phase_offset
        outputs = pl.pallas_call(
            functools.partial(encode_kernel, slots, group, picks),
            in_specs=[in_smem] * 3 + [in_vmem] * 7,
            out_specs=[pl.BlockSpec(memory_space=pltpu.HBM)] + [in_vmem] * ROW_PARTS,
            out_shape=[jax.ShapeDtypeStruct((slots, rows, lanes), jnp.bfloat16)]
            + [jax.ShapeDtypeStruct((part, lanes), jnp.bfloat16)] * ROW_PARTS,
            scratch_shapes=[
                pltpu.VMEM((rows, lanes), jnp.float32),
                pltpu.VMEM((round_up(slots, 8), round_up(rows, LANE_TILE)), jnp.float32),
                pltpu.VMEM((slots, rows, lanes), jnp.bfloat16),
                pltpu.SemaphoreType.DMA((slots,)),
            ],
            compiler_params=pltpu.CompilerParams(vmem_limit_bytes=VMEM_BYTES),
            cost_estimate=pl.CostEstimate(
                flops=places * (slots + 1) * 16 * length**3,
                bytes_accessed=6_000_000,
                transcendentals=0,
            ),
            name="encode",
        )(
            shift_index,
            group_order,
            place,
            image,
            coil_map,
            kspace,
            offset,
            *tables,
        )
        held_back.append(outputs[1])
        return outputs

    def gradient(step, terms, encoded):
        return pl.pallas_call(
            functools.partial(gradient_kernel, step % ROW_PARTS, factor, on_line),
            out_shape=jax.ShapeDtypeStruct((slots, part), jnp.float32),
            compiler_params=pltpu.CompilerParams(vmem_limit_bytes=VMEM_BYTES),
            cost_estimate=pl.CostEstimate(
                flops=places * slots * 4 * length**2, bytes_accessed=1_500_000, transcendentals=0
            ),
            name="gradient",
        )(*terms, encoded)

    if on_line:
        gradients = line_of_four(encode, gradient, groups * ROW_PARTS)
    else:
        encoded = [encode(group) for group in range(groups)]
        reduced = lax.psum([list(outputs[1:]) for outputs in encoded], "slc")
        gradients = [
            gradient(index, (piece,), encoded[group][0])
            for group in range(groups)
            for index, piece in enumerate(reduced[group])
        ]
    by_class = jnp.stack(
        [
            jnp.concatenate(gradients[group * ROW_PARTS : (group + 1) * ROW_PARTS], axis=1)
            for group in range(groups)
        ],
        axis=1,
    )[:, :, :length]
    if whole_classes:
        local = by_class.reshape(per_device, length)
    else:
        local = lax.dynamic_slice_in_dim(by_class[0], first, per_device, axis=0)
    return sum_over_replicas(local)


def solution(mesh):
    placed = (
        P(("grp", "vol"), "slc", None, None, None),
        P(("grp", "coil"), "slc", None, None, None),
        P(("grp", "vol"), "slc", "coil", None, None, None),
        P("slc"),
        P("slc", None),
        P(),
    )
    return jax.shard_map(
        body, mesh=mesh, in_specs=placed, out_specs=P(("grp", "slc"), None), check_vma=False
    )
```

```python
import functools
import math

import jax
import jax.numpy as jnp
import ml_dtypes
import numpy as np
from jax import lax
from jax.experimental import pallas as pl
from jax.experimental.pallas import tpu as pltpu
from jax.sharding import PartitionSpec as P

MB = 8
ROW_TILE = 16
LANE_TILE = 128
ROW_PARTS = 2
LAG = 3
VMEM_BYTES = 24 * 1024 * 1024


def round_up(value, multiple):
    return -(-value // multiple) * multiple


def fourier_tables(length):
    positions = np.arange(length, dtype=np.int32)
    product = positions[:, None] * positions[None, :] % length
    radians = np.float32(2.0 * math.pi / length) * product.astype(np.float32)
    factor = np.float32(1.0 / math.sqrt(length))
    return (
        (np.cos(radians) * factor).astype(ml_dtypes.bfloat16),
        (-np.sin(radians) * factor).astype(ml_dtypes.bfloat16),
    )


def dft_matrices(length, rows):
    cos_table, sin_table = fourier_tables(length)
    cosine, sine = cos_table.astype(np.float64), sin_table.astype(np.float64)
    left_re = np.zeros((2 * rows, length), np.float64)
    left_im = np.zeros((2 * rows, length), np.float64)
    left_re[:length], left_re[rows : rows + length] = cosine, sine
    left_im[:length], left_im[rows : rows + length] = -sine, cosine
    gram_re = cosine.T @ cosine + sine.T @ sine
    gram_im = sine.T @ cosine - cosine.T @ sine
    gram = np.stack(
        [np.concatenate([gram_im, -gram_re], 1), np.concatenate([gram_re, gram_im], 1)]
    )
    adjoint = np.stack(
        [np.concatenate([-sine, -cosine], 1), np.concatenate([cosine, -sine], 1)]
    )
    left = np.stack([left_re, left_im])
    gram = np.pad(gram, ((0, 0), (0, round_up(length, LANE_TILE) - length), (0, 0)))
    return tuple(part.astype(ml_dtypes.bfloat16) for part in (left, gram, adjoint))


def dot(left, right):
    return jnp.dot(left, right, preferred_element_type=jnp.float32)


def phase_columns(shift_ref, offset_ref, angle, rows_of, length):
    lines = lax.broadcasted_iota(jnp.int32, (1, length), 1) - length // 2
    angle[...] = jnp.zeros_like(angle)
    for slot, row in enumerate(rows_of):
        turns = (shift_ref[row] * lines) & (MB - 1)
        angle[slot : slot + 1, :length] = (
            2.0 * math.pi / MB * turns.astype(jnp.float32) + offset_ref[pl.ds(row, 1), :]
        )
    return jnp.cos(angle[...]).T, jnp.sin(angle[...]).T


def encode_kernel(slots, group, whole_classes, *refs):
    shift_ref, order_ref, place_ref, image_ref, map_ref, kspace_ref, offset_ref = refs[:7]
    left_ref, gram_ref, adjoint_ref, shifted = refs[7:11]
    out_refs = refs[11:-9]
    total, angle, wide, raw_image, raw_map, raw_kspace, adjoint, arrived, owner_arrived = refs[-9:]
    vols, coils, length = image_ref.shape[0], map_ref.shape[0], image_ref.shape[-1]
    _, rows, lanes = shifted.shape
    part = rows // len(out_refs)
    groups = order_ref.shape[0]
    if whole_classes:
        rows_of = [slot * groups + group for slot in range(slots)]
    else:
        rows_of = [place_ref[1]]
    owner = order_ref[group] == lax.axis_index("slc")

    image_copies, map_copies = {}, {}
    for slot, row in enumerate(rows_of):
        for vol in range(vols):
            image_copies[slot, vol] = pltpu.make_async_copy(
                image_ref.at[vol, row], raw_image.at[vol, slot], arrived.at[slot, vol]
            )
            image_copies[slot, vol].start()
        for coil in range(coils):
            map_copies[slot, coil] = pltpu.make_async_copy(
                map_ref.at[coil, row], raw_map.at[coil, slot], arrived.at[slot, vols + coil]
            )
            map_copies[slot, coil].start()
    owner_copies = [
        pltpu.make_async_copy(kspace_ref, raw_kspace, owner_arrived.at[0]),
        pltpu.make_async_copy(adjoint_ref, adjoint, owner_arrived.at[1]),
    ]

    @pl.when(owner)
    def _():
        for copy in owner_copies:
            copy.start()

    tiles = wide.shape[1]

    def planes(raw, buffer):
        mixed = raw.reshape(2 * length, length)[...].astype(jnp.float32)
        for tile in range(tiles):
            at, end = tile * LANE_TILE, min(length, (tile + 1) * LANE_TILE)
            wide[buffer, tile, :, : end - at] = mixed[:, at:end]
        return [
            jnp.concatenate(
                [wide[buffer, tile, pl.ds(kind, length, stride=2), :] for tile in range(tiles)],
                axis=1,
            )
            for kind in range(2)
        ]

    if tiles * LANE_TILE > length:
        for buffer in range(wide.shape[0]):
            wide[buffer, tiles - 1] = jnp.zeros((2 * length, LANE_TILE), jnp.float32)
    if lanes > vols * coils * 2 * length:
        last = slice(lanes - LANE_TILE, lanes)
        total[:, last] = jnp.zeros((rows, LANE_TILE), jnp.float32)
        for slot in range(slots):
            shifted[slot, :, last] = jnp.zeros((rows, LANE_TILE), jnp.bfloat16)
    cosines, sines = phase_columns(shift_ref, offset_ref, angle, rows_of, length)
    sums = [None] * (vols * coils)
    for slot in range(slots):
        cosine = cosines[:rows, slot : slot + 1]
        sine = sines[:rows, slot : slot + 1]
        for vol in range(vols):
            image_copies[slot, vol].wait()
            image_re, image_im = planes(raw_image.at[vol, slot], 0)
            for coil in range(coils):
                place = vol * coils + coil
                base = place * 2 * length
                if vol == 0:
                    map_copies[slot, coil].wait()
                map_re, map_im = planes(raw_map.at[coil, slot], 1 + coil % 2)
                coil_re = (map_re * image_re - map_im * image_im).astype(jnp.bfloat16)
                coil_im = (map_re * image_im + map_im * image_re).astype(jnp.bfloat16)
                partly = dot(left_ref[0], coil_re) + dot(left_ref[1], coil_im)
                part_re, part_im = partly[:rows], partly[rows:]
                shift_re = part_re * cosine - part_im * sine
                shift_im = part_re * sine + part_im * cosine
                shifted[slot, :, base : base + length] = shift_re[:, :length].astype(jnp.bfloat16)
                shifted[slot, :, base + length : base + 2 * length] = shift_im[:, :length].astype(
                    jnp.bfloat16
                )
                if slot > 0:
                    shift_re, shift_im = sums[place][0] + shift_re, sums[place][1] + shift_im
                sums[place] = (shift_re, shift_im)
    for place, (sum_re, sum_im) in enumerate(sums):
        mixed = dot(sum_re.astype(jnp.bfloat16), gram_ref[0]) + dot(
            sum_im.astype(jnp.bfloat16), gram_ref[1]
        )
        if not whole_classes:
            mixed = jnp.where(place_ref[0] > 0, mixed, 0.0)
        total[:, place * 2 * length : (place + 1) * 2 * length] = mixed

    @pl.when(owner)
    def _():
        for copy in owner_copies:
            copy.wait()
        for vol in range(vols):
            for coil in range(coils):
                place = vol * coils + coil
                real, imaginary = planes(raw_kspace.at[vol, 0, coil], 0)
                measured = dot(real[:, :length].astype(jnp.bfloat16), adjoint[0]) + dot(
                    imaginary[:, :length].astype(jnp.bfloat16), adjoint[1]
                )
                total[:length, place * 2 * length : (place + 1) * 2 * length] -= measured

    for index, out_ref in enumerate(out_refs):
        out_ref[...] = total[index * part : (index + 1) * part, :].astype(jnp.bfloat16)


def gradient_kernel(index, factor, on_line, *refs):
    term_refs, shifted_ref, out_ref = refs[:-2], refs[-2], refs[-1]
    slots, _, lanes = shifted_ref.shape
    part = out_ref.shape[1]
    terms = [ref[...].astype(jnp.float32) for ref in term_refs]
    if on_line:
        own, near, across, rest = terms
        position = lax.axis_index("slc")
        edge = (position == 0) | (position == lax.axis_size("slc") - 1)
        residual = own + jnp.where(edge, rest, near + across)
    else:
        residual = terms[0]
    for slot in range(slots):
        shifted = shifted_ref[slot, index * part : (index + 1) * part, :].astype(jnp.float32)
        product = residual * shifted
        tiles = [product[:, at : at + LANE_TILE] for at in range(0, lanes, LANE_TILE)]
        folded = functools.reduce(lambda a, b: a + b, tiles)
        out_ref[slot : slot + 1, :] = factor * jnp.sum(folded.T, axis=0, keepdims=True)


def after(value, *earlier):
    return lax.optimization_barrier((value, *earlier))[0]


def sum_over_replicas(value):
    axes = ("coil", "vol")
    if any(lax.axis_size(axis) != 2 for axis in axes):
        return lax.psum(value, axes)
    swapped = [
        lax.ppermute(value, axes, [(index, index ^ mask) for index in range(4)])
        for mask in (1, 2, 3)
    ]
    return (value + swapped[0]) + (swapped[1] + swapped[2])


def line_of_four(encode, gradient, count):
    position = lax.axis_index("slc")
    edge = (position == 0) | (position == 3)
    outer_pairs = [(0, 1), (1, 0), (2, 3), (3, 2)]
    inner_pairs = [(0, 0), (1, 2), (2, 1), (3, 3)]
    parts = ROW_PARTS
    pieces, shifted, outer, inner, gradients = [], [], [], [], []

    def encode_next(*earlier):
        group = len(shifted)
        if group * parts < count:
            encoded = encode(group, *earlier)
            shifted.append(encoded[0])
            pieces.extend(encoded[1:])

    def outer_next(*earlier):
        step = len(outer)
        back = step - LAG
        payload = pieces[step] if step < count else None
        if back >= 0:
            others = pieces[back] + inner[back]
            payload = others if payload is None else jnp.where(edge, payload, others)
        if earlier:
            payload = after(payload, *earlier)
        outer.append(lax.ppermute(payload, "slc", outer_pairs))
        return payload

    def gradient_next(*earlier):
        step = len(gradients)
        terms = (pieces[step], outer[step], inner[step], outer[step + LAG])
        own = after(terms[0], *earlier) if earlier else terms[0]
        gradients.append(gradient(step, (own, *terms[1:]), shifted[step // parts]))

    while len(outer) < LAG:
        encode_next()
        while len(outer) < min(LAG, len(pieces)):
            outer_next()
    latest = (pieces[-1],)
    for step in range(count):
        half = pieces[step] + after(outer[step], *latest)
        inner.append(lax.ppermute(half, "slc", inner_pairs))
        latest = ()
        if step >= 1:
            latest = (outer_next(half),)
        if len(pieces) < min(count, step + LAG + 2):
            encode_next(*(latest or (half,)))
            latest = (*latest, pieces[-1])
        if step >= LAG + 1:
            gradient_next(*latest)
            latest = (*latest, gradients[-1])
    last = outer_next(*latest)
    while len(gradients) < count:
        gradient_next(last)
    return gradients


def body(images, coil_maps, kspace, shift_index, phase_offset, group_order):
    vols, per_device, _, _, length = images.shape
    coils = coil_maps.shape[0]
    groups = lax.axis_size("slc")
    rows = round_up(length, ROW_TILE * ROW_PARTS)
    part = rows // ROW_PARTS
    places = vols * coils
    lanes = round_up(places * 2 * length, LANE_TILE)
    whole_classes = per_device % groups == 0
    slots = max(1, per_device // groups)
    tables = dft_matrices(length, rows)
    factor = 1.0 / (coils * lax.axis_size("coil") * vols * lax.axis_size("vol"))
    first = (lax.axis_index("slc") * per_device) % groups
    on_line = whole_classes and groups == 4
    in_vmem = pl.BlockSpec(memory_space=pltpu.VMEM)
    in_smem = pl.BlockSpec(memory_space=pltpu.SMEM)
    in_place = pl.BlockSpec(memory_space=pl.ANY)

    def as_it_lies(array):
        view = jnp.swapaxes(array, -3, -2)
        return pltpu.with_memory_space_constraint(view, pltpu.HBM)

    padded = round_up(length, LANE_TILE)
    left, gram, adjoint = tables
    sources = [as_it_lies(array) for array in (images, coil_maps, kspace)]
    adjoint = pltpu.with_memory_space_constraint(jnp.asarray(adjoint), pltpu.HBM)

    def encode(group, *earlier):
        if whole_classes:
            place = np.zeros((2,), np.int32)
        else:
            within = group - first
            held = (within >= 0) & (within < per_device)
            within = jnp.where(held, within, 0)
            place = jnp.stack([held, within]).astype(jnp.int32)
        offset = after(phase_offset, *earlier) if earlier else phase_offset
        return pl.pallas_call(
            functools.partial(encode_kernel, slots, group, whole_classes),
            in_specs=[in_smem] * 3 + [in_place] * 3 + [in_vmem] * 3 + [in_place],
            out_specs=[in_vmem] * (1 + ROW_PARTS),
            out_shape=[jax.ShapeDtypeStruct((slots, rows, lanes), jnp.bfloat16)]
            + [jax.ShapeDtypeStruct((part, lanes), jnp.bfloat16)] * ROW_PARTS,
            scratch_shapes=[
                pltpu.VMEM((rows, lanes), jnp.float32),
                pltpu.VMEM((round_up(slots, 8), round_up(rows, LANE_TILE)), jnp.float32),
                pltpu.VMEM((3, padded // LANE_TILE, 2 * length, LANE_TILE), jnp.float32),
                pltpu.VMEM((vols, slots, length, 2, length), jnp.bfloat16),
                pltpu.VMEM((coils, slots, length, 2, length), jnp.bfloat16),
                pltpu.VMEM((vols, 1, coils, length, 2, length), jnp.bfloat16),
                pltpu.VMEM((2, length, 2 * length), jnp.bfloat16),
                pltpu.SemaphoreType.DMA((slots, vols + coils)),
                pltpu.SemaphoreType.DMA((2,)),
            ],
            compiler_params=pltpu.CompilerParams(vmem_limit_bytes=VMEM_BYTES),
            cost_estimate=pl.CostEstimate(
                flops=places * (slots + 1) * 16 * length**3,
                bytes_accessed=6_000_000,
                transcendentals=0,
            ),
            name="encode",
        )(shift_index, group_order, place, *sources, offset, left, gram, adjoint)

    def gradient(step, terms, encoded):
        return pl.pallas_call(
            functools.partial(gradient_kernel, step % ROW_PARTS, factor, on_line),
            out_shape=jax.ShapeDtypeStruct((slots, part), jnp.float32),
            compiler_params=pltpu.CompilerParams(vmem_limit_bytes=VMEM_BYTES),
            cost_estimate=pl.CostEstimate(
                flops=places * slots * 4 * length**2, bytes_accessed=1_500_000, transcendentals=0
            ),
            name="gradient",
        )(*terms, encoded)

    if on_line:
        gradients = line_of_four(encode, gradient, groups * ROW_PARTS)
    else:
        encoded = [encode(group) for group in range(groups)]
        reduced = lax.psum([list(outputs[1:]) for outputs in encoded], "slc")
        gradients = [
            gradient(index, (piece,), encoded[group][0])
            for group in range(groups)
            for index, piece in enumerate(reduced[group])
        ]
    by_class = jnp.stack(
        [
            jnp.concatenate(gradients[group * ROW_PARTS : (group + 1) * ROW_PARTS], axis=1)
            for group in range(groups)
        ],
        axis=1,
    )[:, :, :length]
    if whole_classes:
        local = by_class.reshape(per_device, length)
    else:
        local = lax.dynamic_slice_in_dim(by_class[0], first, per_device, axis=0)
    return sum_over_replicas(local)


def solution(mesh):
    placed = (
        P(("grp", "vol"), "slc", None, None, None),
        P(("grp", "coil"), "slc", None, None, None),
        P(("grp", "vol"), "slc", "coil", None, None, None),
        P("slc"),
        P("slc", None),
        P(),
    )
    return jax.shard_map(
        body, mesh=mesh, in_specs=placed, out_specs=P(("grp", "slc"), None), check_vma=False
    )
```

```python
import functools
import math

import jax
import jax.numpy as jnp
import ml_dtypes
import numpy as np
from jax import lax
from jax.experimental import pallas as pl
from jax.experimental.pallas import tpu as pltpu
from jax.sharding import PartitionSpec as P

MB = 8
ROW_TILE = 16
LANE_TILE = 128
ROW_PARTS = 2
LAG = 3
VMEM_BYTES = 24 * 1024 * 1024


def round_up(value, multiple):
    return -(-value // multiple) * multiple


def fourier_tables(length):
    positions = np.arange(length, dtype=np.int32)
    product = positions[:, None] * positions[None, :] % length
    radians = np.float32(2.0 * math.pi / length) * product.astype(np.float32)
    factor = np.float32(1.0 / math.sqrt(length))
    return (
        (np.cos(radians) * factor).astype(ml_dtypes.bfloat16),
        (-np.sin(radians) * factor).astype(ml_dtypes.bfloat16),
    )


def dft_matrices(length, rows):
    cos_table, sin_table = fourier_tables(length)
    cosine, sine = cos_table.astype(np.float64), sin_table.astype(np.float64)
    left_re = np.zeros((2 * rows + 8, length), np.float64)
    left_im = np.zeros((2 * rows + 8, length), np.float64)
    left_re[:length], left_re[rows : rows + length] = cosine, sine
    left_im[:length], left_im[rows : rows + length] = -sine, cosine
    gram_re = cosine.T @ cosine + sine.T @ sine
    gram_im = sine.T @ cosine - cosine.T @ sine
    gram = np.stack(
        [np.concatenate([gram_im, -gram_re], 1), np.concatenate([gram_re, gram_im], 1)]
    )
    adjoint = np.stack(
        [np.concatenate([-sine, -cosine], 1), np.concatenate([cosine, -sine], 1)]
    )
    left = np.stack([left_re, left_im])
    return tuple(part.astype(ml_dtypes.bfloat16) for part in (left, gram, adjoint))


def dot(left, right):
    return jnp.dot(left, right, preferred_element_type=jnp.float32)


def start_all(copies):
    for copy in copies:
        copy.start()


def slice_copies(image_ref, map_ref, image_out, map_out, arrived, rows_of):
    vols, coils = image_ref.shape[0], map_ref.shape[0]
    return [
        pltpu.make_async_copy(
            image_ref.at[vol, row], image_out.at[vol, slot], arrived.at[slot, vol]
        )
        for slot, row in enumerate(rows_of)
        for vol in range(vols)
    ] + [
        pltpu.make_async_copy(
            map_ref.at[coil, row], map_out.at[coil, slot], arrived.at[slot, vols + coil]
        )
        for slot, row in enumerate(rows_of)
        for coil in range(coils)
    ]


def fetch_kernel(rows_of, *refs):
    if rows_of is None:
        rows_of, refs = [refs[0][1]], refs[1:]
    shift_ref, offset_ref, image_ref, map_ref, left_ref = refs[:5]
    image_out, map_out, left_out, phase_out = refs[5:9]
    shift, offset, angle, arrived, small = refs[9:]
    copies = slice_copies(image_ref, map_ref, image_out, map_out, arrived, rows_of)
    copies.append(pltpu.make_async_copy(left_ref, left_out, small.at[0]))
    early = [
        pltpu.make_async_copy(shift_ref, shift, small.at[1]),
        pltpu.make_async_copy(offset_ref, offset, small.at[2]),
    ]
    start_all(early)
    start_all(copies)
    for copy in early:
        copy.wait()
    per_device, length = offset.shape
    lines = lax.broadcasted_iota(jnp.int32, (1, length), 1) - length // 2
    angle[...] = jnp.zeros_like(angle)
    for row in range(per_device):
        turns = (shift[row] * lines) & (MB - 1)
        angle[row : row + 1, :length] = (
            2.0 * math.pi / MB * turns.astype(jnp.float32) + offset[row : row + 1, :]
        )
    phase_out[0] = jnp.cos(angle[...]).T
    phase_out[1] = jnp.sin(angle[...]).T
    for copy in copies:
        copy.wait()


def encode_kernel(slots, group, rows_of, next_rows, *refs):
    whole_classes = rows_of is not None
    if not whole_classes:
        place_ref, refs = refs[0], refs[1:]
        next_rows = next_rows and [place_ref[2]]
    phase_ref, image, coil_map, left_ref = refs[:4]
    order_ref, gram_ref, adjoint_ref, kspace_ref, image_ref, map_ref = refs[4:10]
    shifted, refs = refs[10], refs[11:]
    out_refs, refs = refs[:ROW_PARTS], refs[ROW_PARTS:]
    if next_rows:
        next_image, next_map, refs = refs[0], refs[1], refs[2:]
    total, wide, raw_kspace, gram, adjoint, order, arrived, small = refs
    vols, coils, length = image.shape[0], coil_map.shape[0], image.shape[-1]
    _, rows, lanes = shifted.shape
    part = rows // len(out_refs)
    order_copy = pltpu.make_async_copy(order_ref, order, small.at[0])
    gram_copy = pltpu.make_async_copy(gram_ref, gram, small.at[1])
    owner_copies = [
        pltpu.make_async_copy(kspace_ref, raw_kspace, small.at[2]),
        pltpu.make_async_copy(adjoint_ref, adjoint, small.at[3]),
    ]
    next_copies = []
    if next_rows:
        next_copies = slice_copies(image_ref, map_ref, next_image, next_map, arrived, next_rows)
    start_all([order_copy, gram_copy, *next_copies])

    if lanes > vols * coils * 2 * length:
        last = slice(lanes - LANE_TILE, lanes)
        total[:, last] = jnp.zeros((rows, LANE_TILE), jnp.float32)
        for slot in range(slots):
            shifted[slot, :, last] = jnp.zeros((rows, LANE_TILE), jnp.bfloat16)
    sums = [None] * (vols * coils)
    for slot in range(slots):
        if whole_classes:
            column = rows_of[slot]
            cosine = phase_ref[0, :rows, column : column + 1]
            sine = phase_ref[1, :rows, column : column + 1]
        else:
            cosine, sine = phase_ref[0, :rows], phase_ref[1, :rows]
        for vol in range(vols):
            image_re = image[vol, slot, 0].astype(jnp.float32)
            image_im = image[vol, slot, 1].astype(jnp.float32)
            for coil in range(coils):
                place = vol * coils + coil
                base = place * 2 * length
                map_re = coil_map[coil, slot, 0].astype(jnp.float32)
                map_im = coil_map[coil, slot, 1].astype(jnp.float32)
                coil_re = (map_re * image_re - map_im * image_im).astype(jnp.bfloat16)
                coil_im = (map_re * image_im + map_im * image_re).astype(jnp.bfloat16)
                partly = dot(left_ref[0, : 2 * rows], coil_re) + dot(
                    left_ref[1, : 2 * rows], coil_im
                )
                part_re, part_im = partly[:rows], partly[rows:]
                shift_re = part_re * cosine - part_im * sine
                shift_im = part_re * sine + part_im * cosine
                shifted[slot, :, base : base + length] = shift_re.astype(jnp.bfloat16)
                shifted[slot, :, base + length : base + 2 * length] = shift_im.astype(
                    jnp.bfloat16
                )
                if slot > 0:
                    shift_re, shift_im = sums[place][0] + shift_re, sums[place][1] + shift_im
                sums[place] = (shift_re, shift_im)
        if slot == 0:
            order_copy.wait()
            owner = order[group] == lax.axis_index("slc")

            @pl.when(owner)
            def _():
                start_all(owner_copies)

    gram_copy.wait()
    for place, (sum_re, sum_im) in enumerate(sums):
        mixed = dot(sum_re.astype(jnp.bfloat16), gram[0]) + dot(
            sum_im.astype(jnp.bfloat16), gram[1]
        )
        if not whole_classes:
            mixed = jnp.where(place_ref[0] > 0, mixed, 0.0)
        total[:, place * 2 * length : (place + 1) * 2 * length] = mixed

    @pl.when(owner)
    def _():
        for copy in owner_copies:
            copy.wait()
        for vol in range(vols):
            for coil in range(coils):
                place = vol * coils + coil
                lying = raw_kspace.at[vol, 0, coil].reshape(2 * length, length)[...]
                measured = None
                for kind in range(2):
                    for tile in range(wide.shape[0]):
                        at, end = tile * LANE_TILE, min(length, (tile + 1) * LANE_TILE)
                        if kind == 0:
                            wide[tile, :, : end - at] = lying[:, at:end].astype(jnp.float32)
                        rows_read = wide[tile, pl.ds(kind, length, stride=2), :]
                        term = dot(
                            rows_read[:, : end - at].astype(jnp.bfloat16), adjoint[kind, at:end, :]
                        )
                        measured = term if measured is None else measured + term
                total[:length, place * 2 * length : (place + 1) * 2 * length] -= measured

    for index, out_ref in enumerate(out_refs):
        out_ref[...] = total[index * part : (index + 1) * part, :].astype(jnp.bfloat16)
    for copy in next_copies:
        copy.wait()


def gradient_kernel(index, factor, on_line, *refs):
    term_refs, shifted_ref, out_ref = refs[:-2], refs[-2], refs[-1]
    slots, _, lanes = shifted_ref.shape
    part = out_ref.shape[1]
    terms = [ref[...].astype(jnp.float32) for ref in term_refs]
    if on_line:
        own, near, across, rest = terms
        position = lax.axis_index("slc")
        edge = (position == 0) | (position == lax.axis_size("slc") - 1)
        residual = own + jnp.where(edge, rest, near + across)
    else:
        residual = terms[0]
    for slot in range(slots):
        shifted = shifted_ref[slot, index * part : (index + 1) * part, :].astype(jnp.float32)
        product = residual * shifted
        tiles = [product[:, at : at + LANE_TILE] for at in range(0, lanes, LANE_TILE)]
        folded = functools.reduce(lambda a, b: a + b, tiles)
        out_ref[slot : slot + 1, :] = factor * jnp.sum(folded.T, axis=0, keepdims=True)


def after(value, *earlier):
    return lax.optimization_barrier((value, *earlier))[0]


def sum_over_replicas(value):
    axes = ("coil", "vol")
    if any(lax.axis_size(axis) != 2 for axis in axes):
        return lax.psum(value, axes)
    swapped = [
        lax.ppermute(value, axes, [(index, index ^ mask) for index in range(4)])
        for mask in (1, 2, 3)
    ]
    return (value + swapped[0]) + (swapped[1] + swapped[2])


def line_of_four(encode, gradient, count):
    position = lax.axis_index("slc")
    edge = (position == 0) | (position == 3)
    outer_pairs = [(0, 1), (1, 0), (2, 3), (3, 2)]
    inner_pairs = [(0, 0), (1, 2), (2, 1), (3, 3)]
    parts = ROW_PARTS
    pieces, shifted, outer, inner, gradients = [], [], [], [], []

    def encode_next(*earlier):
        group = len(shifted)
        if group * parts < count:
            encoded = encode(group, *earlier)
            shifted.append(encoded[0])
            pieces.extend(encoded[1:])

    def outer_next(*earlier):
        step = len(outer)
        back = step - LAG
        payload = pieces[step] if step < count else None
        if back >= 0:
            others = pieces[back] + inner[back]
            payload = others if payload is None else jnp.where(edge, payload, others)
        if earlier:
            payload = after(payload, *earlier)
        outer.append(lax.ppermute(payload, "slc", outer_pairs))
        return payload

    def gradient_next(*earlier):
        step = len(gradients)
        terms = (pieces[step], outer[step], inner[step], outer[step + LAG])
        own = after(terms[0], *earlier) if earlier else terms[0]
        gradients.append(gradient(step, (own, *terms[1:]), shifted[step // parts]))

    while len(outer) < LAG:
        encode_next()
        while len(outer) < min(LAG, len(pieces)):
            outer_next()
    latest = (pieces[-1],)
    for step in range(count):
        half = pieces[step] + after(outer[step], *latest)
        inner.append(lax.ppermute(half, "slc", inner_pairs))
        latest = ()
        if step >= 1:
            latest = (outer_next(half),)
        if len(pieces) < min(count, step + LAG + 2):
            encode_next(*(latest or (half,)))
            latest = (*latest, pieces[-1])
        if step >= LAG + 1:
            gradient_next(*latest)
            latest = (*latest, gradients[-1])
    last = outer_next(*latest)
    while len(gradients) < count:
        gradient_next(last)
    return gradients


def body(images, coil_maps, kspace, shift_index, phase_offset, group_order):
    vols, per_device, _, _, length = images.shape
    coils = coil_maps.shape[0]
    groups = lax.axis_size("slc")
    rows = round_up(length, ROW_TILE * ROW_PARTS)
    part = rows // ROW_PARTS
    places = vols * coils
    lanes = round_up(places * 2 * length, LANE_TILE)
    whole_classes = per_device % groups == 0
    slots = max(1, per_device // groups)
    tables = dft_matrices(length, rows)
    factor = 1.0 / (coils * lax.axis_size("coil") * vols * lax.axis_size("vol"))
    first = (lax.axis_index("slc") * per_device) % groups
    on_line = whole_classes and groups == 4
    in_vmem = pl.BlockSpec(memory_space=pltpu.VMEM)
    in_smem = pl.BlockSpec(memory_space=pltpu.SMEM)
    in_place = pl.BlockSpec(memory_space=pl.ANY)

    def in_hbm(array):
        return pltpu.with_memory_space_constraint(jnp.asarray(array), pltpu.HBM)

    def rows_of_class(group):
        return [slot * groups + group for slot in range(slots)] if whole_classes else None

    def place_of(group):
        if whole_classes:
            return ()
        held = [(group + step - first, per_device) for step in range(2)]
        inside = [(within >= 0) & (within < size) for within, size in held]
        rows_held = [jnp.where(yes, held[i][0], 0) for i, yes in enumerate(inside)]
        return (jnp.stack([inside[0], rows_held[0], rows_held[1]]).astype(jnp.int32),)

    left, gram, adjoint = (in_hbm(table) for table in tables)
    lying = [in_hbm(jnp.swapaxes(array, -3, -2)) for array in (images, coil_maps, kspace)]
    order = in_hbm(group_order)
    tiles = round_up(length, LANE_TILE) // LANE_TILE
    raw_shapes = [
        jax.ShapeDtypeStruct((count, slots, length, 2, length), jnp.bfloat16)
        for count in (vols, coils)
    ]
    scalar_specs = [] if whole_classes else [in_smem]
    padded_rows = round_up(rows, LANE_TILE)
    slice_semaphores = pltpu.SemaphoreType.DMA((slots, vols + coils))
    *raw, left, phases = pl.pallas_call(
        functools.partial(fetch_kernel, rows_of_class(0)),
        in_specs=scalar_specs + [in_place] * 5,
        out_specs=[in_vmem] * 4,
        out_shape=raw_shapes
        + [
            jax.ShapeDtypeStruct(left.shape, left.dtype),
            jax.ShapeDtypeStruct((2, padded_rows, per_device), jnp.float32),
        ],
        scratch_shapes=[
            pltpu.SMEM((per_device,), jnp.int32),
            pltpu.VMEM((per_device, length), jnp.float32),
            pltpu.VMEM((per_device, padded_rows), jnp.float32),
            slice_semaphores,
            pltpu.SemaphoreType.DMA((3,)),
        ],
        compiler_params=pltpu.CompilerParams(vmem_limit_bytes=VMEM_BYTES),
        name="fetch",
    )(*place_of(0), in_hbm(shift_index), in_hbm(phase_offset), *lying[:2], left)

    def encode(group, *earlier):
        image, coil_map = (jnp.swapaxes(array, -3, -2) for array in raw)
        has_next = group + 1 < groups
        place, group_phases = place_of(group), phases
        if not whole_classes:
            group_phases = lax.dynamic_slice_in_dim(phases, place[0][1], 1, axis=2)
        if earlier:
            image = after(image, *earlier)
        outputs = pl.pallas_call(
            functools.partial(
                encode_kernel,
                slots,
                group,
                rows_of_class(group),
                (rows_of_class(group + 1) or [0]) if has_next else None,
            ),
            in_specs=scalar_specs + [in_vmem] * 4 + [in_place] * 6,
            out_specs=[in_vmem] * (1 + ROW_PARTS + 2 * has_next),
            out_shape=[jax.ShapeDtypeStruct((slots, rows, lanes), jnp.bfloat16)]
            + [jax.ShapeDtypeStruct((part, lanes), jnp.bfloat16)] * ROW_PARTS
            + raw_shapes * has_next,
            scratch_shapes=[
                pltpu.VMEM((rows, lanes), jnp.float32),
                pltpu.VMEM((tiles, 2 * length, LANE_TILE), jnp.float32),
                pltpu.VMEM(lying[2].shape, jnp.bfloat16),
                pltpu.VMEM(gram.shape, jnp.bfloat16),
                pltpu.VMEM(adjoint.shape, jnp.bfloat16),
                pltpu.SMEM((groups,), jnp.int32),
                slice_semaphores,
                pltpu.SemaphoreType.DMA((4,)),
            ],
            compiler_params=pltpu.CompilerParams(vmem_limit_bytes=VMEM_BYTES),
            cost_estimate=pl.CostEstimate(
                flops=places * (slots + 1) * 16 * length**3,
                bytes_accessed=6_000_000,
                transcendentals=0,
            ),
            name="encode",
        )(
            *place,
            group_phases,
            image,
            coil_map,
            left,
            order,
            gram,
            adjoint,
            lying[2],
            *lying[:2],
        )
        raw[:] = outputs[1 + ROW_PARTS :]
        return outputs[: 1 + ROW_PARTS]

    def gradient(step, terms, encoded):
        return pl.pallas_call(
            functools.partial(gradient_kernel, step % ROW_PARTS, factor, on_line),
            out_shape=jax.ShapeDtypeStruct((slots, part), jnp.float32),
            compiler_params=pltpu.CompilerParams(vmem_limit_bytes=VMEM_BYTES),
            cost_estimate=pl.CostEstimate(
                flops=places * slots * 4 * length**2, bytes_accessed=1_500_000, transcendentals=0
            ),
            name="gradient",
        )(*terms, encoded)

    if on_line:
        gradients = line_of_four(encode, gradient, groups * ROW_PARTS)
    else:
        encoded = [encode(group) for group in range(groups)]
        reduced = lax.psum([list(outputs[1:]) for outputs in encoded], "slc")
        gradients = [
            gradient(index, (piece,), encoded[group][0])
            for group in range(groups)
            for index, piece in enumerate(reduced[group])
        ]
    by_class = jnp.stack(
        [
            jnp.concatenate(gradients[group * ROW_PARTS : (group + 1) * ROW_PARTS], axis=1)
            for group in range(groups)
        ],
        axis=1,
    )[:, :, :length]
    if whole_classes:
        local = by_class.reshape(per_device, length)
    else:
        local = lax.dynamic_slice_in_dim(by_class[0], first, per_device, axis=0)
    return sum_over_replicas(local)


def solution(mesh):
    placed = (
        P(("grp", "vol"), "slc", None, None, None),
        P(("grp", "coil"), "slc", None, None, None),
        P(("grp", "vol"), "slc", "coil", None, None, None),
        P("slc"),
        P("slc", None),
        P(),
    )
    return jax.shard_map(
        body, mesh=mesh, in_specs=placed, out_specs=P(("grp", "slc"), None), check_vma=False
    )
```

```python
import functools
import math

import jax
import jax.numpy as jnp
import ml_dtypes
import numpy as np
from jax import lax
from jax.experimental import pallas as pl
from jax.experimental.pallas import tpu as pltpu
from jax.sharding import PartitionSpec as P

MB = 8
ROW_TILE = 16
LANE_TILE = 128
ROW_PARTS = 1
LAG = 2
VMEM_BYTES = 24 * 1024 * 1024


def round_up(value, multiple):
    return -(-value // multiple) * multiple


def fourier_tables(length):
    positions = np.arange(length, dtype=np.int32)
    product = positions[:, None] * positions[None, :] % length
    radians = np.float32(2.0 * math.pi / length) * product.astype(np.float32)
    factor = np.float32(1.0 / math.sqrt(length))
    return (
        (np.cos(radians) * factor).astype(ml_dtypes.bfloat16),
        (-np.sin(radians) * factor).astype(ml_dtypes.bfloat16),
    )


def dft_matrices(length, rows):
    cos_table, sin_table = fourier_tables(length)
    cosine, sine = cos_table.astype(np.float64), sin_table.astype(np.float64)
    left_re = np.zeros((2 * rows + 8, length), np.float64)
    left_im = np.zeros((2 * rows + 8, length), np.float64)
    left_re[:length], left_re[rows : rows + length] = cosine, sine
    left_im[:length], left_im[rows : rows + length] = -sine, cosine
    gram_re = cosine.T @ cosine + sine.T @ sine
    gram_im = sine.T @ cosine - cosine.T @ sine
    gram = np.stack(
        [np.concatenate([gram_im, -gram_re], 1), np.concatenate([gram_re, gram_im], 1)]
    )
    adjoint = np.stack(
        [np.concatenate([-sine, -cosine], 1), np.concatenate([cosine, -sine], 1)]
    )
    left = np.stack([left_re, left_im])
    return tuple(part.astype(ml_dtypes.bfloat16) for part in (left, gram, adjoint))


def dot(left, right):
    return jnp.dot(left, right, preferred_element_type=jnp.float32)


def start_all(copies):
    for copy in copies:
        copy.start()


def slice_copies(image_ref, map_ref, image_out, map_out, arrived, rows_of):
    vols, coils = image_ref.shape[0], map_ref.shape[0]
    return [
        pltpu.make_async_copy(
            image_ref.at[vol, row], image_out.at[vol, slot], arrived.at[slot, vol]
        )
        for slot, row in enumerate(rows_of)
        for vol in range(vols)
    ] + [
        pltpu.make_async_copy(
            map_ref.at[coil, row], map_out.at[coil, slot], arrived.at[slot, vols + coil]
        )
        for slot, row in enumerate(rows_of)
        for coil in range(coils)
    ]


def fetch_kernel(rows_of, *refs):
    if rows_of is None:
        rows_of, refs = [refs[0][1]], refs[1:]
    shift_ref, offset_ref, image_ref, map_ref, left_ref = refs[:5]
    image_out, map_out, left_out, phase_out = refs[5:9]
    shift, offset, angle, arrived, small = refs[9:]
    copies = slice_copies(image_ref, map_ref, image_out, map_out, arrived, rows_of)
    copies.append(pltpu.make_async_copy(left_ref, left_out, small.at[0]))
    early = [
        pltpu.make_async_copy(shift_ref, shift, small.at[1]),
        pltpu.make_async_copy(offset_ref, offset, small.at[2]),
    ]
    start_all(early)
    start_all(copies)
    for copy in early:
        copy.wait()
    per_device, length = offset.shape
    lines = lax.broadcasted_iota(jnp.int32, (1, length), 1) - length // 2
    angle[...] = jnp.zeros_like(angle)
    for row in range(per_device):
        turns = (shift[row] * lines) & (MB - 1)
        angle[row : row + 1, :length] = (
            2.0 * math.pi / MB * turns.astype(jnp.float32) + offset[row : row + 1, :]
        )
    phase_out[0] = jnp.cos(angle[...]).T
    phase_out[1] = jnp.sin(angle[...]).T
    for copy in copies:
        copy.wait()


def encode_kernel(slots, group, rows_of, next_rows, *refs):
    whole_classes = rows_of is not None
    if not whole_classes:
        place_ref, refs = refs[0], refs[1:]
        next_rows = next_rows and [place_ref[2]]
    phase_ref, image, coil_map, left_ref = refs[:4]
    order_ref, gram_ref, adjoint_ref, kspace_ref, image_ref, map_ref = refs[4:10]
    shifted, refs = refs[10], refs[11:]
    out_refs, refs = refs[:ROW_PARTS], refs[ROW_PARTS:]
    if next_rows:
        next_image, next_map, refs = refs[0], refs[1], refs[2:]
    total, wide, raw_kspace, gram, adjoint, order, arrived, small = refs
    vols, coils, length = image.shape[0], coil_map.shape[0], image.shape[-1]
    _, rows, lanes = shifted.shape
    part = rows // len(out_refs)
    order_copy = pltpu.make_async_copy(order_ref, order, small.at[0])
    gram_copy = pltpu.make_async_copy(gram_ref, gram, small.at[1])
    owner_copies = [
        pltpu.make_async_copy(kspace_ref, raw_kspace, small.at[2]),
        pltpu.make_async_copy(adjoint_ref, adjoint, small.at[3]),
    ]
    next_copies = []
    if next_rows:
        next_copies = slice_copies(image_ref, map_ref, next_image, next_map, arrived, next_rows)
    start_all([order_copy, gram_copy, *next_copies])

    if lanes > vols * coils * 2 * length:
        last = slice(lanes - LANE_TILE, lanes)
        total[:, last] = jnp.zeros((rows, LANE_TILE), jnp.float32)
        for slot in range(slots):
            shifted[slot, :, last] = jnp.zeros((rows, LANE_TILE), jnp.bfloat16)
    sums = [None] * (vols * coils)
    for slot in range(slots):
        if whole_classes:
            column = rows_of[slot]
            cosine = phase_ref[0, :rows, column : column + 1]
            sine = phase_ref[1, :rows, column : column + 1]
        else:
            cosine, sine = phase_ref[0, :rows], phase_ref[1, :rows]
        for vol in range(vols):
            image_re = image[vol, slot, 0].astype(jnp.float32)
            image_im = image[vol, slot, 1].astype(jnp.float32)
            for coil in range(coils):
                place = vol * coils + coil
                base = place * 2 * length
                map_re = coil_map[coil, slot, 0].astype(jnp.float32)
                map_im = coil_map[coil, slot, 1].astype(jnp.float32)
                coil_re = (map_re * image_re - map_im * image_im).astype(jnp.bfloat16)
                coil_im = (map_re * image_im + map_im * image_re).astype(jnp.bfloat16)
                partly = dot(left_ref[0, : 2 * rows], coil_re) + dot(
                    left_ref[1, : 2 * rows], coil_im
                )
                part_re, part_im = partly[:rows], partly[rows:]
                shift_re = part_re * cosine - part_im * sine
                shift_im = part_re * sine + part_im * cosine
                shifted[slot, :, base : base + length] = shift_re.astype(jnp.bfloat16)
                shifted[slot, :, base + length : base + 2 * length] = shift_im.astype(
                    jnp.bfloat16
                )
                if slot > 0:
                    shift_re, shift_im = sums[place][0] + shift_re, sums[place][1] + shift_im
                sums[place] = (shift_re, shift_im)
        if slot == 0:
            order_copy.wait()
            owner = order[group] == lax.axis_index("slc")

            @pl.when(owner)
            def _():
                start_all(owner_copies)

    gram_copy.wait()
    for place, (sum_re, sum_im) in enumerate(sums):
        mixed = dot(sum_re.astype(jnp.bfloat16), gram[0]) + dot(
            sum_im.astype(jnp.bfloat16), gram[1]
        )
        if not whole_classes:
            mixed = jnp.where(place_ref[0] > 0, mixed, 0.0)
        total[:, place * 2 * length : (place + 1) * 2 * length] = mixed

    @pl.when(owner)
    def _():
        for copy in owner_copies:
            copy.wait()
        for vol in range(vols):
            for coil in range(coils):
                place = vol * coils + coil
                lying = raw_kspace.at[vol, 0, coil].reshape(2 * length, length)[...]
                measured = None
                for kind in range(2):
                    for tile in range(wide.shape[0]):
                        at, end = tile * LANE_TILE, min(length, (tile + 1) * LANE_TILE)
                        if kind == 0:
                            wide[tile, :, : end - at] = lying[:, at:end].astype(jnp.float32)
                        rows_read = wide[tile, pl.ds(kind, length, stride=2), :]
                        term = dot(
                            rows_read[:, : end - at].astype(jnp.bfloat16), adjoint[kind, at:end, :]
                        )
                        measured = term if measured is None else measured + term
                total[:length, place * 2 * length : (place + 1) * 2 * length] -= measured

    for index, out_ref in enumerate(out_refs):
        out_ref[...] = total[index * part : (index + 1) * part, :].astype(jnp.bfloat16)
    for copy in next_copies:
        copy.wait()


def gradient_kernel(index, factor, on_line, *refs):
    term_refs, shifted_ref, out_ref = refs[:-2], refs[-2], refs[-1]
    slots, _, lanes = shifted_ref.shape
    part = out_ref.shape[1]
    terms = [ref[...].astype(jnp.float32) for ref in term_refs]
    if on_line:
        own, near, across, rest = terms
        position = lax.axis_index("slc")
        edge = (position == 0) | (position == lax.axis_size("slc") - 1)
        residual = own + jnp.where(edge, rest, near + across)
    else:
        residual = terms[0]
    for slot in range(slots):
        shifted = shifted_ref[slot, index * part : (index + 1) * part, :].astype(jnp.float32)
        product = residual * shifted
        tiles = [product[:, at : at + LANE_TILE] for at in range(0, lanes, LANE_TILE)]
        folded = functools.reduce(lambda a, b: a + b, tiles)
        out_ref[slot : slot + 1, :] = factor * jnp.sum(folded.T, axis=0, keepdims=True)


def after(value, *earlier):
    return lax.optimization_barrier((value, *earlier))[0]


def sum_over_replicas(value):
    axes = ("coil", "vol")
    if any(lax.axis_size(axis) != 2 for axis in axes):
        return lax.psum(value, axes)
    swapped = [
        lax.ppermute(value, axes, [(index, index ^ mask) for index in range(4)])
        for mask in (1, 2, 3)
    ]
    return (value + swapped[0]) + (swapped[1] + swapped[2])


def line_of_four(encode, gradient, count):
    position = lax.axis_index("slc")
    edge = (position == 0) | (position == 3)
    outer_pairs = [(0, 1), (1, 0), (2, 3), (3, 2)]
    inner_pairs = [(0, 0), (1, 2), (2, 1), (3, 3)]
    parts = ROW_PARTS
    pieces, shifted, outer, inner, gradients = [], [], [], [], []

    def encode_next(*earlier):
        group = len(shifted)
        if group * parts < count:
            encoded = encode(group, *earlier)
            shifted.append(encoded[0])
            pieces.extend(encoded[1:])

    def outer_next(*earlier):
        step = len(outer)
        back = step - LAG
        payload = pieces[step] if step < count else None
        if back >= 0:
            others = pieces[back] + inner[back]
            payload = others if payload is None else jnp.where(edge, payload, others)
        if earlier:
            payload = after(payload, *earlier)
        outer.append(lax.ppermute(payload, "slc", outer_pairs))
        return payload

    def gradient_next(*earlier):
        step = len(gradients)
        terms = (pieces[step], outer[step], inner[step], outer[step + LAG])
        own = after(terms[0], *earlier) if earlier else terms[0]
        gradients.append(gradient(step, (own, *terms[1:]), shifted[step // parts]))

    while len(outer) < LAG:
        encode_next()
        while len(outer) < min(LAG, len(pieces)):
            outer_next()
    latest = (pieces[-1],)
    for step in range(count):
        half = pieces[step] + after(outer[step], *latest)
        inner.append(lax.ppermute(half, "slc", inner_pairs))
        latest = ()
        if step >= 1:
            latest = (outer_next(half),)
        if len(pieces) < min(count, step + LAG + 2):
            encode_next(*(latest or (half,)))
            latest = (*latest, pieces[-1])
        if step >= LAG + 1:
            gradient_next(*latest)
            latest = (*latest, gradients[-1])
    last = outer_next(*latest)
    while len(gradients) < count:
        gradient_next(last)
    return gradients


def body(images, coil_maps, kspace, shift_index, phase_offset, group_order):
    vols, per_device, _, _, length = images.shape
    coils = coil_maps.shape[0]
    groups = lax.axis_size("slc")
    rows = round_up(length, ROW_TILE * ROW_PARTS)
    part = rows // ROW_PARTS
    places = vols * coils
    lanes = round_up(places * 2 * length, LANE_TILE)
    whole_classes = per_device % groups == 0
    slots = max(1, per_device // groups)
    tables = dft_matrices(length, rows)
    factor = 1.0 / (coils * lax.axis_size("coil") * vols * lax.axis_size("vol"))
    first = (lax.axis_index("slc") * per_device) % groups
    on_line = whole_classes and groups == 4
    in_vmem = pl.BlockSpec(memory_space=pltpu.VMEM)
    in_smem = pl.BlockSpec(memory_space=pltpu.SMEM)
    in_place = pl.BlockSpec(memory_space=pl.ANY)

    def in_hbm(array):
        return pltpu.with_memory_space_constraint(jnp.asarray(array), pltpu.HBM)

    def rows_of_class(group):
        return [slot * groups + group for slot in range(slots)] if whole_classes else None

    def place_of(group):
        if whole_classes:
            return ()
        held = [(group + step - first, per_device) for step in range(2)]
        inside = [(within >= 0) & (within < size) for within, size in held]
        rows_held = [jnp.where(yes, held[i][0], 0) for i, yes in enumerate(inside)]
        return (jnp.stack([inside[0], rows_held[0], rows_held[1]]).astype(jnp.int32),)

    left, gram, adjoint = (in_hbm(table) for table in tables)
    lying = [in_hbm(jnp.swapaxes(array, -3, -2)) for array in (images, coil_maps, kspace)]
    order = in_hbm(group_order)
    tiles = round_up(length, LANE_TILE) // LANE_TILE
    raw_shapes = [
        jax.ShapeDtypeStruct((count, slots, length, 2, length), jnp.bfloat16)
        for count in (vols, coils)
    ]
    scalar_specs = [] if whole_classes else [in_smem]
    padded_rows = round_up(rows, LANE_TILE)
    slice_semaphores = pltpu.SemaphoreType.DMA((slots, vols + coils))
    *raw, left, phases = pl.pallas_call(
        functools.partial(fetch_kernel, rows_of_class(0)),
        in_specs=scalar_specs + [in_place] * 5,
        out_specs=[in_vmem] * 4,
        out_shape=raw_shapes
        + [
            jax.ShapeDtypeStruct(left.shape, left.dtype),
            jax.ShapeDtypeStruct((2, padded_rows, per_device), jnp.float32),
        ],
        scratch_shapes=[
            pltpu.SMEM((per_device,), jnp.int32),
            pltpu.VMEM((per_device, length), jnp.float32),
            pltpu.VMEM((per_device, padded_rows), jnp.float32),
            slice_semaphores,
            pltpu.SemaphoreType.DMA((3,)),
        ],
        compiler_params=pltpu.CompilerParams(vmem_limit_bytes=VMEM_BYTES),
        name="fetch",
    )(*place_of(0), in_hbm(shift_index), in_hbm(phase_offset), *lying[:2], left)

    def encode(group, *earlier):
        image, coil_map = (jnp.swapaxes(array, -3, -2) for array in raw)
        has_next = group + 1 < groups
        place, group_phases = place_of(group), phases
        if not whole_classes:
            group_phases = lax.dynamic_slice_in_dim(phases, place[0][1], 1, axis=2)
        if earlier:
            image = after(image, *earlier)
        outputs = pl.pallas_call(
            functools.partial(
                encode_kernel,
                slots,
                group,
                rows_of_class(group),
                (rows_of_class(group + 1) or [0]) if has_next else None,
            ),
            in_specs=scalar_specs + [in_vmem] * 4 + [in_place] * 6,
            out_specs=[in_vmem] * (1 + ROW_PARTS + 2 * has_next),
            out_shape=[jax.ShapeDtypeStruct((slots, rows, lanes), jnp.bfloat16)]
            + [jax.ShapeDtypeStruct((part, lanes), jnp.bfloat16)] * ROW_PARTS
            + raw_shapes * has_next,
            scratch_shapes=[
                pltpu.VMEM((rows, lanes), jnp.float32),
                pltpu.VMEM((tiles, 2 * length, LANE_TILE), jnp.float32),
                pltpu.VMEM(lying[2].shape, jnp.bfloat16),
                pltpu.VMEM(gram.shape, jnp.bfloat16),
                pltpu.VMEM(adjoint.shape, jnp.bfloat16),
                pltpu.SMEM((groups,), jnp.int32),
                slice_semaphores,
                pltpu.SemaphoreType.DMA((4,)),
            ],
            compiler_params=pltpu.CompilerParams(vmem_limit_bytes=VMEM_BYTES),
            cost_estimate=pl.CostEstimate(
                flops=places * (slots + 1) * 16 * length**3,
                bytes_accessed=6_000_000,
                transcendentals=0,
            ),
            name="encode",
        )(
            *place,
            group_phases,
            image,
            coil_map,
            left,
            order,
            gram,
            adjoint,
            lying[2],
            *lying[:2],
        )
        raw[:] = outputs[1 + ROW_PARTS :]
        return outputs[: 1 + ROW_PARTS]

    def gradient(step, terms, encoded):
        return pl.pallas_call(
            functools.partial(gradient_kernel, step % ROW_PARTS, factor, on_line),
            out_shape=jax.ShapeDtypeStruct((slots, part), jnp.float32),
            compiler_params=pltpu.CompilerParams(vmem_limit_bytes=VMEM_BYTES),
            cost_estimate=pl.CostEstimate(
                flops=places * slots * 4 * length**2, bytes_accessed=1_500_000, transcendentals=0
            ),
            name="gradient",
        )(*terms, encoded)

    if on_line:
        gradients = line_of_four(encode, gradient, groups * ROW_PARTS)
    else:
        encoded = [encode(group) for group in range(groups)]
        reduced = lax.psum([list(outputs[1:]) for outputs in encoded], "slc")
        gradients = [
            gradient(index, (piece,), encoded[group][0])
            for group in range(groups)
            for index, piece in enumerate(reduced[group])
        ]
    by_class = jnp.stack(
        [
            jnp.concatenate(gradients[group * ROW_PARTS : (group + 1) * ROW_PARTS], axis=1)
            for group in range(groups)
        ],
        axis=1,
    )[:, :, :length]
    if whole_classes:
        local = by_class.reshape(per_device, length)
    else:
        local = lax.dynamic_slice_in_dim(by_class[0], first, per_device, axis=0)
    return sum_over_replicas(local)


def solution(mesh):
    placed = (
        P(("grp", "vol"), "slc", None, None, None),
        P(("grp", "coil"), "slc", None, None, None),
        P(("grp", "vol"), "slc", "coil", None, None, None),
        P("slc"),
        P("slc", None),
        P(),
    )
    return jax.shard_map(
        body, mesh=mesh, in_specs=placed, out_specs=P(("grp", "slc"), None), check_vma=False
    )
```

```python
import functools
import math

import jax
import jax.numpy as jnp
import ml_dtypes
import numpy as np
from jax import lax
from jax.experimental import pallas as pl
from jax.experimental.pallas import tpu as pltpu
from jax.sharding import PartitionSpec as P

MB = 8
ROW_TILE = 16
LANE_TILE = 128
SPLIT = 2
VMEM_BYTES = 24 * 1024 * 1024


def round_up(value, multiple):
    return -(-value // multiple) * multiple


def fourier_tables(length):
    positions = np.arange(length, dtype=np.int32)
    product = positions[:, None] * positions[None, :] % length
    radians = np.float32(2.0 * math.pi / length) * product.astype(np.float32)
    factor = np.float32(1.0 / math.sqrt(length))
    return (
        (np.cos(radians) * factor).astype(ml_dtypes.bfloat16),
        (-np.sin(radians) * factor).astype(ml_dtypes.bfloat16),
    )


def dft_matrices(length, rows):
    cos_table, sin_table = fourier_tables(length)
    cosine, sine = cos_table.astype(np.float64), sin_table.astype(np.float64)
    left_re = np.zeros((2 * rows + 8, length), np.float64)
    left_im = np.zeros((2 * rows + 8, length), np.float64)
    left_re[:length], left_re[rows : rows + length] = cosine, sine
    left_im[:length], left_im[rows : rows + length] = -sine, cosine
    gram_re = cosine.T @ cosine + sine.T @ sine
    gram_im = sine.T @ cosine - cosine.T @ sine
    gram = np.stack(
        [np.concatenate([gram_im, -gram_re], 1), np.concatenate([gram_re, gram_im], 1)]
    )
    adjoint = np.stack(
        [np.concatenate([-sine, -cosine], 1), np.concatenate([cosine, -sine], 1)]
    )
    left = np.stack([left_re, left_im])
    return tuple(part.astype(ml_dtypes.bfloat16) for part in (left, gram, adjoint))


def dot(left, right):
    return jnp.dot(left, right, preferred_element_type=jnp.float32)


def start_all(copies):
    for copy in copies:
        copy.start()


def slice_copies(image_ref, map_ref, image_out, map_out, arrived, rows_of):
    vols, coils = image_ref.shape[0], map_ref.shape[0]
    return [
        pltpu.make_async_copy(
            image_ref.at[vol, row], image_out.at[vol, slot], arrived.at[slot, vol]
        )
        for slot, row in enumerate(rows_of)
        for vol in range(vols)
    ] + [
        pltpu.make_async_copy(
            map_ref.at[coil, row], map_out.at[coil, slot], arrived.at[slot, vols + coil]
        )
        for slot, row in enumerate(rows_of)
        for coil in range(coils)
    ]


def fetch_kernel(rows_of, *refs):
    if rows_of is None:
        rows_of, refs = [refs[0][1]], refs[1:]
    shift_ref, offset_ref, image_ref, map_ref, left_ref = refs[:5]
    image_out, map_out, left_out, phase_out = refs[5:9]
    shift, offset, angle, arrived, small = refs[9:]
    copies = slice_copies(image_ref, map_ref, image_out, map_out, arrived, rows_of)
    copies.append(pltpu.make_async_copy(left_ref, left_out, small.at[0]))
    early = [
        pltpu.make_async_copy(shift_ref, shift, small.at[1]),
        pltpu.make_async_copy(offset_ref, offset, small.at[2]),
    ]
    start_all(early)
    start_all(copies)
    for copy in early:
        copy.wait()
    per_device, length = offset.shape
    lines = lax.broadcasted_iota(jnp.int32, (1, length), 1) - length // 2
    angle[...] = jnp.zeros_like(angle)
    for row in range(per_device):
        turns = (shift[row] * lines) & (MB - 1)
        angle[row : row + 1, :length] = (
            2.0 * math.pi / MB * turns.astype(jnp.float32) + offset[row : row + 1, :]
        )
    phase_out[0] = jnp.cos(angle[...]).T
    phase_out[1] = jnp.sin(angle[...]).T
    for copy in copies:
        copy.wait()


def encode_kernel(slots, parts, group, rows_of, next_rows, *refs):
    whole_classes = rows_of is not None
    if not whole_classes:
        place_ref, refs = refs[0], refs[1:]
        next_rows = next_rows and [place_ref[2]]
    phase_ref, image, coil_map, left_ref = refs[:4]
    order_ref, gram_ref, adjoint_ref, kspace_ref, image_ref, map_ref = refs[4:10]
    shifted, refs = refs[10], refs[11:]
    out_refs, refs = refs[:parts], refs[parts:]
    if next_rows:
        next_image, next_map, refs = refs[0], refs[1], refs[2:]
    total, wide, raw_kspace, gram, adjoint, order, arrived, small = refs
    vols, coils, length = image.shape[0], coil_map.shape[0], image.shape[-1]
    _, rows, lanes = shifted.shape
    part = rows // len(out_refs)
    order_copy = pltpu.make_async_copy(order_ref, order, small.at[0])
    gram_copy = pltpu.make_async_copy(gram_ref, gram, small.at[1])
    owner_copies = [
        pltpu.make_async_copy(kspace_ref, raw_kspace, small.at[2]),
        pltpu.make_async_copy(adjoint_ref, adjoint, small.at[3]),
    ]
    next_copies = []
    if next_rows:
        next_copies = slice_copies(image_ref, map_ref, next_image, next_map, arrived, next_rows)
    start_all([order_copy, gram_copy, *next_copies])

    if lanes > vols * coils * 2 * length:
        last = slice(lanes - LANE_TILE, lanes)
        total[:, last] = jnp.zeros((rows, LANE_TILE), jnp.float32)
        for slot in range(slots):
            shifted[slot, :, last] = jnp.zeros((rows, LANE_TILE), jnp.bfloat16)
    sums = [None] * (vols * coils)
    for slot in range(slots):
        if whole_classes:
            column = rows_of[slot]
            cosine = phase_ref[0, :rows, column : column + 1]
            sine = phase_ref[1, :rows, column : column + 1]
        else:
            cosine, sine = phase_ref[0, :rows], phase_ref[1, :rows]
        for vol in range(vols):
            image_re = image[vol, slot, 0].astype(jnp.float32)
            image_im = image[vol, slot, 1].astype(jnp.float32)
            for coil in range(coils):
                place = vol * coils + coil
                base = place * 2 * length
                map_re = coil_map[coil, slot, 0].astype(jnp.float32)
                map_im = coil_map[coil, slot, 1].astype(jnp.float32)
                coil_re = (map_re * image_re - map_im * image_im).astype(jnp.bfloat16)
                coil_im = (map_re * image_im + map_im * image_re).astype(jnp.bfloat16)
                partly = dot(left_ref[0, : 2 * rows], coil_re) + dot(
                    left_ref[1, : 2 * rows], coil_im
                )
                part_re, part_im = partly[:rows], partly[rows:]
                shift_re = part_re * cosine - part_im * sine
                shift_im = part_re * sine + part_im * cosine
                shifted[slot, :, base : base + length] = shift_re.astype(jnp.bfloat16)
                shifted[slot, :, base + length : base + 2 * length] = shift_im.astype(
                    jnp.bfloat16
                )
                if slot > 0:
                    shift_re, shift_im = sums[place][0] + shift_re, sums[place][1] + shift_im
                sums[place] = (shift_re, shift_im)
        if slot == 0:
            order_copy.wait()
            owner = order[group] == lax.axis_index("slc")

            @pl.when(owner)
            def _():
                start_all(owner_copies)

    gram_copy.wait()
    for place, (sum_re, sum_im) in enumerate(sums):
        mixed = dot(sum_re.astype(jnp.bfloat16), gram[0]) + dot(
            sum_im.astype(jnp.bfloat16), gram[1]
        )
        if not whole_classes:
            mixed = jnp.where(place_ref[0] > 0, mixed, 0.0)
        total[:, place * 2 * length : (place + 1) * 2 * length] = mixed

    @pl.when(owner)
    def _():
        for copy in owner_copies:
            copy.wait()
        for vol in range(vols):
            for coil in range(coils):
                place = vol * coils + coil
                lying = raw_kspace.at[vol, 0, coil].reshape(2 * length, length)[...]
                measured = None
                for kind in range(2):
                    for tile in range(wide.shape[0]):
                        at, end = tile * LANE_TILE, min(length, (tile + 1) * LANE_TILE)
                        if kind == 0:
                            wide[tile, :, : end - at] = lying[:, at:end].astype(jnp.float32)
                        rows_read = wide[tile, pl.ds(kind, length, stride=2), :]
                        term = dot(
                            rows_read[:, : end - at].astype(jnp.bfloat16), adjoint[kind, at:end, :]
                        )
                        measured = term if measured is None else measured + term
                total[:length, place * 2 * length : (place + 1) * 2 * length] -= measured

    for index, out_ref in enumerate(out_refs):
        out_ref[...] = total[index * part : (index + 1) * part, :].astype(jnp.bfloat16)
    for copy in next_copies:
        copy.wait()


def gradient_kernel(start, factor, on_line, *refs):
    term_refs, shifted_ref, out_ref = refs[:-2], refs[-2], refs[-1]
    slots, rows, lanes = shifted_ref.shape
    part = out_ref.shape[1]
    span = slice(start, start + part)
    terms = [
        (ref[span, :] if ref.shape[0] == rows else ref[...]).astype(jnp.float32)
        for ref in term_refs
    ]
    if on_line:
        own, near, across, rest = terms
        position = lax.axis_index("slc")
        edge = (position == 0) | (position == lax.axis_size("slc") - 1)
        residual = own + jnp.where(edge, rest, near + across)
    else:
        residual = terms[0]
    for slot in range(slots):
        product = residual * shifted_ref[slot, span, :].astype(jnp.float32)
        tiles = [product[:, at : at + LANE_TILE] for at in range(0, lanes, LANE_TILE)]
        folded = functools.reduce(lambda a, b: a + b, tiles)
        out_ref[slot : slot + 1, :] = factor * jnp.sum(folded.T, axis=0, keepdims=True)


def after(value, *earlier):
    return lax.optimization_barrier((value, *earlier))[0]


def sum_over_replicas(value):
    axes = ("coil", "vol")
    if any(lax.axis_size(axis) != 2 for axis in axes):
        return lax.psum(value, axes)
    swapped = [
        lax.ppermute(value, axes, [(index, index ^ mask) for index in range(4)])
        for mask in (1, 2, 3)
    ]
    return (value + swapped[0]) + (swapped[1] + swapped[2])


def line_of_four(encode, gradient):
    position = lax.axis_index("slc")
    edge = (position == 0) | (position == 3)

    def outer(value):
        return lax.ppermute(value, "slc", [(0, 1), (1, 0), (2, 3), (3, 2)])

    def inner(value):
        return lax.ppermute(value, "slc", [(0, 0), (1, 2), (2, 1), (3, 3)])

    def halves(value):
        middle = value.shape[0] // SPLIT
        return value[:middle], value[middle:]

    shifted0, own0a, own0b = encode(0, SPLIT)
    near0a = outer(own0a)
    shifted1, own1 = encode(1, 1)
    near0b = outer(after(own0b, own1))
    shifted2, own2 = encode(2, 1, own1)
    near1 = outer(after(own1, own2))
    half0a = own0a + after(near0a, own2)
    across0a = inner(half0a)
    shifted3, own3 = encode(3, 1, half0a)
    half0b = own0b + after(near0b, own3)
    across0b = inner(half0b)
    back0 = jnp.concatenate([own0a + after(across0a, half0b), own0b + across0b], axis=0)
    payload2 = jnp.where(edge, own2, back0)
    near2 = outer(payload2)
    half1 = own1 + after(near1, payload2)
    across1 = inner(half1)
    half2 = own2 + after(near2, half1)
    across2 = inner(half2)
    payload3 = jnp.where(edge, own3, own1 + after(across1, half2))
    near3 = outer(payload3)
    gradient0a = gradient(0, 0, (after(own0a, payload3), near0a, across0a, near2), shifted0)
    gradient0b = gradient(0, 1, (after(own0b, payload3), near0b, across0b, near2), shifted0)
    back2 = own2 + after(across2, gradient0a, gradient0b)
    rest2 = outer(back2)
    own3a, own3b = halves(own3)
    near3a, near3b = halves(near3)
    half3a = own3a + after(near3a, back2)
    across3a = inner(half3a)
    half3b = own3b + after(near3b, half3a)
    gradient1 = gradient(1, None, (after(own1, half3a), near1, across1, near3), shifted1)
    across3b = inner(after(half3b, gradient1))
    back3a = own3a + after(across3a, half3b, gradient1)
    rest3a = outer(back3a)
    back3b = own3b + after(across3b, back3a)
    rest3b = outer(back3b)
    gradient2 = gradient(2, None, (after(own2, back3b), near2, across2, rest2), shifted2)
    gradient3a = gradient(3, 0, (own3a, near3a, across3a, rest3a), shifted3)
    gradient3b = gradient(3, 1, (own3b, near3b, across3b, rest3b), shifted3)
    return [
        jnp.concatenate([gradient0a, gradient0b], axis=1),
        gradient1,
        gradient2,
        jnp.concatenate([gradient3a, gradient3b], axis=1),
    ]


def body(images, coil_maps, kspace, shift_index, phase_offset, group_order):
    vols, per_device, _, _, length = images.shape
    coils = coil_maps.shape[0]
    groups = lax.axis_size("slc")
    rows = round_up(length, ROW_TILE * SPLIT)
    places = vols * coils
    lanes = round_up(places * 2 * length, LANE_TILE)
    whole_classes = per_device % groups == 0
    slots = max(1, per_device // groups)
    tables = dft_matrices(length, rows)
    factor = 1.0 / (coils * lax.axis_size("coil") * vols * lax.axis_size("vol"))
    first = (lax.axis_index("slc") * per_device) % groups
    on_line = whole_classes and groups == 4
    in_vmem = pl.BlockSpec(memory_space=pltpu.VMEM)
    in_smem = pl.BlockSpec(memory_space=pltpu.SMEM)
    in_place = pl.BlockSpec(memory_space=pl.ANY)

    def in_hbm(array):
        return pltpu.with_memory_space_constraint(jnp.asarray(array), pltpu.HBM)

    def rows_of_class(group):
        return [slot * groups + group for slot in range(slots)] if whole_classes else None

    def place_of(group):
        if whole_classes:
            return ()
        held = [(group + step - first, per_device) for step in range(2)]
        inside = [(within >= 0) & (within < size) for within, size in held]
        rows_held = [jnp.where(yes, held[i][0], 0) for i, yes in enumerate(inside)]
        return (jnp.stack([inside[0], rows_held[0], rows_held[1]]).astype(jnp.int32),)

    left, gram, adjoint = (in_hbm(table) for table in tables)
    lying = [in_hbm(jnp.swapaxes(array, -3, -2)) for array in (images, coil_maps, kspace)]
    order = in_hbm(group_order)
    tiles = round_up(length, LANE_TILE) // LANE_TILE
    raw_shapes = [
        jax.ShapeDtypeStruct((count, slots, length, 2, length), jnp.bfloat16)
        for count in (vols, coils)
    ]
    scalar_specs = [] if whole_classes else [in_smem]
    padded_rows = round_up(rows, LANE_TILE)
    slice_semaphores = pltpu.SemaphoreType.DMA((slots, vols + coils))
    *raw, left, phases = pl.pallas_call(
        functools.partial(fetch_kernel, rows_of_class(0)),
        in_specs=scalar_specs + [in_place] * 5,
        out_specs=[in_vmem] * 4,
        out_shape=raw_shapes
        + [
            jax.ShapeDtypeStruct(left.shape, left.dtype),
            jax.ShapeDtypeStruct((2, padded_rows, per_device), jnp.float32),
        ],
        scratch_shapes=[
            pltpu.SMEM((per_device,), jnp.int32),
            pltpu.VMEM((per_device, length), jnp.float32),
            pltpu.VMEM((per_device, padded_rows), jnp.float32),
            slice_semaphores,
            pltpu.SemaphoreType.DMA((3,)),
        ],
        compiler_params=pltpu.CompilerParams(vmem_limit_bytes=VMEM_BYTES),
        name="fetch",
    )(*place_of(0), in_hbm(shift_index), in_hbm(phase_offset), *lying[:2], left)

    def encode(group, parts, *earlier):
        image, coil_map = (jnp.swapaxes(array, -3, -2) for array in raw)
        has_next = group + 1 < groups
        place, group_phases = place_of(group), phases
        if not whole_classes:
            group_phases = lax.dynamic_slice_in_dim(phases, place[0][1], 1, axis=2)
        if earlier:
            image = after(image, *earlier)
        outputs = pl.pallas_call(
            functools.partial(
                encode_kernel,
                slots,
                parts,
                group,
                rows_of_class(group),
                (rows_of_class(group + 1) or [0]) if has_next else None,
            ),
            in_specs=scalar_specs + [in_vmem] * 4 + [in_place] * 6,
            out_specs=[in_vmem] * (1 + parts + 2 * has_next),
            out_shape=[jax.ShapeDtypeStruct((slots, rows, lanes), jnp.bfloat16)]
            + [jax.ShapeDtypeStruct((rows // parts, lanes), jnp.bfloat16)] * parts
            + raw_shapes * has_next,
            scratch_shapes=[
                pltpu.VMEM((rows, lanes), jnp.float32),
                pltpu.VMEM((tiles, 2 * length, LANE_TILE), jnp.float32),
                pltpu.VMEM(lying[2].shape, jnp.bfloat16),
                pltpu.VMEM(gram.shape, jnp.bfloat16),
                pltpu.VMEM(adjoint.shape, jnp.bfloat16),
                pltpu.SMEM((groups,), jnp.int32),
                slice_semaphores,
                pltpu.SemaphoreType.DMA((4,)),
            ],
            compiler_params=pltpu.CompilerParams(vmem_limit_bytes=VMEM_BYTES),
            cost_estimate=pl.CostEstimate(
                flops=length**3, bytes_accessed=length**2, transcendentals=0
            ),
            name="encode",
        )(
            *place,
            group_phases,
            image,
            coil_map,
            left,
            order,
            gram,
            adjoint,
            lying[2],
            *lying[:2],
        )
        raw[:] = outputs[1 + parts :]
        return outputs[: 1 + parts]

    def gradient(group, half, terms, encoded):
        part = rows if half is None else rows // SPLIT
        return pl.pallas_call(
            functools.partial(gradient_kernel, (half or 0) * part, factor, on_line),
            out_shape=jax.ShapeDtypeStruct((slots, part), jnp.float32),
            compiler_params=pltpu.CompilerParams(vmem_limit_bytes=VMEM_BYTES),
            cost_estimate=pl.CostEstimate(
                flops=length**2, bytes_accessed=length**2, transcendentals=0
            ),
            name="gradient",
        )(*terms, encoded)

    if on_line:
        gradients = line_of_four(encode, gradient)
    else:
        encoded = [encode(group, 1) for group in range(groups)]
        reduced = lax.psum([own for _, own in encoded], "slc")
        gradients = [
            gradient(group, None, (reduced[group],), encoded[group][0]) for group in range(groups)
        ]
    by_class = jnp.stack(gradients, axis=1)[:, :, :length]
    if whole_classes:
        local = by_class.reshape(per_device, length)
    else:
        local = lax.dynamic_slice_in_dim(by_class[0], first, per_device, axis=0)
    return sum_over_replicas(local)


def solution(mesh):
    placed = (
        P(("grp", "vol"), "slc", None, None, None),
        P(("grp", "coil"), "slc", None, None, None),
        P(("grp", "vol"), "slc", "coil", None, None, None),
        P("slc"),
        P("slc", None),
        P(),
    )
    return jax.shard_map(
        body, mesh=mesh, in_specs=placed, out_specs=P(("grp", "slc"), None), check_vma=False
    )
```

```python
import functools
import math

import jax
import jax.numpy as jnp
import ml_dtypes
import numpy as np
from jax import lax
from jax.experimental import pallas as pl
from jax.experimental.pallas import tpu as pltpu
from jax.sharding import PartitionSpec as P

MB = 8
ROW_TILE = 16
LANE_TILE = 128
VMEM_BYTES = 24 * 1024 * 1024


def round_up(value, multiple):
    return -(-value // multiple) * multiple


def fourier_tables(length):
    positions = np.arange(length, dtype=np.int32)
    product = positions[:, None] * positions[None, :] % length
    radians = np.float32(2.0 * math.pi / length) * product.astype(np.float32)
    factor = np.float32(1.0 / math.sqrt(length))
    return (
        (np.cos(radians) * factor).astype(ml_dtypes.bfloat16),
        (-np.sin(radians) * factor).astype(ml_dtypes.bfloat16),
    )


def dft_matrices(length, rows):
    cos_table, sin_table = fourier_tables(length)
    cosine, sine = cos_table.astype(np.float64), sin_table.astype(np.float64)
    left_re = np.zeros((2 * rows + 8, length), np.float64)
    left_im = np.zeros((2 * rows + 8, length), np.float64)
    left_re[:length], left_re[rows : rows + length] = cosine, sine
    left_im[:length], left_im[rows : rows + length] = -sine, cosine
    gram_re = cosine.T @ cosine + sine.T @ sine
    gram_im = sine.T @ cosine - cosine.T @ sine
    gram = np.stack(
        [np.concatenate([gram_im, -gram_re], 1), np.concatenate([gram_re, gram_im], 1)]
    )
    adjoint = np.stack(
        [np.concatenate([-sine, -cosine], 1), np.concatenate([cosine, -sine], 1)]
    )
    left = np.stack([left_re, left_im])
    return tuple(part.astype(ml_dtypes.bfloat16) for part in (left, gram, adjoint))


def dot(left, right):
    return jnp.dot(left, right, preferred_element_type=jnp.float32)


def start_all(copies):
    for copy in copies:
        copy.start()


def slice_copies(image_ref, map_ref, image_out, map_out, arrived, rows_of):
    vols, coils = image_ref.shape[0], map_ref.shape[0]
    return [
        pltpu.make_async_copy(
            image_ref.at[vol, row], image_out.at[vol, slot], arrived.at[slot, vol]
        )
        for slot, row in enumerate(rows_of)
        for vol in range(vols)
    ] + [
        pltpu.make_async_copy(
            map_ref.at[coil, row], map_out.at[coil, slot], arrived.at[slot, vols + coil]
        )
        for slot, row in enumerate(rows_of)
        for coil in range(coils)
    ]


def fetch_kernel(rows_of, *refs):
    if rows_of is None:
        rows_of, refs = [refs[0][1]], refs[1:]
    shift_ref, offset_ref, image_ref, map_ref, left_ref = refs[:5]
    image_out, map_out, left_out, phase_out = refs[5:9]
    shift, offset, angle, arrived, small = refs[9:]
    copies = slice_copies(image_ref, map_ref, image_out, map_out, arrived, rows_of)
    copies.append(pltpu.make_async_copy(left_ref, left_out, small.at[0]))
    early = [
        pltpu.make_async_copy(shift_ref, shift, small.at[1]),
        pltpu.make_async_copy(offset_ref, offset, small.at[2]),
    ]
    start_all(early)
    start_all(copies)
    for copy in early:
        copy.wait()
    per_device, length = offset.shape
    lines = lax.broadcasted_iota(jnp.int32, (1, length), 1) - length // 2
    angle[...] = jnp.zeros_like(angle)
    for row in range(per_device):
        turns = (shift[row] * lines) & (MB - 1)
        angle[row : row + 1, :length] = (
            2.0 * math.pi / MB * turns.astype(jnp.float32) + offset[row : row + 1, :]
        )
    phase_out[0] = jnp.cos(angle[...]).T
    phase_out[1] = jnp.sin(angle[...]).T
    for copy in copies:
        copy.wait()


def encode_kernel(slots, group, rows_of, next_rows, *refs):
    whole_classes = rows_of is not None
    if not whole_classes:
        place_ref, refs = refs[0], refs[1:]
        next_rows = next_rows and [place_ref[2]]
    phase_ref, image, coil_map, left_ref = refs[:4]
    order_ref, gram_ref, adjoint_ref, kspace_ref, image_ref, map_ref = refs[4:10]
    shifted, refs = refs[10], refs[11:]
    out_ref, refs = refs[0], refs[1:]
    if next_rows:
        next_image, next_map, refs = refs[0], refs[1], refs[2:]
    total, wide, raw_kspace, gram, adjoint, order, arrived, small = refs
    vols, coils, length = image.shape[0], coil_map.shape[0], image.shape[-1]
    _, rows, lanes = shifted.shape
    order_copy = pltpu.make_async_copy(order_ref, order, small.at[0])
    gram_copy = pltpu.make_async_copy(gram_ref, gram, small.at[1])
    owner_copies = [
        pltpu.make_async_copy(kspace_ref, raw_kspace, small.at[2]),
        pltpu.make_async_copy(adjoint_ref, adjoint, small.at[3]),
    ]
    next_copies = []
    if next_rows:
        next_copies = slice_copies(image_ref, map_ref, next_image, next_map, arrived, next_rows)
    start_all([order_copy, gram_copy, *next_copies])

    if lanes > vols * coils * 2 * length:
        last = slice(lanes - LANE_TILE, lanes)
        total[:, last] = jnp.zeros((rows, LANE_TILE), jnp.float32)
        for slot in range(slots):
            shifted[slot, :, last] = jnp.zeros((rows, LANE_TILE), jnp.bfloat16)
    sums = [None] * (vols * coils)
    for slot in range(slots):
        if whole_classes:
            column = rows_of[slot]
            cosine = phase_ref[0, :rows, column : column + 1]
            sine = phase_ref[1, :rows, column : column + 1]
        else:
            cosine, sine = phase_ref[0, :rows], phase_ref[1, :rows]
        for vol in range(vols):
            image_re = image[vol, slot, 0].astype(jnp.float32)
            image_im = image[vol, slot, 1].astype(jnp.float32)
            for coil in range(coils):
                place = vol * coils + coil
                base = place * 2 * length
                map_re = coil_map[coil, slot, 0].astype(jnp.float32)
                map_im = coil_map[coil, slot, 1].astype(jnp.float32)
                coil_re = (map_re * image_re - map_im * image_im).astype(jnp.bfloat16)
                coil_im = (map_re * image_im + map_im * image_re).astype(jnp.bfloat16)
                partly = dot(left_ref[0, : 2 * rows], coil_re) + dot(
                    left_ref[1, : 2 * rows], coil_im
                )
                part_re, part_im = partly[:rows], partly[rows:]
                shift_re = part_re * cosine - part_im * sine
                shift_im = part_re * sine + part_im * cosine
                shifted[slot, :, base : base + length] = shift_re.astype(jnp.bfloat16)
                shifted[slot, :, base + length : base + 2 * length] = shift_im.astype(
                    jnp.bfloat16
                )
                if slot > 0:
                    shift_re, shift_im = sums[place][0] + shift_re, sums[place][1] + shift_im
                sums[place] = (shift_re, shift_im)
        if slot == 0:
            order_copy.wait()
            owner = order[group] == lax.axis_index("slc")

            @pl.when(owner)
            def _():
                start_all(owner_copies)

    gram_copy.wait()
    for place, (sum_re, sum_im) in enumerate(sums):
        mixed = dot(sum_re.astype(jnp.bfloat16), gram[0]) + dot(
            sum_im.astype(jnp.bfloat16), gram[1]
        )
        if not whole_classes:
            mixed = jnp.where(place_ref[0] > 0, mixed, 0.0)
        total[:, place * 2 * length : (place + 1) * 2 * length] = mixed

    @pl.when(owner)
    def _():
        for copy in owner_copies:
            copy.wait()
        for vol in range(vols):
            for coil in range(coils):
                place = vol * coils + coil
                lying = raw_kspace.at[vol, 0, coil].reshape(2 * length, length)[...]
                measured = None
                for kind in range(2):
                    for tile in range(wide.shape[0]):
                        at, end = tile * LANE_TILE, min(length, (tile + 1) * LANE_TILE)
                        if kind == 0:
                            wide[tile, :, : end - at] = lying[:, at:end].astype(jnp.float32)
                        rows_read = wide[tile, pl.ds(kind, length, stride=2), :]
                        term = dot(
                            rows_read[:, : end - at].astype(jnp.bfloat16), adjoint[kind, at:end, :]
                        )
                        measured = term if measured is None else measured + term
                total[:length, place * 2 * length : (place + 1) * 2 * length] -= measured

    out_ref[...] = total[...].astype(jnp.bfloat16)
    for copy in next_copies:
        copy.wait()


def line_place():
    position = lax.axis_index("slc")
    edge = (position == 0) | (position == lax.axis_size("slc") - 1)
    return edge, lax.axis_index("vol") % 2 == 0


def gradient_kernel(factor, on_line, *refs):
    term_refs, shifted_ref, out_ref = refs[:-2], refs[-2], refs[-1]
    slots, _, lanes = shifted_ref.shape
    terms = [ref[...].astype(jnp.float32) for ref in term_refs]
    residual = terms[0]
    if on_line:
        edge, leads = line_place()
        inside = jnp.where(leads, terms[1] + terms[2], terms[2] + terms[3])
        residual += jnp.where(edge, jnp.where(leads, terms[3], terms[4]), inside)
    for slot in range(slots):
        product = residual * shifted_ref[slot].astype(jnp.float32)
        tiles = [product[:, at : at + LANE_TILE] for at in range(0, lanes, LANE_TILE)]
        folded = functools.reduce(lambda a, b: a + b, tiles)
        out_ref[slot : slot + 1, :] = factor * jnp.sum(folded.T, axis=0, keepdims=True)


def after(value, *earlier):
    return lax.optimization_barrier((value, *earlier))[0]


def sum_over_replicas(value):
    axes = ("coil", "vol")
    if any(lax.axis_size(axis) != 2 for axis in axes):
        return lax.psum(value, axes)
    swapped = [
        lax.ppermute(value, axes, [(index, index ^ mask) for index in range(4)])
        for mask in (1, 2, 3)
    ]
    return (value + swapped[0]) + (swapped[1] + swapped[2])


def line_of_four(encode, gradient, count):
    edge, leads = line_place()
    cores = lax.axis_size("vol")
    outer_pairs = [(0, 1), (1, 0), (2, 3), (3, 2)]
    inner_pairs = [(0, 0), (1, 2), (2, 1), (3, 3)]

    def exchange(value, step):
        pairs = [
            (source * cores + core, target * cores + core)
            for core in range(cores)
            for source, target in ((outer_pairs, inner_pairs)[(step + core) % 2])
        ]
        return lax.ppermute(value, ("slc", "vol"), pairs)

    shifted, own = map(list, zip(encode(0)))
    payload, received, gradients = own[0], [], []
    for step in range(2 * count + 2):
        received.append(exchange(payload, step))
        group = step // 2
        if step % 2 == 0 and group + 1 < count:
            encoded = encode(group + 1, payload) if step else encode(1)
            shifted.append(encoded[0])
            own.append(encoded[1])
        done = group - 2
        if step % 2 == 0 and done >= 0:
            terms = (own[done], *received[2 * done : 2 * done + 4])
            gradients.append(gradient((after(terms[0], payload), *terms[1:]), shifted[done]))
        if step == 2 * count + 1:
            break
        arrived = received[-1]
        if step % 2 == 0:
            before = own[group - 1] if group else own[0]
            if group < count:
                mine = own[group]
                payload = jnp.where(
                    leads, mine + arrived, jnp.where(edge, mine, before + arrived)
                )
            else:
                payload = before + arrived
        else:
            payload = own[group] + arrived
            if group + 1 < count:
                payload = jnp.where(leads & edge, own[group + 1], payload)
    last = count - 1
    gradients.append(gradient((own[last], *received[2 * last : 2 * last + 4]), shifted[last]))
    return gradients


def body(images, coil_maps, kspace, shift_index, phase_offset, group_order):
    vols, per_device, _, _, length = images.shape
    coils = coil_maps.shape[0]
    groups = lax.axis_size("slc")
    rows = round_up(length, ROW_TILE)
    places = vols * coils
    lanes = round_up(places * 2 * length, LANE_TILE)
    whole_classes = per_device % groups == 0
    slots = max(1, per_device // groups)
    tables = dft_matrices(length, rows)
    factor = 1.0 / (coils * lax.axis_size("coil") * vols * lax.axis_size("vol"))
    first = (lax.axis_index("slc") * per_device) % groups
    on_line = whole_classes and groups == 4
    in_vmem = pl.BlockSpec(memory_space=pltpu.VMEM)
    in_smem = pl.BlockSpec(memory_space=pltpu.SMEM)
    in_place = pl.BlockSpec(memory_space=pl.ANY)

    def in_hbm(array):
        return pltpu.with_memory_space_constraint(jnp.asarray(array), pltpu.HBM)

    def rows_of_class(group):
        return [slot * groups + group for slot in range(slots)] if whole_classes else None

    def place_of(group):
        if whole_classes:
            return ()
        held = [(group + step - first, per_device) for step in range(2)]
        inside = [(within >= 0) & (within < size) for within, size in held]
        rows_held = [jnp.where(yes, held[i][0], 0) for i, yes in enumerate(inside)]
        return (jnp.stack([inside[0], rows_held[0], rows_held[1]]).astype(jnp.int32),)

    left, gram, adjoint = (in_hbm(table) for table in tables)
    lying = [in_hbm(jnp.swapaxes(array, -3, -2)) for array in (images, coil_maps, kspace)]
    order = in_hbm(group_order)
    tiles = round_up(length, LANE_TILE) // LANE_TILE
    raw_shapes = [
        jax.ShapeDtypeStruct((count, slots, length, 2, length), jnp.bfloat16)
        for count in (vols, coils)
    ]
    scalar_specs = [] if whole_classes else [in_smem]
    padded_rows = round_up(rows, LANE_TILE)
    slice_semaphores = pltpu.SemaphoreType.DMA((slots, vols + coils))
    *raw, left, phases = pl.pallas_call(
        functools.partial(fetch_kernel, rows_of_class(0)),
        in_specs=scalar_specs + [in_place] * 5,
        out_specs=[in_vmem] * 4,
        out_shape=raw_shapes
        + [
            jax.ShapeDtypeStruct(left.shape, left.dtype),
            jax.ShapeDtypeStruct((2, padded_rows, per_device), jnp.float32),
        ],
        scratch_shapes=[
            pltpu.SMEM((per_device,), jnp.int32),
            pltpu.VMEM((per_device, length), jnp.float32),
            pltpu.VMEM((per_device, padded_rows), jnp.float32),
            slice_semaphores,
            pltpu.SemaphoreType.DMA((3,)),
        ],
        compiler_params=pltpu.CompilerParams(vmem_limit_bytes=VMEM_BYTES),
        name="fetch",
    )(*place_of(0), in_hbm(shift_index), in_hbm(phase_offset), *lying[:2], left)

    def encode(group, *earlier):
        image, coil_map = (jnp.swapaxes(array, -3, -2) for array in raw)
        has_next = group + 1 < groups
        place, group_phases = place_of(group), phases
        if not whole_classes:
            group_phases = lax.dynamic_slice_in_dim(phases, place[0][1], 1, axis=2)
        if earlier:
            image = after(image, *earlier)
        outputs = pl.pallas_call(
            functools.partial(
                encode_kernel,
                slots,
                group,
                rows_of_class(group),
                (rows_of_class(group + 1) or [0]) if has_next else None,
            ),
            in_specs=scalar_specs + [in_vmem] * 4 + [in_place] * 6,
            out_specs=[in_vmem] * (2 + 2 * has_next),
            out_shape=[jax.ShapeDtypeStruct((slots, rows, lanes), jnp.bfloat16)]
            + [jax.ShapeDtypeStruct((rows, lanes), jnp.bfloat16)]
            + raw_shapes * has_next,
            scratch_shapes=[
                pltpu.VMEM((rows, lanes), jnp.float32),
                pltpu.VMEM((tiles, 2 * length, LANE_TILE), jnp.float32),
                pltpu.VMEM(lying[2].shape, jnp.bfloat16),
                pltpu.VMEM(gram.shape, jnp.bfloat16),
                pltpu.VMEM(adjoint.shape, jnp.bfloat16),
                pltpu.SMEM((groups,), jnp.int32),
                slice_semaphores,
                pltpu.SemaphoreType.DMA((4,)),
            ],
            compiler_params=pltpu.CompilerParams(vmem_limit_bytes=VMEM_BYTES),
            cost_estimate=pl.CostEstimate(
                flops=places * (slots + 1) * 16 * length**3,
                bytes_accessed=6_000_000,
                transcendentals=0,
            ),
            name="encode",
        )(
            *place,
            group_phases,
            image,
            coil_map,
            left,
            order,
            gram,
            adjoint,
            lying[2],
            *lying[:2],
        )
        raw[:] = outputs[2:]
        return outputs[:2]

    def gradient(terms, encoded):
        return pl.pallas_call(
            functools.partial(gradient_kernel, factor, on_line),
            out_shape=jax.ShapeDtypeStruct((slots, rows), jnp.float32),
            compiler_params=pltpu.CompilerParams(vmem_limit_bytes=VMEM_BYTES),
            cost_estimate=pl.CostEstimate(
                flops=places * slots * 4 * length**2, bytes_accessed=1_500_000, transcendentals=0
            ),
            name="gradient",
        )(*terms, encoded)

    if on_line:
        gradients = line_of_four(encode, gradient, groups)
    else:
        encoded = [encode(group) for group in range(groups)]
        reduced = lax.psum([own for _, own in encoded], "slc")
        gradients = [gradient((reduced[group],), encoded[group][0]) for group in range(groups)]
    by_class = jnp.stack(gradients, axis=1)[:, :, :length]
    if whole_classes:
        local = by_class.reshape(per_device, length)
    else:
        local = lax.dynamic_slice_in_dim(by_class[0], first, per_device, axis=0)
    return sum_over_replicas(local)


def solution(mesh):
    placed = (
        P(("grp", "vol"), "slc", None, None, None),
        P(("grp", "coil"), "slc", None, None, None),
        P(("grp", "vol"), "slc", "coil", None, None, None),
        P("slc"),
        P("slc", None),
        P(),
    )
    return jax.shard_map(
        body, mesh=mesh, in_specs=placed, out_specs=P(("grp", "slc"), None), check_vma=False
    )
```

```python
import functools
import math

import jax
import jax.numpy as jnp
import ml_dtypes
import numpy as np
from jax import lax
from jax.experimental import pallas as pl
from jax.experimental.pallas import tpu as pltpu
from jax.sharding import PartitionSpec as P

MB = 8
ROW_TILE = 16
LANE_TILE = 128
VMEM_BYTES = 24 * 1024 * 1024


def round_up(value, multiple):
    return -(-value // multiple) * multiple


def fourier_tables(length):
    positions = np.arange(length, dtype=np.int32)
    product = positions[:, None] * positions[None, :] % length
    radians = np.float32(2.0 * math.pi / length) * product.astype(np.float32)
    factor = np.float32(1.0 / math.sqrt(length))
    return (
        (np.cos(radians) * factor).astype(ml_dtypes.bfloat16),
        (-np.sin(radians) * factor).astype(ml_dtypes.bfloat16),
    )


def dft_matrices(length, rows):
    cos_table, sin_table = fourier_tables(length)
    cosine, sine = cos_table.astype(np.float64), sin_table.astype(np.float64)
    left_re = np.zeros((2 * rows + 8, length), np.float64)
    left_im = np.zeros((2 * rows + 8, length), np.float64)
    left_re[:length], left_re[rows : rows + length] = cosine, sine
    left_im[:length], left_im[rows : rows + length] = -sine, cosine
    gram_re = cosine.T @ cosine + sine.T @ sine
    gram_im = sine.T @ cosine - cosine.T @ sine
    gram = np.stack(
        [np.concatenate([gram_im, -gram_re], 1), np.concatenate([gram_re, gram_im], 1)]
    )
    adjoint = np.stack(
        [np.concatenate([-sine, -cosine], 1), np.concatenate([cosine, -sine], 1)]
    )
    left = np.stack([left_re, left_im])
    return tuple(part.astype(ml_dtypes.bfloat16) for part in (left, gram, adjoint))


def dot(left, right):
    return jnp.dot(left, right, preferred_element_type=jnp.float32)


def start_all(copies):
    for copy in copies:
        copy.start()


def slice_copies(image_ref, map_ref, image_out, map_out, arrived, rows_of):
    vols, coils = image_ref.shape[0], map_ref.shape[0]
    return [
        pltpu.make_async_copy(
            image_ref.at[vol, row], image_out.at[vol, slot], arrived.at[slot, vol]
        )
        for slot, row in enumerate(rows_of)
        for vol in range(vols)
    ] + [
        pltpu.make_async_copy(
            map_ref.at[coil, row], map_out.at[coil, slot], arrived.at[slot, vols + coil]
        )
        for slot, row in enumerate(rows_of)
        for coil in range(coils)
    ]


def fetch_kernel(rows_of, *refs):
    if rows_of is None:
        rows_of, refs = [refs[0][1]], refs[1:]
    shift_ref, offset_ref, image_ref, map_ref, left_ref = refs[:5]
    image_out, map_out, left_out, phase_out = refs[5:9]
    shift, offset, angle, arrived, small = refs[9:]
    copies = slice_copies(image_ref, map_ref, image_out, map_out, arrived, rows_of)
    copies.append(pltpu.make_async_copy(left_ref, left_out, small.at[0]))
    early = [
        pltpu.make_async_copy(shift_ref, shift, small.at[1]),
        pltpu.make_async_copy(offset_ref, offset, small.at[2]),
    ]
    start_all(early)
    start_all(copies)
    for copy in early:
        copy.wait()
    per_device, length = offset.shape
    lines = lax.broadcasted_iota(jnp.int32, (1, length), 1) - length // 2
    angle[...] = jnp.zeros_like(angle)
    for row in range(per_device):
        turns = (shift[row] * lines) & (MB - 1)
        angle[row : row + 1, :length] = (
            2.0 * math.pi / MB * turns.astype(jnp.float32) + offset[row : row + 1, :]
        )
    phase_out[:, :per_device] = jnp.cos(angle[...]).T
    phase_out[:, per_device:] = jnp.sin(angle[...]).T
    for copy in copies:
        copy.wait()


def encode_kernel(slots, group, rows_of, next_rows, *refs):
    whole_classes = rows_of is not None
    if not whole_classes:
        place_ref, refs = refs[0], refs[1:]
        next_rows = next_rows and [place_ref[2]]
    phase_ref, image, coil_map, left_ref = refs[:4]
    order_ref, gram_ref, adjoint_ref, kspace_ref, image_ref, map_ref = refs[4:10]
    refs = refs[10:]
    if group > 0:
        earlier_ref, refs = refs[0], refs[1:]
    shifted, out_ref, refs = refs[0], refs[1], refs[2:]
    if group > 0:
        kept_ref, refs = refs[0], refs[1:]
    if next_rows:
        next_image, next_map, refs = refs[0], refs[1], refs[2:]
    total, wide, raw_kspace, gram, adjoint, order, arrived, small = refs
    vols, coils, length = image.shape[0], coil_map.shape[0], image.shape[-1]
    _, rows, lanes = shifted.shape
    order_copy = pltpu.make_async_copy(order_ref, order, small.at[0])
    gram_copy = pltpu.make_async_copy(gram_ref, gram, small.at[1])
    owner_copies = [
        pltpu.make_async_copy(kspace_ref, raw_kspace, small.at[2]),
        pltpu.make_async_copy(adjoint_ref, adjoint, small.at[3]),
    ]
    next_copies = []
    if next_rows:
        next_copies = slice_copies(image_ref, map_ref, next_image, next_map, arrived, next_rows)
    if group > 0:
        next_copies.append(pltpu.make_async_copy(earlier_ref, kept_ref, small.at[4]))
    start_all([order_copy, gram_copy, *next_copies])

    if lanes > vols * coils * 2 * length:
        last = slice(lanes - LANE_TILE, lanes)
        total[:, last] = jnp.zeros((rows, LANE_TILE), jnp.float32)
        for slot in range(slots):
            shifted[slot, :, last] = jnp.zeros((rows, LANE_TILE), jnp.bfloat16)
    sums = [None] * (vols * coils)
    for slot in range(slots):
        if whole_classes:
            column = rows_of[slot]
            half = phase_ref.shape[1] // 2
            cosine = phase_ref[:rows, column : column + 1]
            sine = phase_ref[:rows, half + column : half + column + 1]
        else:
            cosine, sine = phase_ref[:rows, :1], phase_ref[:rows, 1:]
        for vol in range(vols):
            image_re = image[vol, slot, 0].astype(jnp.float32)
            image_im = image[vol, slot, 1].astype(jnp.float32)
            for coil in range(coils):
                place = vol * coils + coil
                base = place * 2 * length
                map_re = coil_map[coil, slot, 0].astype(jnp.float32)
                map_im = coil_map[coil, slot, 1].astype(jnp.float32)
                coil_re = (map_re * image_re - map_im * image_im).astype(jnp.bfloat16)
                coil_im = (map_re * image_im + map_im * image_re).astype(jnp.bfloat16)
                partly = dot(left_ref[0, : 2 * rows], coil_re) + dot(
                    left_ref[1, : 2 * rows], coil_im
                )
                part_re, part_im = partly[:rows], partly[rows:]
                shift_re = part_re * cosine - part_im * sine
                shift_im = part_re * sine + part_im * cosine
                shifted[slot, :, base : base + length] = shift_re.astype(jnp.bfloat16)
                shifted[slot, :, base + length : base + 2 * length] = shift_im.astype(
                    jnp.bfloat16
                )
                if slot > 0:
                    shift_re, shift_im = sums[place][0] + shift_re, sums[place][1] + shift_im
                sums[place] = (shift_re, shift_im)
        if slot == 0:
            order_copy.wait()
            owner = order[group] == lax.axis_index("slc")

            @pl.when(owner)
            def _():
                start_all(owner_copies)

    gram_copy.wait()
    for place, (sum_re, sum_im) in enumerate(sums):
        mixed = dot(sum_re.astype(jnp.bfloat16), gram[0]) + dot(
            sum_im.astype(jnp.bfloat16), gram[1]
        )
        if not whole_classes:
            mixed = jnp.where(place_ref[0] > 0, mixed, 0.0)
        total[:, place * 2 * length : (place + 1) * 2 * length] = mixed

    @pl.when(owner)
    def _():
        for copy in owner_copies:
            copy.wait()
        for vol in range(vols):
            for coil in range(coils):
                place = vol * coils + coil
                lying = raw_kspace.at[vol, 0, coil].reshape(2 * length, length)[...]
                measured = None
                for kind in range(2):
                    for tile in range(wide.shape[0]):
                        at, end = tile * LANE_TILE, min(length, (tile + 1) * LANE_TILE)
                        if kind == 0:
                            wide[tile, :, : end - at] = lying[:, at:end].astype(jnp.float32)
                        rows_read = wide[tile, pl.ds(kind, length, stride=2), :]
                        term = dot(
                            rows_read[:, : end - at].astype(jnp.bfloat16), adjoint[kind, at:end, :]
                        )
                        measured = term if measured is None else measured + term
                total[:length, place * 2 * length : (place + 1) * 2 * length] -= measured

    out_ref[...] = total[...].astype(jnp.bfloat16)
    for copy in next_copies:
        copy.wait()


def at_line_end():
    position = lax.axis_index("slc")
    return (position == 0) | (position == lax.axis_size("slc") - 1)


def gradient_kernel(factor, on_line, *refs):
    term_refs, shifted_ref, out_ref = refs[:-2], refs[-2], refs[-1]
    slots, _, lanes = shifted_ref.shape
    terms = [ref[...].astype(jnp.float32) for ref in term_refs]
    residual = terms[0]
    if on_line:
        near, across, rest = terms[1:]
        residual += jnp.where(at_line_end(), rest, near + across)
    for slot in range(slots):
        product = residual * shifted_ref[slot].astype(jnp.float32)
        tiles = [product[:, at : at + LANE_TILE] for at in range(0, lanes, LANE_TILE)]
        folded = functools.reduce(lambda a, b: a + b, tiles)
        out_ref[slot : slot + 1, :] = factor * jnp.sum(folded.T, axis=0, keepdims=True)


def after(value, *earlier):
    return lax.optimization_barrier((value, *earlier))[0]


def sum_over_replicas(value):
    axes = ("coil", "vol")
    if any(lax.axis_size(axis) != 2 for axis in axes):
        return lax.psum(value, axes)
    swapped = [
        lax.ppermute(value, axes, [(index, index ^ mask) for index in range(4)])
        for mask in (1, 2, 3)
    ]
    return (value + swapped[0]) + (swapped[1] + swapped[2])


def line_of_four(encode, gradient, count):
    edge = at_line_end()

    def outer(value):
        return lax.ppermute(value, "slc", [(0, 1), (1, 0), (2, 3), (3, 2)])

    def inner(value):
        return lax.ppermute(value, "slc", [(0, 0), (1, 2), (2, 1), (3, 3)])

    own = [encode(0)]
    near, across, gradients = [outer(own[0])], [], []
    while len(own) < min(3, count):
        own.append(encode(len(own)))
    latest = own[-1]
    for step in range(1, count + 2):
        arrived = after(near[-1], latest)
        half = own[step - 1] + arrived if step <= count else None
        payload = own[step] if step < count else None
        if step >= 2:
            others = own[step - 2] + after(across[step - 2], near[-1] if half is None else half)
            payload = others if payload is None else jnp.where(edge, payload, others)
        else:
            payload = after(payload, half)
        if half is not None:
            across.append(inner(half))
        near.append(outer(payload))
        latest = payload
        if len(own) < count:
            own.append(encode(len(own), payload))
            latest = own[-1]
        if step >= 3:
            done = step - 3
            terms = (own[done], near[done], across[done], near[done + 2])
            gradients.append(gradient((after(terms[0], payload), *terms[1:]), done))
    last = count - 1
    gradients.append(gradient((own[last], near[last], across[last], near[last + 2]), last))
    return gradients


def body(images, coil_maps, kspace, shift_index, phase_offset, group_order):
    vols, per_device, _, _, length = images.shape
    coils = coil_maps.shape[0]
    groups = lax.axis_size("slc")
    rows = round_up(length, ROW_TILE)
    places = vols * coils
    lanes = round_up(places * 2 * length, LANE_TILE)
    whole_classes = per_device % groups == 0
    slots = max(1, per_device // groups)
    tables = dft_matrices(length, rows)
    factor = 1.0 / (coils * lax.axis_size("coil") * vols * lax.axis_size("vol"))
    first = (lax.axis_index("slc") * per_device) % groups
    on_line = whole_classes and groups == 4
    in_vmem = pl.BlockSpec(memory_space=pltpu.VMEM)
    in_smem = pl.BlockSpec(memory_space=pltpu.SMEM)
    in_place = pl.BlockSpec(memory_space=pl.ANY)

    def in_hbm(array):
        return pltpu.with_memory_space_constraint(jnp.asarray(array), pltpu.HBM)

    def rows_of_class(group):
        return [slot * groups + group for slot in range(slots)] if whole_classes else None

    def place_of(group):
        if whole_classes:
            return ()
        held = [(group + step - first, per_device) for step in range(2)]
        inside = [(within >= 0) & (within < size) for within, size in held]
        rows_held = [jnp.where(yes, held[i][0], 0) for i, yes in enumerate(inside)]
        return (jnp.stack([inside[0], rows_held[0], rows_held[1]]).astype(jnp.int32),)

    left, gram, adjoint = (in_hbm(table) for table in tables)
    lying = [in_hbm(jnp.swapaxes(array, -3, -2)) for array in (images, coil_maps, kspace)]
    order = in_hbm(group_order)
    tiles = round_up(length, LANE_TILE) // LANE_TILE
    raw_shapes = [
        jax.ShapeDtypeStruct((count, slots, length, 2, length), jnp.bfloat16)
        for count in (vols, coils)
    ]
    scalar_specs = [] if whole_classes else [in_smem]
    padded_rows = round_up(rows, LANE_TILE)
    slice_semaphores = pltpu.SemaphoreType.DMA((slots, vols + coils))
    *raw, left, phases = pl.pallas_call(
        functools.partial(fetch_kernel, rows_of_class(0)),
        in_specs=scalar_specs + [in_place] * 5,
        out_specs=[in_vmem] * 4,
        out_shape=raw_shapes
        + [
            jax.ShapeDtypeStruct(left.shape, left.dtype),
            jax.ShapeDtypeStruct((padded_rows, 2 * per_device), jnp.float32),
        ],
        scratch_shapes=[
            pltpu.SMEM((per_device,), jnp.int32),
            pltpu.VMEM((per_device, length), jnp.float32),
            pltpu.VMEM((per_device, padded_rows), jnp.float32),
            slice_semaphores,
            pltpu.SemaphoreType.DMA((3,)),
        ],
        compiler_params=pltpu.CompilerParams(vmem_limit_bytes=VMEM_BYTES),
        name="fetch",
    )(*place_of(0), in_hbm(shift_index), in_hbm(phase_offset), *lying[:2], left)

    latest, kept = [], []

    def encode(group, *earlier):
        image, coil_map = (jnp.swapaxes(array, -3, -2) for array in raw)
        has_next = group + 1 < groups
        place, group_phases = place_of(group), phases
        if not whole_classes:
            group_phases = jnp.take(
                phases, jnp.stack([place[0][1], place[0][1] + per_device]), axis=1
            )
        if earlier:
            image = after(image, *earlier)
        kept_shape = pltpu.HBM((slots, rows, lanes), jnp.bfloat16)
        outputs = pl.pallas_call(
            functools.partial(
                encode_kernel,
                slots,
                group,
                rows_of_class(group),
                (rows_of_class(group + 1) or [0]) if has_next else None,
            ),
            in_specs=scalar_specs + [in_vmem] * 4 + [in_place] * 6 + [in_vmem] * len(latest),
            out_specs=[in_vmem] * 2 + [in_place] * len(latest) + [in_vmem] * 2 * has_next,
            out_shape=[
                jax.ShapeDtypeStruct((slots, rows, lanes), jnp.bfloat16),
                jax.ShapeDtypeStruct((rows, lanes), jnp.bfloat16),
            ]
            + [kept_shape] * len(latest)
            + raw_shapes * has_next,
            scratch_shapes=[
                pltpu.VMEM((rows, lanes), jnp.float32),
                pltpu.VMEM((tiles, 2 * length, LANE_TILE), jnp.float32),
                pltpu.VMEM(lying[2].shape, jnp.bfloat16),
                pltpu.VMEM(gram.shape, jnp.bfloat16),
                pltpu.VMEM(adjoint.shape, jnp.bfloat16),
                pltpu.SMEM((groups,), jnp.int32),
                slice_semaphores,
                pltpu.SemaphoreType.DMA((5,)),
            ],
            compiler_params=pltpu.CompilerParams(vmem_limit_bytes=VMEM_BYTES),
            cost_estimate=pl.CostEstimate(
                flops=places * (slots + 1) * 16 * length**3,
                bytes_accessed=6_000_000,
                transcendentals=0,
            ),
            name="encode",
        )(
            *place,
            group_phases,
            image,
            coil_map,
            left,
            order,
            gram,
            adjoint,
            lying[2],
            *lying[:2],
            *latest,
        )
        raw[:] = outputs[2 + len(latest) :]
        kept.extend(outputs[2 : 2 + len(latest)])
        latest[:] = outputs[:1]
        return outputs[1]

    def shifted_of(group):
        return (kept + latest)[group]

    def gradient(terms, group):
        return pl.pallas_call(
            functools.partial(gradient_kernel, factor, on_line),
            out_shape=jax.ShapeDtypeStruct((slots, rows), jnp.float32),
            compiler_params=pltpu.CompilerParams(vmem_limit_bytes=VMEM_BYTES),
            cost_estimate=pl.CostEstimate(
                flops=places * slots * 4 * length**2, bytes_accessed=1_500_000, transcendentals=0
            ),
            name="gradient",
        )(*terms, shifted_of(group))

    if on_line:
        gradients = line_of_four(encode, gradient, groups)
    else:
        reduced = lax.psum([encode(group) for group in range(groups)], "slc")
        gradients = [gradient((reduced[group],), group) for group in range(groups)]
    by_class = jnp.stack(gradients, axis=1)[:, :, :length]
    if whole_classes:
        local = by_class.reshape(per_device, length)
    else:
        local = lax.dynamic_slice_in_dim(by_class[0], first, per_device, axis=0)
    return sum_over_replicas(local)


def solution(mesh):
    placed = (
        P(("grp", "vol"), "slc", None, None, None),
        P(("grp", "coil"), "slc", None, None, None),
        P(("grp", "vol"), "slc", "coil", None, None, None),
        P("slc"),
        P("slc", None),
        P(),
    )
    return jax.shard_map(
        body, mesh=mesh, in_specs=placed, out_specs=P(("grp", "slc"), None), check_vma=False
    )
```

```python
import functools
import math

import jax
import jax.numpy as jnp
import ml_dtypes
import numpy as np
from jax import lax
from jax.experimental import pallas as pl
from jax.experimental.pallas import tpu as pltpu
from jax.sharding import PartitionSpec as P

MB = 8
ROW_TILE = 16
LANE_TILE = 128
PARTS = 1
VMEM_BYTES = 24 * 1024 * 1024


def round_up(value, multiple):
    return -(-value // multiple) * multiple


def fourier_tables(length):
    positions = np.arange(length, dtype=np.int32)
    product = positions[:, None] * positions[None, :] % length
    radians = np.float32(2.0 * math.pi / length) * product.astype(np.float32)
    factor = np.float32(1.0 / math.sqrt(length))
    return (
        (np.cos(radians) * factor).astype(ml_dtypes.bfloat16),
        (-np.sin(radians) * factor).astype(ml_dtypes.bfloat16),
    )


def dft_matrices(length, rows):
    cos_table, sin_table = fourier_tables(length)
    cosine, sine = cos_table.astype(np.float64), sin_table.astype(np.float64)
    left_re = np.zeros((2 * rows + 8, length), np.float64)
    left_im = np.zeros((2 * rows + 8, length), np.float64)
    left_re[:length], left_re[rows : rows + length] = cosine, sine
    left_im[:length], left_im[rows : rows + length] = -sine, cosine
    gram_re = cosine.T @ cosine + sine.T @ sine
    gram_im = sine.T @ cosine - cosine.T @ sine
    gram = np.stack(
        [np.concatenate([gram_im, -gram_re], 1), np.concatenate([gram_re, gram_im], 1)]
    )
    adjoint = np.stack(
        [np.concatenate([-sine, -cosine], 1), np.concatenate([cosine, -sine], 1)]
    )
    left = np.stack([left_re, left_im])
    return tuple(part.astype(ml_dtypes.bfloat16) for part in (left, gram, adjoint))


def dot(left, right):
    return jnp.dot(left, right, preferred_element_type=jnp.float32)


def at_line_end():
    position = lax.axis_index("slc")
    return (position == 0) | (position == lax.axis_size("slc") - 1)


def start_all(copies):
    for copy in copies:
        copy.start()


def slice_copies(image_ref, map_ref, image_out, map_out, arrived, rows_of):
    vols, coils = image_ref.shape[0], map_ref.shape[0]
    return [
        pltpu.make_async_copy(
            image_ref.at[vol, row], image_out.at[vol, slot], arrived.at[slot, vol]
        )
        for slot, row in enumerate(rows_of)
        for vol in range(vols)
    ] + [
        pltpu.make_async_copy(
            map_ref.at[coil, row], map_out.at[coil, slot], arrived.at[slot, vols + coil]
        )
        for slot, row in enumerate(rows_of)
        for coil in range(coils)
    ]


def fetch_kernel(rows_of, *refs):
    if rows_of is None:
        rows_of, refs = [refs[0][1]], refs[1:]
    shift_ref, offset_ref, image_ref, map_ref, left_ref = refs[:5]
    image_out, map_out, left_out, phase_out, ends_out = refs[5:10]
    shift, offset, angle, arrived, small = refs[10:]
    copies = slice_copies(image_ref, map_ref, image_out, map_out, arrived, rows_of)
    copies.append(pltpu.make_async_copy(left_ref, left_out, small.at[0]))
    early = [
        pltpu.make_async_copy(shift_ref, shift, small.at[1]),
        pltpu.make_async_copy(offset_ref, offset, small.at[2]),
    ]
    start_all(early)
    start_all(copies)
    ends_out[...] = jnp.where(at_line_end(), 1.0, 0.0) * jnp.ones_like(ends_out)
    for copy in early:
        copy.wait()
    per_device, length = offset.shape
    lines = lax.broadcasted_iota(jnp.int32, (1, length), 1) - length // 2
    angle[...] = jnp.zeros_like(angle)
    for row in range(per_device):
        turns = (shift[row] * lines) & (MB - 1)
        angle[row : row + 1, :length] = (
            2.0 * math.pi / MB * turns.astype(jnp.float32) + offset[row : row + 1, :]
        )
    phase_out[:, :per_device] = jnp.cos(angle[...]).T
    phase_out[:, per_device:] = jnp.sin(angle[...]).T
    for copy in copies:
        copy.wait()


def encode_kernel(slots, group, rows_of, next_rows, *refs):
    whole_classes = rows_of is not None
    if not whole_classes:
        place_ref, refs = refs[0], refs[1:]
        next_rows = next_rows and [place_ref[2]]
    phase_ref, image, coil_map, left_ref = refs[:4]
    order_ref, gram_ref, adjoint_ref, kspace_ref, image_ref, map_ref = refs[4:10]
    refs = refs[10:]
    shifted, refs = refs[0], refs[1:]
    out_refs, refs = refs[:PARTS], refs[PARTS:]
    if next_rows:
        next_image, next_map, refs = refs[0], refs[1], refs[2:]
    total, wide, raw_kspace, gram, adjoint, order, arrived, small = refs
    vols, coils, length = image.shape[0], coil_map.shape[0], image.shape[-1]
    _, rows, lanes = shifted.shape
    order_copy = pltpu.make_async_copy(order_ref, order, small.at[0])
    gram_copy = pltpu.make_async_copy(gram_ref, gram, small.at[1])
    owner_copies = [
        pltpu.make_async_copy(kspace_ref, raw_kspace, small.at[2]),
        pltpu.make_async_copy(adjoint_ref, adjoint, small.at[3]),
    ]
    next_copies = []
    if next_rows:
        next_copies = slice_copies(image_ref, map_ref, next_image, next_map, arrived, next_rows)
    start_all([order_copy, gram_copy, *next_copies])

    if lanes > vols * coils * 2 * length:
        last = slice(lanes - LANE_TILE, lanes)
        total[:, last] = jnp.zeros((rows, LANE_TILE), jnp.float32)
        for slot in range(slots):
            shifted[slot, :, last] = jnp.zeros((rows, LANE_TILE), jnp.bfloat16)
    sums = [None] * (vols * coils)
    for slot in range(slots):
        if whole_classes:
            column = rows_of[slot]
            half = phase_ref.shape[1] // 2
            cosine = phase_ref[:rows, column : column + 1]
            sine = phase_ref[:rows, half + column : half + column + 1]
        else:
            cosine, sine = phase_ref[:rows, :1], phase_ref[:rows, 1:]
        for vol in range(vols):
            image_re = image[vol, slot, 0].astype(jnp.float32)
            image_im = image[vol, slot, 1].astype(jnp.float32)
            for coil in range(coils):
                place = vol * coils + coil
                base = place * 2 * length
                map_re = coil_map[coil, slot, 0].astype(jnp.float32)
                map_im = coil_map[coil, slot, 1].astype(jnp.float32)
                coil_re = (map_re * image_re - map_im * image_im).astype(jnp.bfloat16)
                coil_im = (map_re * image_im + map_im * image_re).astype(jnp.bfloat16)
                partly = dot(left_ref[0, : 2 * rows], coil_re) + dot(
                    left_ref[1, : 2 * rows], coil_im
                )
                part_re, part_im = partly[:rows], partly[rows:]
                shift_re = part_re * cosine - part_im * sine
                shift_im = part_re * sine + part_im * cosine
                shifted[slot, :, base : base + length] = shift_re.astype(jnp.bfloat16)
                shifted[slot, :, base + length : base + 2 * length] = shift_im.astype(
                    jnp.bfloat16
                )
                if slot > 0:
                    shift_re, shift_im = sums[place][0] + shift_re, sums[place][1] + shift_im
                sums[place] = (shift_re, shift_im)
        if slot == 0:
            order_copy.wait()
            owner = order[group] == lax.axis_index("slc")

            @pl.when(owner)
            def _():
                start_all(owner_copies)

    gram_copy.wait()
    for place, (sum_re, sum_im) in enumerate(sums):
        mixed = dot(sum_re.astype(jnp.bfloat16), gram[0]) + dot(
            sum_im.astype(jnp.bfloat16), gram[1]
        )
        if not whole_classes:
            mixed = jnp.where(place_ref[0] > 0, mixed, 0.0)
        total[:, place * 2 * length : (place + 1) * 2 * length] = mixed

    @pl.when(owner)
    def _():
        for copy in owner_copies:
            copy.wait()
        for vol in range(vols):
            for coil in range(coils):
                place = vol * coils + coil
                lying = raw_kspace.at[vol, 0, coil].reshape(2 * length, length)[...]
                measured = None
                for kind in range(2):
                    for tile in range(wide.shape[0]):
                        at, end = tile * LANE_TILE, min(length, (tile + 1) * LANE_TILE)
                        if kind == 0:
                            wide[tile, :, : end - at] = lying[:, at:end].astype(jnp.float32)
                        rows_read = wide[tile, pl.ds(kind, length, stride=2), :]
                        term = dot(
                            rows_read[:, : end - at].astype(jnp.bfloat16), adjoint[kind, at:end, :]
                        )
                        measured = term if measured is None else measured + term
                total[:length, place * 2 * length : (place + 1) * 2 * length] -= measured

    part = rows // PARTS
    for index, out_ref in enumerate(out_refs):
        out_ref[...] = total[index * part : (index + 1) * part, :].astype(jnp.bfloat16)
    for copy in next_copies:
        copy.wait()


def gradient_kernel(index, factor, on_line, *refs):
    term_refs, shifted_ref, out_ref = refs[:-2], refs[-2], refs[-1]
    slots, rows, lanes = shifted_ref.shape
    part = rows // PARTS
    terms = [ref[...].astype(jnp.float32) for ref in term_refs]
    residual = terms[0]
    if on_line:
        near, across, rest = terms[1:]
        residual += jnp.where(at_line_end(), rest, near + across)
    for slot in range(slots):
        product = residual * shifted_ref[slot, index * part : (index + 1) * part, :].astype(
            jnp.float32
        )
        tiles = [product[:, at : at + LANE_TILE] for at in range(0, lanes, LANE_TILE)]
        folded = functools.reduce(lambda a, b: a + b, tiles)
        out_ref[slot : slot + 1, :] = factor * jnp.sum(folded.T, axis=0, keepdims=True)


def after(value, *earlier):
    return lax.optimization_barrier((value, *earlier))[0]


def sum_over_replicas(value):
    axes = ("coil", "vol")
    if any(lax.axis_size(axis) != 2 for axis in axes):
        return lax.psum(value, axes)
    swapped = [
        lax.ppermute(value, axes, [(index, index ^ mask) for index in range(4)])
        for mask in (1, 2, 3)
    ]
    return (value + swapped[0]) + (swapped[1] + swapped[2])


def line_of_four(encode, gradient, groups, ends):
    cores = lax.axis_size("vol")
    count = groups * PARTS
    outer_pairs = [(0, 1), (1, 0), (2, 3), (3, 2)]
    inner_pairs = [
        (source * cores + core, target * cores + (core ^ 1 if swap and cores % 2 == 0 else core))
        for source, target, swap in ((0, 0, True), (1, 2, False), (2, 1, False), (3, 3, True))
        for core in range(cores)
    ]

    def outer(value):
        return lax.ppermute(value, "slc", outer_pairs)

    def inner(value):
        return lax.ppermute(value, ("slc", "vol"), inner_pairs)

    own = [*encode(0)]
    near, across, gradients, encoded = [outer(own[0])], [], [], 1

    def encode_more(wanted, *earlier):
        nonlocal encoded
        while len(own) < min(wanted, count):
            own.extend(encode(encoded, *earlier))
            encoded += 1

    encode_more(3)
    latest = own[-1]
    for step in range(1, count + 2):
        arrived = after(near[-1], latest)
        half = own[step - 1] + arrived if step <= count else None
        payload = own[step] if step < count else None
        if step >= 2:
            others = own[step - 2] + after(across[step - 2], near[-1] if half is None else half)
            payload = others if payload is None else jnp.where(ends > 0, payload, others)
        else:
            payload = after(payload, half)
        if half is not None:
            across.append(inner(half))
        near.append(outer(payload))
        latest = payload
        encode_more(step + 3, payload)
        latest = own[-1] if step + 1 < count else payload
        if step >= 3:
            done = step - 3
            terms = (own[done], near[done], across[done], near[done + 2])
            gradients.append(gradient((after(terms[0], payload), *terms[1:]), done))
    last = count - 1
    gradients.append(gradient((own[last], near[last], across[last], near[last + 2]), last))
    return gradients


def body(images, coil_maps, kspace, shift_index, phase_offset, group_order):
    vols, per_device, _, _, length = images.shape
    coils = coil_maps.shape[0]
    groups = lax.axis_size("slc")
    rows = round_up(length, ROW_TILE * PARTS)
    places = vols * coils
    lanes = round_up(places * 2 * length, LANE_TILE)
    whole_classes = per_device % groups == 0
    slots = max(1, per_device // groups)
    tables = dft_matrices(length, rows)
    factor = 1.0 / (coils * lax.axis_size("coil") * vols * lax.axis_size("vol"))
    first = (lax.axis_index("slc") * per_device) % groups
    on_line = whole_classes and groups == 4
    in_vmem = pl.BlockSpec(memory_space=pltpu.VMEM)
    in_smem = pl.BlockSpec(memory_space=pltpu.SMEM)
    in_place = pl.BlockSpec(memory_space=pl.ANY)

    def in_hbm(array):
        return pltpu.with_memory_space_constraint(jnp.asarray(array), pltpu.HBM)

    def rows_of_class(group):
        return [slot * groups + group for slot in range(slots)] if whole_classes else None

    def place_of(group):
        if whole_classes:
            return ()
        held = [(group + step - first, per_device) for step in range(2)]
        inside = [(within >= 0) & (within < size) for within, size in held]
        rows_held = [jnp.where(yes, held[i][0], 0) for i, yes in enumerate(inside)]
        return (jnp.stack([inside[0], rows_held[0], rows_held[1]]).astype(jnp.int32),)

    left, gram, adjoint = (in_hbm(table) for table in tables)
    lying = [in_hbm(jnp.swapaxes(array, -3, -2)) for array in (images, coil_maps, kspace)]
    order = in_hbm(group_order)
    tiles = round_up(length, LANE_TILE) // LANE_TILE
    raw_shapes = [
        jax.ShapeDtypeStruct((count, slots, length, 2, length), jnp.bfloat16)
        for count in (vols, coils)
    ]
    scalar_specs = [] if whole_classes else [in_smem]
    padded_rows = round_up(rows, LANE_TILE)
    slice_semaphores = pltpu.SemaphoreType.DMA((slots, vols + coils))
    *raw, left, phases, ends = pl.pallas_call(
        functools.partial(fetch_kernel, rows_of_class(0)),
        in_specs=scalar_specs + [in_place] * 5,
        out_specs=[in_vmem] * 5,
        out_shape=raw_shapes
        + [
            jax.ShapeDtypeStruct(left.shape, left.dtype),
            jax.ShapeDtypeStruct((padded_rows, 2 * per_device), jnp.float32),
            jax.ShapeDtypeStruct((1, lanes), jnp.float32),
        ],
        scratch_shapes=[
            pltpu.SMEM((per_device,), jnp.int32),
            pltpu.VMEM((per_device, length), jnp.float32),
            pltpu.VMEM((per_device, padded_rows), jnp.float32),
            slice_semaphores,
            pltpu.SemaphoreType.DMA((3,)),
        ],
        compiler_params=pltpu.CompilerParams(vmem_limit_bytes=VMEM_BYTES),
        name="fetch",
    )(*place_of(0), in_hbm(shift_index), in_hbm(phase_offset), *lying[:2], left)

    shifted = []

    def encode(group, *earlier):
        image, coil_map = (jnp.swapaxes(array, -3, -2) for array in raw)
        has_next = group + 1 < groups
        place, group_phases = place_of(group), phases
        if not whole_classes:
            group_phases = jnp.take(
                phases, jnp.stack([place[0][1], place[0][1] + per_device]), axis=1
            )
        if earlier:
            image = after(image, *earlier)
        outputs = pl.pallas_call(
            functools.partial(
                encode_kernel,
                slots,
                group,
                rows_of_class(group),
                (rows_of_class(group + 1) or [0]) if has_next else None,
            ),
            in_specs=scalar_specs + [in_vmem] * 4 + [in_place] * 6,
            out_specs=[in_vmem] * (1 + PARTS + 2 * has_next),
            out_shape=[jax.ShapeDtypeStruct((slots, rows, lanes), jnp.bfloat16)]
            + [jax.ShapeDtypeStruct((rows // PARTS, lanes), jnp.bfloat16)] * PARTS
            + raw_shapes * has_next,
            scratch_shapes=[
                pltpu.VMEM((rows, lanes), jnp.float32),
                pltpu.VMEM((tiles, 2 * length, LANE_TILE), jnp.float32),
                pltpu.VMEM(lying[2].shape, jnp.bfloat16),
                pltpu.VMEM(gram.shape, jnp.bfloat16),
                pltpu.VMEM(adjoint.shape, jnp.bfloat16),
                pltpu.SMEM((groups,), jnp.int32),
                slice_semaphores,
                pltpu.SemaphoreType.DMA((4,)),
            ],
            compiler_params=pltpu.CompilerParams(vmem_limit_bytes=VMEM_BYTES),
            cost_estimate=pl.CostEstimate(
                flops=places * (slots + 1) * 16 * length**3,
                bytes_accessed=6_000_000,
                transcendentals=0,
            ),
            name="encode",
        )(
            *place,
            group_phases,
            image,
            coil_map,
            left,
            order,
            gram,
            adjoint,
            lying[2],
            *lying[:2],
        )
        raw[:] = outputs[1 + PARTS :]
        shifted.append(outputs[0])
        return outputs[1 : 1 + PARTS]

    def gradient(terms, piece):
        group, index = divmod(piece, PARTS)
        return pl.pallas_call(
            functools.partial(gradient_kernel, index, factor, on_line),
            out_shape=jax.ShapeDtypeStruct((slots, rows // PARTS), jnp.float32),
            compiler_params=pltpu.CompilerParams(vmem_limit_bytes=VMEM_BYTES),
            cost_estimate=pl.CostEstimate(
                flops=places * slots * 4 * length**2, bytes_accessed=1_500_000, transcendentals=0
            ),
            name="gradient",
        )(*terms, shifted[group])

    if on_line:
        gradients = line_of_four(encode, gradient, groups, ends)
    else:
        reduced = lax.psum([piece for group in range(groups) for piece in encode(group)], "slc")
        gradients = [gradient((piece,), index) for index, piece in enumerate(reduced)]
    by_class = jnp.stack(
        [
            jnp.concatenate(gradients[group * PARTS : (group + 1) * PARTS], axis=1)
            for group in range(groups)
        ],
        axis=1,
    )[:, :, :length]
    if whole_classes:
        local = by_class.reshape(per_device, length)
    else:
        local = lax.dynamic_slice_in_dim(by_class[0], first, per_device, axis=0)
    return sum_over_replicas(local)


def solution(mesh):
    placed = (
        P(("grp", "vol"), "slc", None, None, None),
        P(("grp", "coil"), "slc", None, None, None),
        P(("grp", "vol"), "slc", "coil", None, None, None),
        P("slc"),
        P("slc", None),
        P(),
    )
    return jax.shard_map(
        body, mesh=mesh, in_specs=placed, out_specs=P(("grp", "slc"), None), check_vma=False
    )
```

```python
import functools
import math

import jax
import jax.numpy as jnp
import ml_dtypes
import numpy as np
from jax import lax
from jax.experimental import pallas as pl
from jax.experimental.pallas import tpu as pltpu
from jax.sharding import PartitionSpec as P

MB = 8
ROW_TILE = 16
LANE_TILE = 128
PARTS = 2
VMEM_BYTES = 24 * 1024 * 1024


def round_up(value, multiple):
    return -(-value // multiple) * multiple


def fourier_tables(length):
    positions = np.arange(length, dtype=np.int32)
    product = positions[:, None] * positions[None, :] % length
    radians = np.float32(2.0 * math.pi / length) * product.astype(np.float32)
    factor = np.float32(1.0 / math.sqrt(length))
    return (
        (np.cos(radians) * factor).astype(ml_dtypes.bfloat16),
        (-np.sin(radians) * factor).astype(ml_dtypes.bfloat16),
    )


def dft_matrices(length, rows):
    cos_table, sin_table = fourier_tables(length)
    cosine, sine = cos_table.astype(np.float64), sin_table.astype(np.float64)
    left_re = np.zeros((2 * rows + 8, length), np.float64)
    left_im = np.zeros((2 * rows + 8, length), np.float64)
    left_re[:length], left_re[rows : rows + length] = cosine, sine
    left_im[:length], left_im[rows : rows + length] = -sine, cosine
    gram_re = cosine.T @ cosine + sine.T @ sine
    gram_im = sine.T @ cosine - cosine.T @ sine
    gram = np.stack(
        [np.concatenate([gram_im, -gram_re], 1), np.concatenate([gram_re, gram_im], 1)]
    )
    adjoint = np.stack(
        [np.concatenate([-sine, -cosine], 1), np.concatenate([cosine, -sine], 1)]
    )
    left = np.stack([left_re, left_im])
    return tuple(part.astype(ml_dtypes.bfloat16) for part in (left, gram, adjoint))


def dot(left, right):
    return jnp.dot(left, right, preferred_element_type=jnp.float32)


def at_line_end():
    position = lax.axis_index("slc")
    return (position == 0) | (position == lax.axis_size("slc") - 1)


def start_all(copies):
    for copy in copies:
        copy.start()


def slice_copies(image_ref, map_ref, image_out, map_out, arrived, rows_of):
    vols, coils = image_ref.shape[0], map_ref.shape[0]
    return [
        pltpu.make_async_copy(
            image_ref.at[vol, row], image_out.at[vol, slot], arrived.at[slot, vol]
        )
        for slot, row in enumerate(rows_of)
        for vol in range(vols)
    ] + [
        pltpu.make_async_copy(
            map_ref.at[coil, row], map_out.at[coil, slot], arrived.at[slot, vols + coil]
        )
        for slot, row in enumerate(rows_of)
        for coil in range(coils)
    ]


def fetch_kernel(rows_of, *refs):
    if rows_of is None:
        rows_of, refs = [refs[0][1]], refs[1:]
    shift_ref, offset_ref, image_ref, map_ref, left_ref = refs[:5]
    image_out, map_out, left_out, phase_out, ends_out = refs[5:10]
    shift, offset, angle, arrived, small = refs[10:]
    copies = slice_copies(image_ref, map_ref, image_out, map_out, arrived, rows_of)
    copies.append(pltpu.make_async_copy(left_ref, left_out, small.at[0]))
    early = [
        pltpu.make_async_copy(shift_ref, shift, small.at[1]),
        pltpu.make_async_copy(offset_ref, offset, small.at[2]),
    ]
    start_all(early)
    start_all(copies)
    ends_out[...] = jnp.where(at_line_end(), 1.0, 0.0) * jnp.ones_like(ends_out)
    for copy in early:
        copy.wait()
    per_device, length = offset.shape
    lines = lax.broadcasted_iota(jnp.int32, (1, length), 1) - length // 2
    angle[...] = jnp.zeros_like(angle)
    for row in range(per_device):
        turns = (shift[row] * lines) & (MB - 1)
        angle[row : row + 1, :length] = (
            2.0 * math.pi / MB * turns.astype(jnp.float32) + offset[row : row + 1, :]
        )
    phase_out[:, :per_device] = jnp.cos(angle[...]).T
    phase_out[:, per_device:] = jnp.sin(angle[...]).T
    for copy in copies:
        copy.wait()


def encode_kernel(slots, group, rows_of, next_rows, *refs):
    whole_classes = rows_of is not None
    if not whole_classes:
        place_ref, refs = refs[0], refs[1:]
        next_rows = next_rows and [place_ref[2]]
    phase_ref, image, coil_map, left_ref = refs[:4]
    order_ref, gram_ref, adjoint_ref, kspace_ref, image_ref, map_ref = refs[4:10]
    refs = refs[10:]
    shifted, refs = refs[0], refs[1:]
    out_refs, refs = refs[:PARTS], refs[PARTS:]
    if next_rows:
        next_image, next_map, refs = refs[0], refs[1], refs[2:]
    total, wide, raw_kspace, gram, adjoint, order, arrived, small = refs
    vols, coils, length = image.shape[0], coil_map.shape[0], image.shape[-1]
    _, rows, lanes = shifted.shape
    order_copy = pltpu.make_async_copy(order_ref, order, small.at[0])
    gram_copy = pltpu.make_async_copy(gram_ref, gram, small.at[1])
    owner_copies = [
        pltpu.make_async_copy(kspace_ref, raw_kspace, small.at[2]),
        pltpu.make_async_copy(adjoint_ref, adjoint, small.at[3]),
    ]
    next_copies = []
    if next_rows:
        next_copies = slice_copies(image_ref, map_ref, next_image, next_map, arrived, next_rows)
    start_all([order_copy, gram_copy, *next_copies])

    if lanes > vols * coils * 2 * length:
        last = slice(lanes - LANE_TILE, lanes)
        total[:, last] = jnp.zeros((rows, LANE_TILE), jnp.float32)
        for slot in range(slots):
            shifted[slot, :, last] = jnp.zeros((rows, LANE_TILE), jnp.bfloat16)
    sums = [None] * (vols * coils)
    for slot in range(slots):
        if whole_classes:
            column = rows_of[slot]
            half = phase_ref.shape[1] // 2
            cosine = phase_ref[:rows, column : column + 1]
            sine = phase_ref[:rows, half + column : half + column + 1]
        else:
            cosine, sine = phase_ref[:rows, :1], phase_ref[:rows, 1:]
        for vol in range(vols):
            image_re = image[vol, slot, 0].astype(jnp.float32)
            image_im = image[vol, slot, 1].astype(jnp.float32)
            for coil in range(coils):
                place = vol * coils + coil
                base = place * 2 * length
                map_re = coil_map[coil, slot, 0].astype(jnp.float32)
                map_im = coil_map[coil, slot, 1].astype(jnp.float32)
                coil_re = (map_re * image_re - map_im * image_im).astype(jnp.bfloat16)
                coil_im = (map_re * image_im + map_im * image_re).astype(jnp.bfloat16)
                partly = dot(left_ref[0, : 2 * rows], coil_re) + dot(
                    left_ref[1, : 2 * rows], coil_im
                )
                part_re, part_im = partly[:rows], partly[rows:]
                shift_re = part_re * cosine - part_im * sine
                shift_im = part_re * sine + part_im * cosine
                shifted[slot, :, base : base + length] = shift_re.astype(jnp.bfloat16)
                shifted[slot, :, base + length : base + 2 * length] = shift_im.astype(
                    jnp.bfloat16
                )
                if slot > 0:
                    shift_re, shift_im = sums[place][0] + shift_re, sums[place][1] + shift_im
                sums[place] = (shift_re, shift_im)
        if slot == 0:
            order_copy.wait()
            owner = order[group] == lax.axis_index("slc")

            @pl.when(owner)
            def _():
                start_all(owner_copies)

    gram_copy.wait()
    for place, (sum_re, sum_im) in enumerate(sums):
        mixed = dot(sum_re.astype(jnp.bfloat16), gram[0]) + dot(
            sum_im.astype(jnp.bfloat16), gram[1]
        )
        if not whole_classes:
            mixed = jnp.where(place_ref[0] > 0, mixed, 0.0)
        total[:, place * 2 * length : (place + 1) * 2 * length] = mixed

    @pl.when(owner)
    def _():
        for copy in owner_copies:
            copy.wait()
        for vol in range(vols):
            for coil in range(coils):
                place = vol * coils + coil
                lying = raw_kspace.at[vol, 0, coil].reshape(2 * length, length)[...]
                measured = None
                for kind in range(2):
                    for tile in range(wide.shape[0]):
                        at, end = tile * LANE_TILE, min(length, (tile + 1) * LANE_TILE)
                        if kind == 0:
                            wide[tile, :, : end - at] = lying[:, at:end].astype(jnp.float32)
                        rows_read = wide[tile, pl.ds(kind, length, stride=2), :]
                        term = dot(
                            rows_read[:, : end - at].astype(jnp.bfloat16), adjoint[kind, at:end, :]
                        )
                        measured = term if measured is None else measured + term
                total[:length, place * 2 * length : (place + 1) * 2 * length] -= measured

    part = rows // PARTS
    for index, out_ref in enumerate(out_refs):
        out_ref[...] = total[index * part : (index + 1) * part, :].astype(jnp.bfloat16)
    for copy in next_copies:
        copy.wait()


def gradient_kernel(index, factor, on_line, *refs):
    term_refs, shifted_ref, out_ref = refs[:-2], refs[-2], refs[-1]
    slots, rows, lanes = shifted_ref.shape
    part = rows // PARTS
    terms = [ref[...].astype(jnp.float32) for ref in term_refs]
    residual = terms[0]
    if on_line:
        near, across, rest = terms[1:]
        residual += jnp.where(at_line_end(), rest, near + across)
    for slot in range(slots):
        product = residual * shifted_ref[slot, index * part : (index + 1) * part, :].astype(
            jnp.float32
        )
        tiles = [product[:, at : at + LANE_TILE] for at in range(0, lanes, LANE_TILE)]
        folded = functools.reduce(lambda a, b: a + b, tiles)
        out_ref[slot : slot + 1, :] = factor * jnp.sum(folded.T, axis=0, keepdims=True)


def after(value, *earlier):
    return lax.optimization_barrier((value, *earlier))[0]


def sum_over_replicas(value):
    axes = ("coil", "vol")
    if any(lax.axis_size(axis) != 2 for axis in axes):
        return lax.psum(value, axes)
    swapped = [
        lax.ppermute(value, axes, [(index, index ^ mask) for index in range(4)])
        for mask in (1, 2, 3)
    ]
    return (value + swapped[0]) + (swapped[1] + swapped[2])


def line_of_four(encode, gradient, groups, ends):
    cores = lax.axis_size("vol")
    count = groups * PARTS
    outer_pairs = [(0, 1), (1, 0), (2, 3), (3, 2)]
    inner_pairs = [
        (source * cores + core, target * cores + (core ^ 1 if swap and cores % 2 == 0 else core))
        for source, target, swap in ((0, 0, True), (1, 2, False), (2, 1, False), (3, 3, True))
        for core in range(cores)
    ]

    def outer(value):
        return lax.ppermute(value, "slc", outer_pairs)

    def inner(value):
        return lax.ppermute(value, ("slc", "vol"), inner_pairs)

    own = [*encode(0)]
    near, across, gradients, encoded = [outer(own[0])], [], [], 1

    def encode_more(wanted, *earlier):
        nonlocal encoded
        while len(own) < min(wanted, count):
            own.extend(encode(encoded, *earlier))
            encoded += 1

    def gradient_of(piece, *earlier):
        terms = (own[piece], near[piece], across[piece], near[piece + 3])
        if earlier:
            terms = (after(terms[0], *earlier), *terms[1:])
        gradients.append(gradient(terms, piece))

    encode_more(3)
    near.append(outer(after(own[1], own[2])))
    latest = own[2]
    for step in range(count):
        half = own[step] + after(near[step], latest)
        across.append(inner(half))
        payload = own[step + 2] if step + 2 < count else None
        if step >= 1:
            others = own[step - 1] + after(across[step - 1], half)
            payload = others if payload is None else jnp.where(ends > 0, payload, others)
        else:
            payload = after(payload, half)
        near.append(outer(payload))
        latest = payload
        if len(own) < min(step + 4, count):
            encode_more(step + 4, payload)
            latest = own[-1]
        if step >= 3:
            gradient_of(step - 3, payload)
    last = own[count - 1] + after(across[count - 1], latest)
    near.append(outer(last))
    for piece in range(count - 3, count):
        gradient_of(piece, last)
    return gradients


def body(images, coil_maps, kspace, shift_index, phase_offset, group_order):
    vols, per_device, _, _, length = images.shape
    coils = coil_maps.shape[0]
    groups = lax.axis_size("slc")
    rows = round_up(length, ROW_TILE * PARTS)
    places = vols * coils
    lanes = round_up(places * 2 * length, LANE_TILE)
    whole_classes = per_device % groups == 0
    slots = max(1, per_device // groups)
    tables = dft_matrices(length, rows)
    factor = 1.0 / (coils * lax.axis_size("coil") * vols * lax.axis_size("vol"))
    first = (lax.axis_index("slc") * per_device) % groups
    on_line = whole_classes and groups == 4
    in_vmem = pl.BlockSpec(memory_space=pltpu.VMEM)
    in_smem = pl.BlockSpec(memory_space=pltpu.SMEM)
    in_place = pl.BlockSpec(memory_space=pl.ANY)

    def in_hbm(array):
        return pltpu.with_memory_space_constraint(jnp.asarray(array), pltpu.HBM)

    def rows_of_class(group):
        return [slot * groups + group for slot in range(slots)] if whole_classes else None

    def place_of(group):
        if whole_classes:
            return ()
        held = [(group + step - first, per_device) for step in range(2)]
        inside = [(within >= 0) & (within < size) for within, size in held]
        rows_held = [jnp.where(yes, held[i][0], 0) for i, yes in enumerate(inside)]
        return (jnp.stack([inside[0], rows_held[0], rows_held[1]]).astype(jnp.int32),)

    left, gram, adjoint = (in_hbm(table) for table in tables)
    lying = [in_hbm(jnp.swapaxes(array, -3, -2)) for array in (images, coil_maps, kspace)]
    order = in_hbm(group_order)
    tiles = round_up(length, LANE_TILE) // LANE_TILE
    raw_shapes = [
        jax.ShapeDtypeStruct((count, slots, length, 2, length), jnp.bfloat16)
        for count in (vols, coils)
    ]
    scalar_specs = [] if whole_classes else [in_smem]
    padded_rows = round_up(rows, LANE_TILE)
    slice_semaphores = pltpu.SemaphoreType.DMA((slots, vols + coils))
    *raw, left, phases, ends = pl.pallas_call(
        functools.partial(fetch_kernel, rows_of_class(0)),
        in_specs=scalar_specs + [in_place] * 5,
        out_specs=[in_vmem] * 5,
        out_shape=raw_shapes
        + [
            jax.ShapeDtypeStruct(left.shape, left.dtype),
            jax.ShapeDtypeStruct((padded_rows, 2 * per_device), jnp.float32),
            jax.ShapeDtypeStruct((1, lanes), jnp.float32),
        ],
        scratch_shapes=[
            pltpu.SMEM((per_device,), jnp.int32),
            pltpu.VMEM((per_device, length), jnp.float32),
            pltpu.VMEM((per_device, padded_rows), jnp.float32),
            slice_semaphores,
            pltpu.SemaphoreType.DMA((3,)),
        ],
        compiler_params=pltpu.CompilerParams(vmem_limit_bytes=VMEM_BYTES),
        name="fetch",
    )(*place_of(0), in_hbm(shift_index), in_hbm(phase_offset), *lying[:2], left)

    shifted = []

    def encode(group, *earlier):
        image, coil_map = (jnp.swapaxes(array, -3, -2) for array in raw)
        has_next = group + 1 < groups
        place, group_phases = place_of(group), phases
        if not whole_classes:
            group_phases = jnp.take(
                phases, jnp.stack([place[0][1], place[0][1] + per_device]), axis=1
            )
        if earlier:
            image = after(image, *earlier)
        outputs = pl.pallas_call(
            functools.partial(
                encode_kernel,
                slots,
                group,
                rows_of_class(group),
                (rows_of_class(group + 1) or [0]) if has_next else None,
            ),
            in_specs=scalar_specs + [in_vmem] * 4 + [in_place] * 6,
            out_specs=[in_vmem] * (1 + PARTS + 2 * has_next),
            out_shape=[jax.ShapeDtypeStruct((slots, rows, lanes), jnp.bfloat16)]
            + [jax.ShapeDtypeStruct((rows // PARTS, lanes), jnp.bfloat16)] * PARTS
            + raw_shapes * has_next,
            scratch_shapes=[
                pltpu.VMEM((rows, lanes), jnp.float32),
                pltpu.VMEM((tiles, 2 * length, LANE_TILE), jnp.float32),
                pltpu.VMEM(lying[2].shape, jnp.bfloat16),
                pltpu.VMEM(gram.shape, jnp.bfloat16),
                pltpu.VMEM(adjoint.shape, jnp.bfloat16),
                pltpu.SMEM((groups,), jnp.int32),
                slice_semaphores,
                pltpu.SemaphoreType.DMA((4,)),
            ],
            compiler_params=pltpu.CompilerParams(vmem_limit_bytes=VMEM_BYTES),
            cost_estimate=pl.CostEstimate(
                flops=places * (slots + 1) * 16 * length**3,
                bytes_accessed=6_000_000,
                transcendentals=0,
            ),
            name="encode",
        )(
            *place,
            group_phases,
            image,
            coil_map,
            left,
            order,
            gram,
            adjoint,
            lying[2],
            *lying[:2],
        )
        raw[:] = outputs[1 + PARTS :]
        shifted.append(outputs[0])
        return outputs[1 : 1 + PARTS]

    def gradient(terms, piece):
        group, index = divmod(piece, PARTS)
        return pl.pallas_call(
            functools.partial(gradient_kernel, index, factor, on_line),
            out_shape=jax.ShapeDtypeStruct((slots, rows // PARTS), jnp.float32),
            compiler_params=pltpu.CompilerParams(vmem_limit_bytes=VMEM_BYTES),
            cost_estimate=pl.CostEstimate(
                flops=places * slots * 4 * length**2, bytes_accessed=1_500_000, transcendentals=0
            ),
            name="gradient",
        )(*terms, shifted[group])

    if on_line:
        gradients = line_of_four(encode, gradient, groups, ends)
    else:
        reduced = lax.psum([piece for group in range(groups) for piece in encode(group)], "slc")
        gradients = [gradient((piece,), index) for index, piece in enumerate(reduced)]
    by_class = jnp.stack(
        [
            jnp.concatenate(gradients[group * PARTS : (group + 1) * PARTS], axis=1)
            for group in range(groups)
        ],
        axis=1,
    )[:, :, :length]
    if whole_classes:
        local = by_class.reshape(per_device, length)
    else:
        local = lax.dynamic_slice_in_dim(by_class[0], first, per_device, axis=0)
    return sum_over_replicas(local)


def solution(mesh):
    placed = (
        P(("grp", "vol"), "slc", None, None, None),
        P(("grp", "coil"), "slc", None, None, None),
        P(("grp", "vol"), "slc", "coil", None, None, None),
        P("slc"),
        P("slc", None),
        P(),
    )
    return jax.shard_map(
        body, mesh=mesh, in_specs=placed, out_specs=P(("grp", "slc"), None), check_vma=False
    )
```

```python
import functools
import math

import jax
import jax.numpy as jnp
import ml_dtypes
import numpy as np
from jax import lax
from jax.experimental import pallas as pl
from jax.experimental.pallas import tpu as pltpu
from jax.sharding import PartitionSpec as P

MB = 8
ROW_TILE = 16
LANE_TILE = 128
PARTS = 2
VMEM_BYTES = 24 * 1024 * 1024


def round_up(value, multiple):
    return -(-value // multiple) * multiple


def fourier_tables(length):
    positions = np.arange(length, dtype=np.int32)
    product = positions[:, None] * positions[None, :] % length
    radians = np.float32(2.0 * math.pi / length) * product.astype(np.float32)
    factor = np.float32(1.0 / math.sqrt(length))
    return (
        (np.cos(radians) * factor).astype(ml_dtypes.bfloat16),
        (-np.sin(radians) * factor).astype(ml_dtypes.bfloat16),
    )


def dft_matrices(length, rows):
    cos_table, sin_table = fourier_tables(length)
    cosine, sine = cos_table.astype(np.float64), sin_table.astype(np.float64)
    left_re = np.zeros((2 * rows + 8, length), np.float64)
    left_im = np.zeros((2 * rows + 8, length), np.float64)
    left_re[:length], left_re[rows : rows + length] = cosine, sine
    left_im[:length], left_im[rows : rows + length] = -sine, cosine
    gram_re = cosine.T @ cosine + sine.T @ sine
    gram_im = sine.T @ cosine - cosine.T @ sine
    gram = np.stack(
        [np.concatenate([gram_im, -gram_re], 1), np.concatenate([gram_re, gram_im], 1)]
    )
    adjoint = np.stack(
        [np.concatenate([-sine, -cosine], 1), np.concatenate([cosine, -sine], 1)]
    )
    left = np.stack([left_re, left_im])
    return tuple(part.astype(ml_dtypes.bfloat16) for part in (left, gram, adjoint))


def dot(left, right):
    return jnp.dot(left, right, preferred_element_type=jnp.float32)


def at_line_end():
    position = lax.axis_index("slc")
    return (position == 0) | (position == lax.axis_size("slc") - 1)


def start_all(copies):
    for copy in copies:
        copy.start()


def slice_copies(image_ref, map_ref, image_out, map_out, arrived, rows_of):
    vols, coils = image_ref.shape[0], map_ref.shape[0]
    return [
        pltpu.make_async_copy(
            image_ref.at[vol, row], image_out.at[vol, slot], arrived.at[slot, vol]
        )
        for slot, row in enumerate(rows_of)
        for vol in range(vols)
    ] + [
        pltpu.make_async_copy(
            map_ref.at[coil, row], map_out.at[coil, slot], arrived.at[slot, vols + coil]
        )
        for slot, row in enumerate(rows_of)
        for coil in range(coils)
    ]


def fetch_kernel(rows_of, *refs):
    if rows_of is None:
        rows_of, refs = [refs[0][1]], refs[1:]
    shift_ref, offset_ref, image_ref, map_ref, left_ref = refs[:5]
    image_out, map_out, left_out, phase_out, ends_out = refs[5:10]
    shift, offset, angle, arrived, small = refs[10:]
    copies = slice_copies(image_ref, map_ref, image_out, map_out, arrived, rows_of)
    copies.append(pltpu.make_async_copy(left_ref, left_out, small.at[0]))
    early = [
        pltpu.make_async_copy(shift_ref, shift, small.at[1]),
        pltpu.make_async_copy(offset_ref, offset, small.at[2]),
    ]
    start_all(early)
    start_all(copies)
    ends_out[...] = jnp.where(at_line_end(), 1.0, 0.0) * jnp.ones_like(ends_out)
    for copy in early:
        copy.wait()
    per_device, length = offset.shape
    lines = lax.broadcasted_iota(jnp.int32, (1, length), 1) - length // 2
    angle[...] = jnp.zeros_like(angle)
    for row in range(per_device):
        turns = (shift[row] * lines) & (MB - 1)
        angle[row : row + 1, :length] = (
            2.0 * math.pi / MB * turns.astype(jnp.float32) + offset[row : row + 1, :]
        )
    phase_out[:, :per_device] = jnp.cos(angle[...]).T
    phase_out[:, per_device:] = jnp.sin(angle[...]).T
    for copy in copies:
        copy.wait()


def encode_kernel(slots, group, rows_of, next_rows, *refs):
    whole_classes = rows_of is not None
    if not whole_classes:
        place_ref, refs = refs[0], refs[1:]
        next_rows = next_rows and [place_ref[2]]
    phase_ref, image, coil_map, left_ref = refs[:4]
    order_ref, gram_ref, adjoint_ref, kspace_ref, image_ref, map_ref = refs[4:10]
    refs = refs[10:]
    shifted, refs = refs[0], refs[1:]
    out_refs, refs = refs[:PARTS], refs[PARTS:]
    if next_rows:
        next_image, next_map, refs = refs[0], refs[1], refs[2:]
    total, wide, raw_kspace, gram, adjoint, order, arrived, small = refs
    vols, coils, length = image.shape[0], coil_map.shape[0], image.shape[-1]
    _, rows, lanes = shifted.shape
    order_copy = pltpu.make_async_copy(order_ref, order, small.at[0])
    gram_copy = pltpu.make_async_copy(gram_ref, gram, small.at[1])
    owner_copies = [
        pltpu.make_async_copy(kspace_ref, raw_kspace, small.at[2]),
        pltpu.make_async_copy(adjoint_ref, adjoint, small.at[3]),
    ]
    next_copies = []
    if next_rows:
        next_copies = slice_copies(image_ref, map_ref, next_image, next_map, arrived, next_rows)
    start_all([order_copy, gram_copy, *owner_copies, *next_copies])

    if lanes > vols * coils * 2 * length:
        last = slice(lanes - LANE_TILE, lanes)
        total[:, last] = jnp.zeros((rows, LANE_TILE), jnp.float32)
        for slot in range(slots):
            shifted[slot, :, last] = jnp.zeros((rows, LANE_TILE), jnp.bfloat16)
    sums = [None] * (vols * coils)
    for slot in range(slots):
        if whole_classes:
            column = rows_of[slot]
            half = phase_ref.shape[1] // 2
            cosine = phase_ref[:rows, column : column + 1]
            sine = phase_ref[:rows, half + column : half + column + 1]
        else:
            cosine, sine = phase_ref[:rows, :1], phase_ref[:rows, 1:]
        for vol in range(vols):
            image_re = image[vol, slot, 0].astype(jnp.float32)
            image_im = image[vol, slot, 1].astype(jnp.float32)
            for coil in range(coils):
                place = vol * coils + coil
                base = place * 2 * length
                map_re = coil_map[coil, slot, 0].astype(jnp.float32)
                map_im = coil_map[coil, slot, 1].astype(jnp.float32)
                coil_re = (map_re * image_re - map_im * image_im).astype(jnp.bfloat16)
                coil_im = (map_re * image_im + map_im * image_re).astype(jnp.bfloat16)
                partly = dot(left_ref[0, : 2 * rows], coil_re) + dot(
                    left_ref[1, : 2 * rows], coil_im
                )
                part_re, part_im = partly[:rows], partly[rows:]
                shift_re = part_re * cosine - part_im * sine
                shift_im = part_re * sine + part_im * cosine
                shifted[slot, :, base : base + length] = shift_re.astype(jnp.bfloat16)
                shifted[slot, :, base + length : base + 2 * length] = shift_im.astype(
                    jnp.bfloat16
                )
                if slot > 0:
                    shift_re, shift_im = sums[place][0] + shift_re, sums[place][1] + shift_im
                sums[place] = (shift_re, shift_im)
    gram_copy.wait()
    for place, (sum_re, sum_im) in enumerate(sums):
        mixed = dot(sum_re.astype(jnp.bfloat16), gram[0]) + dot(
            sum_im.astype(jnp.bfloat16), gram[1]
        )
        if not whole_classes:
            mixed = jnp.where(place_ref[0] > 0, mixed, 0.0)
        total[:, place * 2 * length : (place + 1) * 2 * length] = mixed

    order_copy.wait()
    for copy in owner_copies:
        copy.wait()

    @pl.when(order[group] == lax.axis_index("slc"))
    def _():
        for vol in range(vols):
            for coil in range(coils):
                place = vol * coils + coil
                lying = raw_kspace.at[vol, 0, coil].reshape(2 * length, length)[...]
                measured = None
                for kind in range(2):
                    for tile in range(wide.shape[0]):
                        at, end = tile * LANE_TILE, min(length, (tile + 1) * LANE_TILE)
                        if kind == 0:
                            wide[tile, :, : end - at] = lying[:, at:end].astype(jnp.float32)
                        rows_read = wide[tile, pl.ds(kind, length, stride=2), :]
                        term = dot(
                            rows_read[:, : end - at].astype(jnp.bfloat16), adjoint[kind, at:end, :]
                        )
                        measured = term if measured is None else measured + term
                total[:length, place * 2 * length : (place + 1) * 2 * length] -= measured

    part = rows // PARTS
    for index, out_ref in enumerate(out_refs):
        out_ref[...] = total[index * part : (index + 1) * part, :].astype(jnp.bfloat16)
    for copy in next_copies:
        copy.wait()


def gradient_kernel(index, factor, on_line, *refs):
    term_refs, shifted_ref, out_ref = refs[:-2], refs[-2], refs[-1]
    slots, rows, lanes = shifted_ref.shape
    part = rows // PARTS
    terms = [ref[...].astype(jnp.float32) for ref in term_refs]
    residual = terms[0]
    if on_line:
        near, across, rest = terms[1:]
        residual += jnp.where(at_line_end(), rest, near + across)
    for slot in range(slots):
        product = residual * shifted_ref[slot, index * part : (index + 1) * part, :].astype(
            jnp.float32
        )
        tiles = [product[:, at : at + LANE_TILE] for at in range(0, lanes, LANE_TILE)]
        folded = functools.reduce(lambda a, b: a + b, tiles)
        out_ref[slot : slot + 1, :] = factor * jnp.sum(folded.T, axis=0, keepdims=True)


def after(value, *earlier):
    return lax.optimization_barrier((value, *earlier))[0]


def sum_over_replicas(value):
    axes = ("coil", "vol")
    if any(lax.axis_size(axis) != 2 for axis in axes):
        return lax.psum(value, axes)
    swapped = [
        lax.ppermute(value, axes, [(index, index ^ mask) for index in range(4)])
        for mask in (1, 2, 3)
    ]
    return (value + swapped[0]) + (swapped[1] + swapped[2])


def line_of_four(encode, gradient, groups, ends):
    cores = lax.axis_size("vol")
    count = groups * PARTS
    outer_pairs = [(0, 1), (1, 0), (2, 3), (3, 2)]
    inner_pairs = [
        (source * cores + core, target * cores + (core ^ 1 if swap and cores % 2 == 0 else core))
        for source, target, swap in ((0, 0, True), (1, 2, False), (2, 1, False), (3, 3, True))
        for core in range(cores)
    ]

    def outer(value):
        return lax.ppermute(value, "slc", outer_pairs)

    def inner(value):
        return lax.ppermute(value, ("slc", "vol"), inner_pairs)

    own = [*encode(0)]
    near, across, gradients, encoded = [outer(own[0])], [], [], 1

    def encode_more(wanted, *earlier):
        nonlocal encoded
        while len(own) < min(wanted, count):
            own.extend(encode(encoded, *earlier))
            encoded += 1

    def gradient_of(piece, *earlier):
        terms = (own[piece], near[piece], across[piece], near[piece + 3])
        if earlier:
            terms = (after(terms[0], *earlier), *terms[1:])
        gradients.append(gradient(terms, piece))

    encode_more(5)
    near.append(outer(after(own[1], own[4])))
    latest = own[4]
    for step in range(count):
        half = own[step] + after(near[step], latest)
        across.append(inner(half))
        payload = own[step + 2] if step + 2 < count else None
        if step >= 1:
            others = own[step - 1] + after(across[step - 1], half)
            payload = others if payload is None else jnp.where(ends > 0, payload, others)
        else:
            payload = after(payload, half)
        near.append(outer(payload))
        latest = payload
        if len(own) < min(step + 7, count):
            encode_more(step + 7, payload)
            latest = own[-1]
        if step >= 3:
            gradient_of(step - 3, payload)
    last = own[count - 1] + after(across[count - 1], latest, near[count])
    near.append(outer(last))
    for piece in range(count - 3, count):
        gradient_of(piece, last)
    return gradients


def body(images, coil_maps, kspace, shift_index, phase_offset, group_order):
    vols, per_device, _, _, length = images.shape
    coils = coil_maps.shape[0]
    groups = lax.axis_size("slc")
    rows = round_up(length, ROW_TILE * PARTS)
    places = vols * coils
    lanes = round_up(places * 2 * length, LANE_TILE)
    whole_classes = per_device % groups == 0
    slots = max(1, per_device // groups)
    tables = dft_matrices(length, rows)
    factor = 1.0 / (coils * lax.axis_size("coil") * vols * lax.axis_size("vol"))
    first = (lax.axis_index("slc") * per_device) % groups
    on_line = whole_classes and groups == 4
    in_vmem = pl.BlockSpec(memory_space=pltpu.VMEM)
    in_smem = pl.BlockSpec(memory_space=pltpu.SMEM)
    in_place = pl.BlockSpec(memory_space=pl.ANY)

    def in_hbm(array):
        return pltpu.with_memory_space_constraint(jnp.asarray(array), pltpu.HBM)

    def rows_of_class(group):
        return [slot * groups + group for slot in range(slots)] if whole_classes else None

    def place_of(group):
        if whole_classes:
            return ()
        held = [(group + step - first, per_device) for step in range(2)]
        inside = [(within >= 0) & (within < size) for within, size in held]
        rows_held = [jnp.where(yes, held[i][0], 0) for i, yes in enumerate(inside)]
        return (jnp.stack([inside[0], rows_held[0], rows_held[1]]).astype(jnp.int32),)

    left, gram, adjoint = (in_hbm(table) for table in tables)
    lying = [in_hbm(jnp.swapaxes(array, -3, -2)) for array in (images, coil_maps, kspace)]
    order = in_hbm(group_order)
    tiles = round_up(length, LANE_TILE) // LANE_TILE
    raw_shapes = [
        jax.ShapeDtypeStruct((count, slots, length, 2, length), jnp.bfloat16)
        for count in (vols, coils)
    ]
    scalar_specs = [] if whole_classes else [in_smem]
    padded_rows = round_up(rows, LANE_TILE)
    slice_semaphores = pltpu.SemaphoreType.DMA((slots, vols + coils))
    *raw, left, phases, ends = pl.pallas_call(
        functools.partial(fetch_kernel, rows_of_class(0)),
        in_specs=scalar_specs + [in_place] * 5,
        out_specs=[in_vmem] * 5,
        out_shape=raw_shapes
        + [
            jax.ShapeDtypeStruct(left.shape, left.dtype),
            jax.ShapeDtypeStruct((padded_rows, 2 * per_device), jnp.float32),
            jax.ShapeDtypeStruct((1, lanes), jnp.float32),
        ],
        scratch_shapes=[
            pltpu.SMEM((per_device,), jnp.int32),
            pltpu.VMEM((per_device, length), jnp.float32),
            pltpu.VMEM((per_device, padded_rows), jnp.float32),
            slice_semaphores,
            pltpu.SemaphoreType.DMA((3,)),
        ],
        compiler_params=pltpu.CompilerParams(vmem_limit_bytes=VMEM_BYTES),
        name="fetch",
    )(*place_of(0), in_hbm(shift_index), in_hbm(phase_offset), *lying[:2], left)

    shifted = []

    def encode(group, *earlier):
        image, coil_map = (jnp.swapaxes(array, -3, -2) for array in raw)
        has_next = group + 1 < groups
        place, group_phases = place_of(group), phases
        if not whole_classes:
            group_phases = jnp.take(
                phases, jnp.stack([place[0][1], place[0][1] + per_device]), axis=1
            )
        if earlier:
            image = after(image, *earlier)
        outputs = pl.pallas_call(
            functools.partial(
                encode_kernel,
                slots,
                group,
                rows_of_class(group),
                (rows_of_class(group + 1) or [0]) if has_next else None,
            ),
            in_specs=scalar_specs + [in_vmem] * 4 + [in_place] * 6,
            out_specs=[in_vmem] * (1 + PARTS + 2 * has_next),
            out_shape=[jax.ShapeDtypeStruct((slots, rows, lanes), jnp.bfloat16)]
            + [jax.ShapeDtypeStruct((rows // PARTS, lanes), jnp.bfloat16)] * PARTS
            + raw_shapes * has_next,
            scratch_shapes=[
                pltpu.VMEM((rows, lanes), jnp.float32),
                pltpu.VMEM((tiles, 2 * length, LANE_TILE), jnp.float32),
                pltpu.VMEM(lying[2].shape, jnp.bfloat16),
                pltpu.VMEM(gram.shape, jnp.bfloat16),
                pltpu.VMEM(adjoint.shape, jnp.bfloat16),
                pltpu.SMEM((groups,), jnp.int32),
                slice_semaphores,
                pltpu.SemaphoreType.DMA((4,)),
            ],
            compiler_params=pltpu.CompilerParams(vmem_limit_bytes=VMEM_BYTES),
            cost_estimate=pl.CostEstimate(
                flops=places * (slots + 1) * 16 * length**3,
                bytes_accessed=6_000_000,
                transcendentals=0,
            ),
            name="encode",
        )(
            *place,
            group_phases,
            image,
            coil_map,
            left,
            order,
            gram,
            adjoint,
            lying[2],
            *lying[:2],
        )
        raw[:] = outputs[1 + PARTS :]
        shifted.append(outputs[0])
        return outputs[1 : 1 + PARTS]

    def gradient(terms, piece):
        group, index = divmod(piece, PARTS)
        return pl.pallas_call(
            functools.partial(gradient_kernel, index, factor, on_line),
            out_shape=jax.ShapeDtypeStruct((slots, rows // PARTS), jnp.float32),
            compiler_params=pltpu.CompilerParams(vmem_limit_bytes=VMEM_BYTES),
            cost_estimate=pl.CostEstimate(
                flops=places * slots * 4 * length**2, bytes_accessed=1_500_000, transcendentals=0
            ),
            name="gradient",
        )(*terms, shifted[group])

    if on_line:
        gradients = line_of_four(encode, gradient, groups, ends)
    else:
        reduced = lax.psum([piece for group in range(groups) for piece in encode(group)], "slc")
        gradients = [gradient((piece,), index) for index, piece in enumerate(reduced)]
    by_class = jnp.stack(
        [
            jnp.concatenate(gradients[group * PARTS : (group + 1) * PARTS], axis=1)
            for group in range(groups)
        ],
        axis=1,
    )[:, :, :length]
    if whole_classes:
        local = by_class.reshape(per_device, length)
    else:
        local = lax.dynamic_slice_in_dim(by_class[0], first, per_device, axis=0)
    return sum_over_replicas(local)


def solution(mesh):
    placed = (
        P(("grp", "vol"), "slc", None, None, None),
        P(("grp", "coil"), "slc", None, None, None),
        P(("grp", "vol"), "slc", "coil", None, None, None),
        P("slc"),
        P("slc", None),
        P(),
    )
    return jax.shard_map(
        body, mesh=mesh, in_specs=placed, out_specs=P(("grp", "slc"), None), check_vma=False
    )
```

```python
import functools
import math

import jax
import jax.numpy as jnp
import ml_dtypes
import numpy as np
from jax import lax
from jax.experimental import pallas as pl
from jax.experimental.pallas import tpu as pltpu
from jax.sharding import PartitionSpec as P

MB = 8
ROW_TILE = 16
LANE_TILE = 128
PARTS = 2
VMEM_BYTES = 24 * 1024 * 1024


def round_up(value, multiple):
    return -(-value // multiple) * multiple


def fourier_tables(length):
    positions = np.arange(length, dtype=np.int32)
    product = positions[:, None] * positions[None, :] % length
    radians = np.float32(2.0 * math.pi / length) * product.astype(np.float32)
    factor = np.float32(1.0 / math.sqrt(length))
    return (
        (np.cos(radians) * factor).astype(ml_dtypes.bfloat16),
        (-np.sin(radians) * factor).astype(ml_dtypes.bfloat16),
    )


def dft_matrices(length, rows):
    cos_table, sin_table = fourier_tables(length)
    cosine, sine = cos_table.astype(np.float64), sin_table.astype(np.float64)
    left_re = np.zeros((2 * rows + 8, length), np.float64)
    left_im = np.zeros((2 * rows + 8, length), np.float64)
    left_re[:length], left_re[rows : rows + length] = cosine, sine
    left_im[:length], left_im[rows : rows + length] = -sine, cosine
    gram_re = cosine.T @ cosine + sine.T @ sine
    gram_im = sine.T @ cosine - cosine.T @ sine
    gram = np.stack(
        [np.concatenate([gram_im, -gram_re], 1), np.concatenate([gram_re, gram_im], 1)]
    )
    adjoint = np.stack(
        [np.concatenate([-sine, -cosine], 1), np.concatenate([cosine, -sine], 1)]
    )
    left = np.stack([left_re, left_im])
    return tuple(part.astype(ml_dtypes.bfloat16) for part in (left, gram, adjoint))


def dot(left, right):
    return jnp.dot(left, right, preferred_element_type=jnp.float32)


def at_line_end():
    position = lax.axis_index("slc")
    return (position == 0) | (position == lax.axis_size("slc") - 1)


def start_all(copies):
    for copy in copies:
        copy.start()


def slice_copies(image_ref, map_ref, image_out, map_out, arrived, rows_of):
    vols, coils = image_ref.shape[0], map_ref.shape[0]
    return [
        pltpu.make_async_copy(
            image_ref.at[vol, row], image_out.at[vol, slot], arrived.at[slot, vol]
        )
        for slot, row in enumerate(rows_of)
        for vol in range(vols)
    ] + [
        pltpu.make_async_copy(
            map_ref.at[coil, row], map_out.at[coil, slot], arrived.at[slot, vols + coil]
        )
        for slot, row in enumerate(rows_of)
        for coil in range(coils)
    ]


def fetch_kernel(rows_of, *refs):
    if rows_of is None:
        rows_of, refs = [refs[0][1]], refs[1:]
    shift_ref, offset_ref, image_ref, map_ref, left_ref = refs[:5]
    image_out, map_out, left_out, phase_out, ends_out = refs[5:10]
    shift, offset, angle, arrived, small = refs[10:]
    copies = slice_copies(image_ref, map_ref, image_out, map_out, arrived, rows_of)
    copies.append(pltpu.make_async_copy(left_ref, left_out, small.at[0]))
    early = [
        pltpu.make_async_copy(shift_ref, shift, small.at[1]),
        pltpu.make_async_copy(offset_ref, offset, small.at[2]),
    ]
    start_all(early)
    start_all(copies)
    ends_out[...] = jnp.where(at_line_end(), 1.0, 0.0) * jnp.ones_like(ends_out)
    for copy in early:
        copy.wait()
    per_device, length = offset.shape
    lines = lax.broadcasted_iota(jnp.int32, (1, length), 1) - length // 2
    angle[...] = jnp.zeros_like(angle)
    for row in range(per_device):
        turns = (shift[row] * lines) & (MB - 1)
        angle[row : row + 1, :length] = (
            2.0 * math.pi / MB * turns.astype(jnp.float32) + offset[row : row + 1, :]
        )
    phase_out[:, :per_device] = jnp.cos(angle[...]).T
    phase_out[:, per_device:] = jnp.sin(angle[...]).T
    for copy in copies:
        copy.wait()


def encode_kernel(slots, group, rows_of, next_rows, *refs):
    whole_classes = rows_of is not None
    if not whole_classes:
        place_ref, refs = refs[0], refs[1:]
        next_rows = next_rows and [place_ref[2]]
    phase_ref, image, coil_map, left_ref = refs[:4]
    order_ref, gram_ref, adjoint_ref, kspace_ref, image_ref, map_ref = refs[4:10]
    refs = refs[10:]
    shifted, refs = refs[0], refs[1:]
    out_refs, refs = refs[:PARTS], refs[PARTS:]
    if next_rows:
        next_image, next_map, refs = refs[0], refs[1], refs[2:]
    total, wide, raw_kspace, gram, adjoint, order, arrived, small = refs
    vols, coils, length = image.shape[0], coil_map.shape[0], image.shape[-1]
    _, rows, lanes = shifted.shape
    order_copy = pltpu.make_async_copy(order_ref, order, small.at[0])
    gram_copy = pltpu.make_async_copy(gram_ref, gram, small.at[1])
    owner_copies = [
        pltpu.make_async_copy(kspace_ref, raw_kspace, small.at[2]),
        pltpu.make_async_copy(adjoint_ref, adjoint, small.at[3]),
    ]
    next_copies = []
    if next_rows:
        next_copies = slice_copies(image_ref, map_ref, next_image, next_map, arrived, next_rows)
    start_all([order_copy, gram_copy, *next_copies])

    if lanes > vols * coils * 2 * length:
        last = slice(lanes - LANE_TILE, lanes)
        total[:, last] = jnp.zeros((rows, LANE_TILE), jnp.float32)
        for slot in range(slots):
            shifted[slot, :, last] = jnp.zeros((rows, LANE_TILE), jnp.bfloat16)
    sums = [None] * (vols * coils)
    for slot in range(slots):
        if whole_classes:
            column = rows_of[slot]
            half = phase_ref.shape[1] // 2
            cosine = phase_ref[:rows, column : column + 1]
            sine = phase_ref[:rows, half + column : half + column + 1]
        else:
            cosine, sine = phase_ref[:rows, :1], phase_ref[:rows, 1:]
        for vol in range(vols):
            image_re = image[vol, slot, 0].astype(jnp.float32)
            image_im = image[vol, slot, 1].astype(jnp.float32)
            for coil in range(coils):
                place = vol * coils + coil
                base = place * 2 * length
                map_re = coil_map[coil, slot, 0].astype(jnp.float32)
                map_im = coil_map[coil, slot, 1].astype(jnp.float32)
                coil_re = (map_re * image_re - map_im * image_im).astype(jnp.bfloat16)
                coil_im = (map_re * image_im + map_im * image_re).astype(jnp.bfloat16)
                partly = dot(left_ref[0, : 2 * rows], coil_re) + dot(
                    left_ref[1, : 2 * rows], coil_im
                )
                part_re, part_im = partly[:rows], partly[rows:]
                shift_re = part_re * cosine - part_im * sine
                shift_im = part_re * sine + part_im * cosine
                shifted[slot, :, base : base + length] = shift_re.astype(jnp.bfloat16)
                shifted[slot, :, base + length : base + 2 * length] = shift_im.astype(
                    jnp.bfloat16
                )
                if slot > 0:
                    shift_re, shift_im = sums[place][0] + shift_re, sums[place][1] + shift_im
                sums[place] = (shift_re, shift_im)
        if slot == 0:
            order_copy.wait()
            owner = order[group] == lax.axis_index("slc")

            @pl.when(owner)
            def _():
                start_all(owner_copies)

    gram_copy.wait()
    for place, (sum_re, sum_im) in enumerate(sums):
        mixed = dot(sum_re.astype(jnp.bfloat16), gram[0]) + dot(
            sum_im.astype(jnp.bfloat16), gram[1]
        )
        if not whole_classes:
            mixed = jnp.where(place_ref[0] > 0, mixed, 0.0)
        total[:, place * 2 * length : (place + 1) * 2 * length] = mixed

    @pl.when(owner)
    def _():
        for copy in owner_copies:
            copy.wait()
        for vol in range(vols):
            for coil in range(coils):
                place = vol * coils + coil
                lying = raw_kspace.at[vol, 0, coil].reshape(2 * length, length)[...]
                measured = None
                for kind in range(2):
                    for tile in range(wide.shape[0]):
                        at, end = tile * LANE_TILE, min(length, (tile + 1) * LANE_TILE)
                        if kind == 0:
                            wide[tile, :, : end - at] = lying[:, at:end].astype(jnp.float32)
                        rows_read = wide[tile, pl.ds(kind, length, stride=2), :]
                        term = dot(
                            rows_read[:, : end - at].astype(jnp.bfloat16), adjoint[kind, at:end, :]
                        )
                        measured = term if measured is None else measured + term
                total[:length, place * 2 * length : (place + 1) * 2 * length] -= measured

    part = rows // PARTS
    for index, out_ref in enumerate(out_refs):
        out_ref[...] = total[index * part : (index + 1) * part, :].astype(jnp.bfloat16)
    for copy in next_copies:
        copy.wait()


def gradient_kernel(index, factor, on_line, *refs):
    term_refs, shifted_ref, out_ref = refs[:-2], refs[-2], refs[-1]
    slots, rows, lanes = shifted_ref.shape
    part = rows // PARTS
    terms = [ref[...].astype(jnp.float32) for ref in term_refs]
    residual = terms[0]
    if on_line:
        near, across, rest = terms[1:]
        residual += jnp.where(at_line_end(), rest, near + across)
    for slot in range(slots):
        product = residual * shifted_ref[slot, index * part : (index + 1) * part, :].astype(
            jnp.float32
        )
        tiles = [product[:, at : at + LANE_TILE] for at in range(0, lanes, LANE_TILE)]
        folded = functools.reduce(lambda a, b: a + b, tiles)
        out_ref[slot : slot + 1, :] = factor * jnp.sum(folded.T, axis=0, keepdims=True)


def after(value, *earlier):
    return lax.optimization_barrier((value, *earlier))[0]


def sum_over_replicas(value):
    axes = ("coil", "vol")
    if any(lax.axis_size(axis) != 2 for axis in axes):
        return lax.psum(value, axes)
    swapped = [
        lax.ppermute(value, axes, [(index, index ^ mask) for index in range(4)])
        for mask in (1, 2, 3)
    ]
    return (value + swapped[0]) + (swapped[1] + swapped[2])


def line_of_four(encode, gradient, groups, ends):
    cores = lax.axis_size("vol")
    count = groups * PARTS
    outer_pairs = [(0, 1), (1, 0), (2, 3), (3, 2)]
    inner_pairs = [
        (source * cores + core, target * cores + (core ^ 1 if swap and cores % 2 == 0 else core))
        for source, target, swap in ((0, 0, True), (1, 2, False), (2, 1, False), (3, 3, True))
        for core in range(cores)
    ]

    def outer(value):
        return lax.ppermute(value, "slc", outer_pairs)

    def inner(value):
        return lax.ppermute(value, ("slc", "vol"), inner_pairs)

    own = [*encode(0)]
    near, across, gradients, encoded = [outer(own[0])], [], [], 1

    def encode_more(wanted, *earlier):
        nonlocal encoded
        while len(own) < min(wanted, count):
            own.extend(encode(encoded, *earlier))
            encoded += 1

    def gradient_of(piece, *earlier):
        terms = (own[piece], near[piece], across[piece], near[piece + 4])
        gradients.append(gradient((after(terms[0], *earlier), *terms[1:]), piece))

    encode_more(3)
    near.append(outer(after(own[1], own[2])))
    encode_more(5)
    latest = own[4]
    for step in range(count):
        half = own[step] + after(near[step], latest)
        across.append(inner(half))
        payload = own[step + 2] if step + 2 < count else None
        if step >= 2:
            others = own[step - 2] + after(across[step - 2], half)
            payload = others if payload is None else jnp.where(ends > 0, payload, others)
        else:
            payload = after(payload, half)
        near.append(outer(payload))
        latest = payload
        if len(own) < min(step + 7, count):
            encode_more(step + 7, payload)
            latest = own[-1]
        if step >= 4:
            gradient_of(step - 4, payload)
    for piece in range(count - 2, count):
        latest = own[piece] + after(across[piece], latest, near[count])
        near.append(outer(latest))
    for piece in range(count - 4, count):
        gradient_of(piece, latest)
    return gradients


def body(images, coil_maps, kspace, shift_index, phase_offset, group_order):
    vols, per_device, _, _, length = images.shape
    coils = coil_maps.shape[0]
    groups = lax.axis_size("slc")
    rows = round_up(length, ROW_TILE * PARTS)
    places = vols * coils
    lanes = round_up(places * 2 * length, LANE_TILE)
    whole_classes = per_device % groups == 0
    slots = max(1, per_device // groups)
    tables = dft_matrices(length, rows)
    factor = 1.0 / (coils * lax.axis_size("coil") * vols * lax.axis_size("vol"))
    first = (lax.axis_index("slc") * per_device) % groups
    on_line = whole_classes and groups == 4
    in_vmem = pl.BlockSpec(memory_space=pltpu.VMEM)
    in_smem = pl.BlockSpec(memory_space=pltpu.SMEM)
    in_place = pl.BlockSpec(memory_space=pl.ANY)

    def in_hbm(array):
        return pltpu.with_memory_space_constraint(jnp.asarray(array), pltpu.HBM)

    def rows_of_class(group):
        return [slot * groups + group for slot in range(slots)] if whole_classes else None

    def place_of(group):
        if whole_classes:
            return ()
        held = [(group + step - first, per_device) for step in range(2)]
        inside = [(within >= 0) & (within < size) for within, size in held]
        rows_held = [jnp.where(yes, held[i][0], 0) for i, yes in enumerate(inside)]
        return (jnp.stack([inside[0], rows_held[0], rows_held[1]]).astype(jnp.int32),)

    left, gram, adjoint = (in_hbm(table) for table in tables)
    lying = [in_hbm(jnp.swapaxes(array, -3, -2)) for array in (images, coil_maps, kspace)]
    order = in_hbm(group_order)
    tiles = round_up(length, LANE_TILE) // LANE_TILE
    raw_shapes = [
        jax.ShapeDtypeStruct((count, slots, length, 2, length), jnp.bfloat16)
        for count in (vols, coils)
    ]
    scalar_specs = [] if whole_classes else [in_smem]
    padded_rows = round_up(rows, LANE_TILE)
    slice_semaphores = pltpu.SemaphoreType.DMA((slots, vols + coils))
    *raw, left, phases, ends = pl.pallas_call(
        functools.partial(fetch_kernel, rows_of_class(0)),
        in_specs=scalar_specs + [in_place] * 5,
        out_specs=[in_vmem] * 5,
        out_shape=raw_shapes
        + [
            jax.ShapeDtypeStruct(left.shape, left.dtype),
            jax.ShapeDtypeStruct((padded_rows, 2 * per_device), jnp.float32),
            jax.ShapeDtypeStruct((1, lanes), jnp.float32),
        ],
        scratch_shapes=[
            pltpu.SMEM((per_device,), jnp.int32),
            pltpu.VMEM((per_device, length), jnp.float32),
            pltpu.VMEM((per_device, padded_rows), jnp.float32),
            slice_semaphores,
            pltpu.SemaphoreType.DMA((3,)),
        ],
        compiler_params=pltpu.CompilerParams(vmem_limit_bytes=VMEM_BYTES),
        name="fetch",
    )(*place_of(0), in_hbm(shift_index), in_hbm(phase_offset), *lying[:2], left)

    shifted = []

    def encode(group, *earlier):
        image, coil_map = (jnp.swapaxes(array, -3, -2) for array in raw)
        has_next = group + 1 < groups
        place, group_phases = place_of(group), phases
        if not whole_classes:
            group_phases = jnp.take(
                phases, jnp.stack([place[0][1], place[0][1] + per_device]), axis=1
            )
        if earlier:
            image = after(image, *earlier)
        outputs = pl.pallas_call(
            functools.partial(
                encode_kernel,
                slots,
                group,
                rows_of_class(group),
                (rows_of_class(group + 1) or [0]) if has_next else None,
            ),
            in_specs=scalar_specs + [in_vmem] * 4 + [in_place] * 6,
            out_specs=[in_vmem] * (1 + PARTS + 2 * has_next),
            out_shape=[jax.ShapeDtypeStruct((slots, rows, lanes), jnp.bfloat16)]
            + [jax.ShapeDtypeStruct((rows // PARTS, lanes), jnp.bfloat16)] * PARTS
            + raw_shapes * has_next,
            scratch_shapes=[
                pltpu.VMEM((rows, lanes), jnp.float32),
                pltpu.VMEM((tiles, 2 * length, LANE_TILE), jnp.float32),
                pltpu.VMEM(lying[2].shape, jnp.bfloat16),
                pltpu.VMEM(gram.shape, jnp.bfloat16),
                pltpu.VMEM(adjoint.shape, jnp.bfloat16),
                pltpu.SMEM((groups,), jnp.int32),
                slice_semaphores,
                pltpu.SemaphoreType.DMA((4,)),
            ],
            compiler_params=pltpu.CompilerParams(vmem_limit_bytes=VMEM_BYTES),
            cost_estimate=pl.CostEstimate(
                flops=places * (slots + 1) * 16 * length**3,
                bytes_accessed=6_000_000,
                transcendentals=0,
            ),
            name="encode",
        )(
            *place,
            group_phases,
            image,
            coil_map,
            left,
            order,
            gram,
            adjoint,
            lying[2],
            *lying[:2],
        )
        raw[:] = outputs[1 + PARTS :]
        shifted.append(outputs[0])
        return outputs[1 : 1 + PARTS]

    def gradient(terms, piece):
        group, index = divmod(piece, PARTS)
        return pl.pallas_call(
            functools.partial(gradient_kernel, index, factor, on_line),
            out_shape=jax.ShapeDtypeStruct((slots, rows // PARTS), jnp.float32),
            compiler_params=pltpu.CompilerParams(vmem_limit_bytes=VMEM_BYTES),
            cost_estimate=pl.CostEstimate(
                flops=places * slots * 4 * length**2, bytes_accessed=1_500_000, transcendentals=0
            ),
            name="gradient",
        )(*terms, shifted[group])

    if on_line:
        gradients = line_of_four(encode, gradient, groups, ends)
    else:
        reduced = lax.psum([piece for group in range(groups) for piece in encode(group)], "slc")
        gradients = [gradient((piece,), index) for index, piece in enumerate(reduced)]
    by_class = jnp.stack(
        [
            jnp.concatenate(gradients[group * PARTS : (group + 1) * PARTS], axis=1)
            for group in range(groups)
        ],
        axis=1,
    )[:, :, :length]
    if whole_classes:
        local = by_class.reshape(per_device, length)
    else:
        local = lax.dynamic_slice_in_dim(by_class[0], first, per_device, axis=0)
    return sum_over_replicas(local)


def solution(mesh):
    placed = (
        P(("grp", "vol"), "slc", None, None, None),
        P(("grp", "coil"), "slc", None, None, None),
        P(("grp", "vol"), "slc", "coil", None, None, None),
        P("slc"),
        P("slc", None),
        P(),
    )
    return jax.shard_map(
        body, mesh=mesh, in_specs=placed, out_specs=P(("grp", "slc"), None), check_vma=False
    )
```

```python
import functools
import math

import jax
import jax.numpy as jnp
import ml_dtypes
import numpy as np
from jax import lax
from jax.experimental import pallas as pl
from jax.experimental.pallas import tpu as pltpu
from jax.sharding import PartitionSpec as P

MB = 8
ROW_TILE = 16
LANE_TILE = 128
PARTS = 2
VMEM_BYTES = 24 * 1024 * 1024


def round_up(value, multiple):
    return -(-value // multiple) * multiple


def fourier_tables(length):
    positions = np.arange(length, dtype=np.int32)
    product = positions[:, None] * positions[None, :] % length
    radians = np.float32(2.0 * math.pi / length) * product.astype(np.float32)
    factor = np.float32(1.0 / math.sqrt(length))
    return (
        (np.cos(radians) * factor).astype(ml_dtypes.bfloat16),
        (-np.sin(radians) * factor).astype(ml_dtypes.bfloat16),
    )


def dft_matrices(length, rows):
    cos_table, sin_table = fourier_tables(length)
    cosine, sine = cos_table.astype(np.float64), sin_table.astype(np.float64)
    left_re = np.zeros((2 * rows + 8, length), np.float64)
    left_im = np.zeros((2 * rows + 8, length), np.float64)
    left_re[:length], left_re[rows : rows + length] = cosine, sine
    left_im[:length], left_im[rows : rows + length] = -sine, cosine
    gram_re = cosine.T @ cosine + sine.T @ sine
    gram_im = sine.T @ cosine - cosine.T @ sine
    gram = np.stack(
        [np.concatenate([gram_im, -gram_re], 1), np.concatenate([gram_re, gram_im], 1)]
    )
    adjoint = np.stack(
        [np.concatenate([-sine, -cosine], 1), np.concatenate([cosine, -sine], 1)]
    )
    left = np.stack([left_re, left_im])
    return tuple(part.astype(ml_dtypes.bfloat16) for part in (left, gram, adjoint))


def dot(left, right):
    return jnp.dot(left, right, preferred_element_type=jnp.float32)


def at_line_end():
    position = lax.axis_index("slc")
    return (position == 0) | (position == lax.axis_size("slc") - 1)


def start_all(copies):
    for copy in copies:
        copy.start()


def slice_copies(image_ref, map_ref, image_out, map_out, arrived, rows_of):
    vols, coils = image_ref.shape[0], map_ref.shape[0]
    return [
        pltpu.make_async_copy(
            image_ref.at[vol, row], image_out.at[vol, slot], arrived.at[slot, vol]
        )
        for slot, row in enumerate(rows_of)
        for vol in range(vols)
    ] + [
        pltpu.make_async_copy(
            map_ref.at[coil, row], map_out.at[coil, slot], arrived.at[slot, vols + coil]
        )
        for slot, row in enumerate(rows_of)
        for coil in range(coils)
    ]


def fetch_kernel(rows_of, *refs):
    if rows_of is None:
        rows_of, refs = [refs[0][1]], refs[1:]
    shift_ref, offset_ref, image_ref, map_ref, left_ref = refs[:5]
    image_out, map_out, left_out, phase_out, ends_out = refs[5:10]
    shift, offset, angle, arrived, small = refs[10:]
    copies = slice_copies(image_ref, map_ref, image_out, map_out, arrived, rows_of)
    copies.append(pltpu.make_async_copy(left_ref, left_out, small.at[0]))
    early = [
        pltpu.make_async_copy(shift_ref, shift, small.at[1]),
        pltpu.make_async_copy(offset_ref, offset, small.at[2]),
    ]
    start_all(early)
    start_all(copies)
    ends_out[...] = jnp.where(at_line_end(), 1.0, 0.0) * jnp.ones_like(ends_out)
    for copy in early:
        copy.wait()
    per_device, length = offset.shape
    lines = lax.broadcasted_iota(jnp.int32, (1, length), 1) - length // 2
    angle[...] = jnp.zeros_like(angle)
    for row in range(per_device):
        turns = (shift[row] * lines) & (MB - 1)
        angle[row : row + 1, :length] = (
            2.0 * math.pi / MB * turns.astype(jnp.float32) + offset[row : row + 1, :]
        )
    phase_out[:, :per_device] = jnp.cos(angle[...]).T
    phase_out[:, per_device:] = jnp.sin(angle[...]).T
    for copy in copies:
        copy.wait()


def encode_kernel(slots, group, rows_of, next_rows, *refs):
    whole_classes = rows_of is not None
    if not whole_classes:
        place_ref, refs = refs[0], refs[1:]
        next_rows = next_rows and [place_ref[2]]
    phase_ref, image, coil_map, left_ref, kspace_ref = refs[:5]
    order_ref, gram_ref, adjoint_ref, image_ref, map_ref = refs[5:10]
    refs = refs[10:]
    shifted, refs = refs[0], refs[1:]
    out_refs, refs = refs[:PARTS], refs[PARTS:]
    if next_rows:
        next_image, next_map, refs = refs[0], refs[1], refs[2:]
    total, gram, adjoint, order, arrived, small = refs
    vols, coils, length = image.shape[0], coil_map.shape[0], image.shape[-1]
    _, rows, lanes = shifted.shape
    order_copy = pltpu.make_async_copy(order_ref, order, small.at[0])
    gram_copy = pltpu.make_async_copy(gram_ref, gram, small.at[1])
    owner_copies = [pltpu.make_async_copy(adjoint_ref, adjoint, small.at[2])]
    next_copies = []
    if next_rows:
        next_copies = slice_copies(image_ref, map_ref, next_image, next_map, arrived, next_rows)
    start_all([order_copy, gram_copy, *next_copies])

    if lanes > vols * coils * 2 * length:
        last = slice(lanes - LANE_TILE, lanes)
        total[:, last] = jnp.zeros((rows, LANE_TILE), jnp.float32)
        for slot in range(slots):
            shifted[slot, :, last] = jnp.zeros((rows, LANE_TILE), jnp.bfloat16)
    sums = [None] * (vols * coils)
    for slot in range(slots):
        if whole_classes:
            column = rows_of[slot]
            half = phase_ref.shape[1] // 2
            cosine = phase_ref[:rows, column : column + 1]
            sine = phase_ref[:rows, half + column : half + column + 1]
        else:
            cosine, sine = phase_ref[:rows, :1], phase_ref[:rows, 1:]
        for vol in range(vols):
            image_re = image[vol, slot, 0].astype(jnp.float32)
            image_im = image[vol, slot, 1].astype(jnp.float32)
            for coil in range(coils):
                place = vol * coils + coil
                base = place * 2 * length
                map_re = coil_map[coil, slot, 0].astype(jnp.float32)
                map_im = coil_map[coil, slot, 1].astype(jnp.float32)
                coil_re = (map_re * image_re - map_im * image_im).astype(jnp.bfloat16)
                coil_im = (map_re * image_im + map_im * image_re).astype(jnp.bfloat16)
                partly = dot(left_ref[0, : 2 * rows], coil_re) + dot(
                    left_ref[1, : 2 * rows], coil_im
                )
                part_re, part_im = partly[:rows], partly[rows:]
                shift_re = part_re * cosine - part_im * sine
                shift_im = part_re * sine + part_im * cosine
                shifted[slot, :, base : base + length] = shift_re.astype(jnp.bfloat16)
                shifted[slot, :, base + length : base + 2 * length] = shift_im.astype(
                    jnp.bfloat16
                )
                if slot > 0:
                    shift_re, shift_im = sums[place][0] + shift_re, sums[place][1] + shift_im
                sums[place] = (shift_re, shift_im)
        if slot == 0:
            order_copy.wait()
            owner = order[group] == lax.axis_index("slc")

            @pl.when(owner)
            def _():
                start_all(owner_copies)

    gram_copy.wait()
    for place, (sum_re, sum_im) in enumerate(sums):
        mixed = dot(sum_re.astype(jnp.bfloat16), gram[0]) + dot(
            sum_im.astype(jnp.bfloat16), gram[1]
        )
        if not whole_classes:
            mixed = jnp.where(place_ref[0] > 0, mixed, 0.0)
        total[:, place * 2 * length : (place + 1) * 2 * length] = mixed

    @pl.when(owner)
    def _():
        for copy in owner_copies:
            copy.wait()
        for vol in range(vols):
            for coil in range(coils):
                place = vol * coils + coil
                measured = dot(kspace_ref[vol, 0, coil, 0], adjoint[0]) + dot(
                    kspace_ref[vol, 0, coil, 1], adjoint[1]
                )
                total[:length, place * 2 * length : (place + 1) * 2 * length] -= measured

    part = rows // PARTS
    for index, out_ref in enumerate(out_refs):
        out_ref[...] = total[index * part : (index + 1) * part, :].astype(jnp.bfloat16)
    for copy in next_copies:
        copy.wait()


def gradient_kernel(index, factor, on_line, *refs):
    term_refs, shifted_ref, out_ref = refs[:-2], refs[-2], refs[-1]
    slots, rows, lanes = shifted_ref.shape
    part = rows // PARTS
    terms = [ref[...].astype(jnp.float32) for ref in term_refs]
    residual = terms[0]
    if on_line:
        near, across, rest = terms[1:]
        residual += jnp.where(at_line_end(), rest, near + across)
    for slot in range(slots):
        product = residual * shifted_ref[slot, index * part : (index + 1) * part, :].astype(
            jnp.float32
        )
        tiles = [product[:, at : at + LANE_TILE] for at in range(0, lanes, LANE_TILE)]
        folded = functools.reduce(lambda a, b: a + b, tiles)
        out_ref[slot : slot + 1, :] = factor * jnp.sum(folded.T, axis=0, keepdims=True)


def after(value, *earlier):
    return lax.optimization_barrier((value, *earlier))[0]


def sum_over_replicas(value):
    axes = ("coil", "vol")
    if any(lax.axis_size(axis) != 2 for axis in axes):
        return lax.psum(value, axes)
    swapped = [
        lax.ppermute(value, axes, [(index, index ^ mask) for index in range(4)])
        for mask in (1, 2, 3)
    ]
    return (value + swapped[0]) + (swapped[1] + swapped[2])


def line_of_four(encode, gradient, groups, ends):
    cores = lax.axis_size("vol")
    count = groups * PARTS
    outer_pairs = [(0, 1), (1, 0), (2, 3), (3, 2)]
    inner_pairs = [
        (source * cores + core, target * cores + (core ^ 1 if swap and cores % 2 == 0 else core))
        for source, target, swap in ((0, 0, True), (1, 2, False), (2, 1, False), (3, 3, True))
        for core in range(cores)
    ]

    def outer(value):
        return lax.ppermute(value, "slc", outer_pairs)

    def inner(value):
        return lax.ppermute(value, ("slc", "vol"), inner_pairs)

    own = [*encode(0)]
    near, across, gradients, encoded = [outer(own[0])], [], [], 1

    def encode_more(wanted, *earlier):
        nonlocal encoded
        while len(own) < min(wanted, count):
            own.extend(encode(encoded, *earlier))
            encoded += 1

    def gradient_of(piece, *earlier):
        terms = (own[piece], near[piece], across[piece], near[piece + 4])
        gradients.append(gradient((after(terms[0], *earlier), *terms[1:]), piece))

    encode_more(3)
    near.append(outer(after(own[1], own[2])))
    encode_more(5)
    latest = own[4]
    for step in range(count):
        half = own[step] + after(near[step], latest)
        across.append(inner(half))
        payload = own[step + 2] if step + 2 < count else None
        if step >= 2:
            others = own[step - 2] + after(across[step - 2], half)
            payload = others if payload is None else jnp.where(ends > 0, payload, others)
        else:
            payload = after(payload, near[step])
        near.append(outer(payload))
        latest = payload
        if len(own) < min(step + 7, count):
            encode_more(step + 7, payload)
            latest = own[-1]
        if step >= 4:
            gradient_of(step - 4, payload)
    for piece in range(count - 2, count):
        latest = own[piece] + after(across[piece], latest, near[count])
        near.append(outer(latest))
    for piece in range(count - 4, count):
        gradient_of(piece, latest)
    return gradients


def body(images, coil_maps, kspace, shift_index, phase_offset, group_order):
    vols, per_device, _, _, length = images.shape
    coils = coil_maps.shape[0]
    groups = lax.axis_size("slc")
    rows = round_up(length, ROW_TILE * PARTS)
    places = vols * coils
    lanes = round_up(places * 2 * length, LANE_TILE)
    whole_classes = per_device % groups == 0
    slots = max(1, per_device // groups)
    tables = dft_matrices(length, rows)
    factor = 1.0 / (coils * lax.axis_size("coil") * vols * lax.axis_size("vol"))
    first = (lax.axis_index("slc") * per_device) % groups
    on_line = whole_classes and groups == 4
    in_vmem = pl.BlockSpec(memory_space=pltpu.VMEM)
    in_smem = pl.BlockSpec(memory_space=pltpu.SMEM)
    in_place = pl.BlockSpec(memory_space=pl.ANY)

    def in_hbm(array):
        return pltpu.with_memory_space_constraint(jnp.asarray(array), pltpu.HBM)

    def rows_of_class(group):
        return [slot * groups + group for slot in range(slots)] if whole_classes else None

    def place_of(group):
        if whole_classes:
            return ()
        held = [(group + step - first, per_device) for step in range(2)]
        inside = [(within >= 0) & (within < size) for within, size in held]
        rows_held = [jnp.where(yes, held[i][0], 0) for i, yes in enumerate(inside)]
        return (jnp.stack([inside[0], rows_held[0], rows_held[1]]).astype(jnp.int32),)

    left, gram, adjoint = (in_hbm(table) for table in tables)
    lying = [in_hbm(jnp.swapaxes(array, -3, -2)) for array in (images, coil_maps)]
    order = in_hbm(group_order)
    raw_shapes = [
        jax.ShapeDtypeStruct((count, slots, length, 2, length), jnp.bfloat16)
        for count in (vols, coils)
    ]
    scalar_specs = [] if whole_classes else [in_smem]
    padded_rows = round_up(rows, LANE_TILE)
    slice_semaphores = pltpu.SemaphoreType.DMA((slots, vols + coils))
    *raw, left, phases, ends = pl.pallas_call(
        functools.partial(fetch_kernel, rows_of_class(0)),
        in_specs=scalar_specs + [in_place] * 5,
        out_specs=[in_vmem] * 5,
        out_shape=raw_shapes
        + [
            jax.ShapeDtypeStruct(left.shape, left.dtype),
            jax.ShapeDtypeStruct((padded_rows, 2 * per_device), jnp.float32),
            jax.ShapeDtypeStruct((1, lanes), jnp.float32),
        ],
        scratch_shapes=[
            pltpu.SMEM((per_device,), jnp.int32),
            pltpu.VMEM((per_device, length), jnp.float32),
            pltpu.VMEM((per_device, padded_rows), jnp.float32),
            slice_semaphores,
            pltpu.SemaphoreType.DMA((3,)),
        ],
        compiler_params=pltpu.CompilerParams(vmem_limit_bytes=VMEM_BYTES),
        name="fetch",
    )(*place_of(0), in_hbm(shift_index), in_hbm(phase_offset), *lying, left)

    shifted = []

    def encode(group, *earlier):
        image, coil_map = (jnp.swapaxes(array, -3, -2) for array in raw)
        has_next = group + 1 < groups
        place, group_phases = place_of(group), phases
        if not whole_classes:
            group_phases = jnp.take(
                phases, jnp.stack([place[0][1], place[0][1] + per_device]), axis=1
            )
        if earlier:
            image = after(image, *earlier)
        outputs = pl.pallas_call(
            functools.partial(
                encode_kernel,
                slots,
                group,
                rows_of_class(group),
                (rows_of_class(group + 1) or [0]) if has_next else None,
            ),
            in_specs=scalar_specs + [in_vmem] * 5 + [in_place] * 5,
            out_specs=[in_vmem] * (1 + PARTS + 2 * has_next),
            out_shape=[jax.ShapeDtypeStruct((slots, rows, lanes), jnp.bfloat16)]
            + [jax.ShapeDtypeStruct((rows // PARTS, lanes), jnp.bfloat16)] * PARTS
            + raw_shapes * has_next,
            scratch_shapes=[
                pltpu.VMEM((rows, lanes), jnp.float32),
                pltpu.VMEM(gram.shape, jnp.bfloat16),
                pltpu.VMEM(adjoint.shape, jnp.bfloat16),
                pltpu.SMEM((groups,), jnp.int32),
                slice_semaphores,
                pltpu.SemaphoreType.DMA((3,)),
            ],
            compiler_params=pltpu.CompilerParams(vmem_limit_bytes=VMEM_BYTES),
            cost_estimate=pl.CostEstimate(
                flops=places * (slots + 1) * 16 * length**3,
                bytes_accessed=6_000_000,
                transcendentals=0,
            ),
            name="encode",
        )(
            *place,
            group_phases,
            image,
            coil_map,
            left,
            kspace,
            order,
            gram,
            adjoint,
            *lying,
        )
        raw[:] = outputs[1 + PARTS :]
        shifted.append(outputs[0])
        return outputs[1 : 1 + PARTS]

    def gradient(terms, piece):
        group, index = divmod(piece, PARTS)
        return pl.pallas_call(
            functools.partial(gradient_kernel, index, factor, on_line),
            out_shape=jax.ShapeDtypeStruct((slots, rows // PARTS), jnp.float32),
            compiler_params=pltpu.CompilerParams(vmem_limit_bytes=VMEM_BYTES),
            cost_estimate=pl.CostEstimate(
                flops=places * slots * 4 * length**2, bytes_accessed=1_500_000, transcendentals=0
            ),
            name="gradient",
        )(*terms, shifted[group])

    if on_line:
        gradients = line_of_four(encode, gradient, groups, ends)
    else:
        reduced = lax.psum([piece for group in range(groups) for piece in encode(group)], "slc")
        gradients = [gradient((piece,), index) for index, piece in enumerate(reduced)]
    by_class = jnp.stack(
        [
            jnp.concatenate(gradients[group * PARTS : (group + 1) * PARTS], axis=1)
            for group in range(groups)
        ],
        axis=1,
    )[:, :, :length]
    if whole_classes:
        local = by_class.reshape(per_device, length)
    else:
        local = lax.dynamic_slice_in_dim(by_class[0], first, per_device, axis=0)
    return sum_over_replicas(local)


def solution(mesh):
    placed = (
        P(("grp", "vol"), "slc", None, None, None),
        P(("grp", "coil"), "slc", None, None, None),
        P(("grp", "vol"), "slc", "coil", None, None, None),
        P("slc"),
        P("slc", None),
        P(),
    )
    return jax.shard_map(
        body, mesh=mesh, in_specs=placed, out_specs=P(("grp", "slc"), None), check_vma=False
    )
```

```python
import functools
import math

import jax
import jax.numpy as jnp
import ml_dtypes
import numpy as np
from jax import lax
from jax.experimental import pallas as pl
from jax.experimental.pallas import tpu as pltpu
from jax.sharding import PartitionSpec as P

MB = 8
ROW_TILE = 16
LANE_TILE = 128
PARTS = 2
VMEM_BYTES = 24 * 1024 * 1024


def round_up(value, multiple):
    return -(-value // multiple) * multiple


def fourier_tables(length):
    positions = np.arange(length, dtype=np.int32)
    product = positions[:, None] * positions[None, :] % length
    radians = np.float32(2.0 * math.pi / length) * product.astype(np.float32)
    factor = np.float32(1.0 / math.sqrt(length))
    return (
        (np.cos(radians) * factor).astype(ml_dtypes.bfloat16),
        (-np.sin(radians) * factor).astype(ml_dtypes.bfloat16),
    )


def dft_matrices(length, rows):
    cos_table, sin_table = fourier_tables(length)
    cosine, sine = cos_table.astype(np.float64), sin_table.astype(np.float64)
    padded = ((0, rows - length), (0, 0))
    real, imaginary = np.pad(cosine, padded), np.pad(sine, padded)
    spare = np.zeros((8, length), np.float64)

    def by_piece(upper, lower):
        pairs = zip(np.split(upper, PARTS), np.split(lower, PARTS))
        return np.concatenate([block for pair in pairs for block in pair] + [spare])

    left_re, left_im = by_piece(real, imaginary), by_piece(-imaginary, real)
    gram_re = cosine.T @ cosine + sine.T @ sine
    gram_im = sine.T @ cosine - cosine.T @ sine
    gram = np.stack(
        [np.concatenate([gram_im, -gram_re], 1), np.concatenate([gram_re, gram_im], 1)]
    )
    adjoint = np.stack(
        [np.concatenate([-sine, -cosine], 1), np.concatenate([cosine, -sine], 1)]
    )
    left = np.stack([left_re, left_im])
    return tuple(part.astype(ml_dtypes.bfloat16) for part in (left, gram, adjoint))


def dot(left, right):
    return jnp.dot(left, right, preferred_element_type=jnp.float32)


def at_line_end():
    position = lax.axis_index("slc")
    return (position == 0) | (position == lax.axis_size("slc") - 1)


def start_all(copies):
    for copy in copies:
        copy.start()


def slice_copies(image_ref, map_ref, image_out, map_out, arrived, rows_of):
    vols, coils = image_ref.shape[0], map_ref.shape[0]
    return [
        pltpu.make_async_copy(
            image_ref.at[vol, row], image_out.at[vol, slot], arrived.at[slot, vol]
        )
        for slot, row in enumerate(rows_of)
        for vol in range(vols)
    ] + [
        pltpu.make_async_copy(
            map_ref.at[coil, row], map_out.at[coil, slot], arrived.at[slot, vols + coil]
        )
        for slot, row in enumerate(rows_of)
        for coil in range(coils)
    ]


def fetch_kernel(rows_of, *refs):
    if rows_of is None:
        rows_of, refs = [refs[0][1]], refs[1:]
    shift_ref, offset_ref, image_ref, map_ref, left_ref = refs[:5]
    image_out, map_out, left_out, phase_out, ends_out = refs[5:10]
    shift, offset, angle, arrived, small = refs[10:]
    copies = slice_copies(image_ref, map_ref, image_out, map_out, arrived, rows_of)
    copies.append(pltpu.make_async_copy(left_ref, left_out, small.at[0]))
    early = [
        pltpu.make_async_copy(shift_ref, shift, small.at[1]),
        pltpu.make_async_copy(offset_ref, offset, small.at[2]),
    ]
    start_all(early)
    start_all(copies)
    ends_out[...] = jnp.where(at_line_end(), 1.0, 0.0) * jnp.ones_like(ends_out)
    for copy in early:
        copy.wait()
    per_device, length = offset.shape
    lines = lax.broadcasted_iota(jnp.int32, (1, length), 1) - length // 2
    angle[...] = jnp.zeros_like(angle)
    for row in range(per_device):
        turns = (shift[row] * lines) & (MB - 1)
        angle[row : row + 1, :length] = (
            2.0 * math.pi / MB * turns.astype(jnp.float32) + offset[row : row + 1, :]
        )
    phase_out[:, :per_device] = jnp.cos(angle[...]).T
    phase_out[:, per_device:] = jnp.sin(angle[...]).T
    for copy in copies:
        copy.wait()


def encode_kernel(slots, group, pieces, rows_of, next_rows, *refs):
    whole_classes = rows_of is not None
    if not whole_classes:
        place_ref, refs = refs[0], refs[1:]
        next_rows = next_rows and [place_ref[2]]
    phase_ref, image, coil_map, left_ref, kspace_ref = refs[:5]
    order_ref, gram_ref, adjoint_ref, image_ref, map_ref = refs[5:10]
    refs = refs[10:]
    shifted, refs = refs[0], refs[1:]
    out_refs, refs = refs[: len(pieces)], refs[len(pieces) :]
    if next_rows:
        next_image, next_map, refs = refs[0], refs[1], refs[2:]
    total, gram, adjoint, order, arrived, small = refs
    vols, coils, length = image.shape[0], coil_map.shape[0], image.shape[-1]
    _, rows, lanes = shifted.shape
    order_copy = pltpu.make_async_copy(order_ref, order, small.at[0])
    gram_copy = pltpu.make_async_copy(gram_ref, gram, small.at[1])
    owner_copies = [pltpu.make_async_copy(adjoint_ref, adjoint, small.at[2])]
    next_copies = []
    if next_rows:
        next_copies = slice_copies(image_ref, map_ref, next_image, next_map, arrived, next_rows)
    start_all([order_copy, gram_copy, *next_copies])

    if lanes > vols * coils * 2 * length:
        last = slice(lanes - LANE_TILE, lanes)
        total[:, last] = jnp.zeros((rows, LANE_TILE), jnp.float32)
        for slot in range(slots):
            shifted[slot, :, last] = jnp.zeros((rows, LANE_TILE), jnp.bfloat16)
    part = rows // len(pieces)
    start, stop = pieces[0] * part, min(length, (pieces[-1] + 1) * part)
    span = slice(start, start + rows)
    left_rows = slice(2 * start, 2 * (start + rows))

    def joined(partly, kind):
        blocks = [partly[(2 * at + kind) * part :][:part] for at in range(len(pieces))]
        return jnp.concatenate(blocks, axis=0)

    sums = [None] * (vols * coils)
    for slot in range(slots):
        if whole_classes:
            column = rows_of[slot]
            half = phase_ref.shape[1] // 2
            cosine = phase_ref[span, column : column + 1]
            sine = phase_ref[span, half + column : half + column + 1]
        else:
            cosine, sine = phase_ref[span, :1], phase_ref[span, 1:]
        for vol in range(vols):
            image_re = image[vol, slot, 0].astype(jnp.float32)
            image_im = image[vol, slot, 1].astype(jnp.float32)
            for coil in range(coils):
                place = vol * coils + coil
                base = place * 2 * length
                map_re = coil_map[coil, slot, 0].astype(jnp.float32)
                map_im = coil_map[coil, slot, 1].astype(jnp.float32)
                coil_re = (map_re * image_re - map_im * image_im).astype(jnp.bfloat16)
                coil_im = (map_re * image_im + map_im * image_re).astype(jnp.bfloat16)
                partly = dot(left_ref[0, left_rows], coil_re) + dot(
                    left_ref[1, left_rows], coil_im
                )
                part_re, part_im = joined(partly, 0), joined(partly, 1)
                shift_re = part_re * cosine - part_im * sine
                shift_im = part_re * sine + part_im * cosine
                shifted[slot, :, base : base + length] = shift_re.astype(jnp.bfloat16)
                shifted[slot, :, base + length : base + 2 * length] = shift_im.astype(
                    jnp.bfloat16
                )
                if slot > 0:
                    shift_re, shift_im = sums[place][0] + shift_re, sums[place][1] + shift_im
                sums[place] = (shift_re, shift_im)
        if slot == 0:
            order_copy.wait()
            owner = order[group] == lax.axis_index("slc")

            @pl.when(owner)
            def _():
                start_all(owner_copies)

    gram_copy.wait()
    for place, (sum_re, sum_im) in enumerate(sums):
        mixed = dot(sum_re.astype(jnp.bfloat16), gram[0]) + dot(
            sum_im.astype(jnp.bfloat16), gram[1]
        )
        if not whole_classes:
            mixed = jnp.where(place_ref[0] > 0, mixed, 0.0)
        total[:, place * 2 * length : (place + 1) * 2 * length] = mixed

    @pl.when(owner)
    def _():
        for copy in owner_copies:
            copy.wait()
        for vol in range(vols):
            for coil in range(coils):
                place = vol * coils + coil
                measured = dot(kspace_ref[vol, 0, coil, 0][start:stop], adjoint[0]) + dot(
                    kspace_ref[vol, 0, coil, 1][start:stop], adjoint[1]
                )
                total[: stop - start, place * 2 * length : (place + 1) * 2 * length] -= measured

    for index, out_ref in enumerate(out_refs):
        out_ref[...] = total[index * part : (index + 1) * part, :].astype(jnp.bfloat16)
    for copy in next_copies:
        copy.wait()


def gradient_kernel(index, factor, on_line, *refs):
    term_refs, shifted_ref, out_ref = refs[:-2], refs[-2], refs[-1]
    slots, _, lanes = shifted_ref.shape
    part = out_ref.shape[1]
    terms = [ref[...].astype(jnp.float32) for ref in term_refs]
    residual = terms[0]
    if on_line:
        near, across, rest = terms[1:]
        residual += jnp.where(at_line_end(), rest, near + across)
    for slot in range(slots):
        product = residual * shifted_ref[slot, index * part : (index + 1) * part, :].astype(
            jnp.float32
        )
        tiles = [product[:, at : at + LANE_TILE] for at in range(0, lanes, LANE_TILE)]
        folded = functools.reduce(lambda a, b: a + b, tiles)
        out_ref[slot : slot + 1, :] = factor * jnp.sum(folded.T, axis=0, keepdims=True)


def after(value, *earlier):
    return lax.optimization_barrier((value, *earlier))[0]


def sum_over_replicas(value):
    axes = ("coil", "vol")
    if any(lax.axis_size(axis) != 2 for axis in axes):
        return lax.psum(value, axes)
    swapped = [
        lax.ppermute(value, axes, [(index, index ^ mask) for index in range(4)])
        for mask in (1, 2, 3)
    ]
    return (value + swapped[0]) + (swapped[1] + swapped[2])


def line_of_four(encode, gradient, groups, ends):
    cores = lax.axis_size("vol")
    count = groups * PARTS
    outer_pairs = [(0, 1), (1, 0), (2, 3), (3, 2)]
    inner_pairs = [
        (source * cores + core, target * cores + (core ^ 1 if swap and cores % 2 == 0 else core))
        for source, target, swap in ((0, 0, True), (1, 2, False), (2, 1, False), (3, 3, True))
        for core in range(cores)
    ]

    def outer(value):
        return lax.ppermute(value, "slc", outer_pairs)

    def inner(value):
        return lax.ppermute(value, ("slc", "vol"), inner_pairs)

    own = [*encode(0, pieces=(0,))]
    near, across, gradients, encoded = [outer(own[0])], [], [], 1
    own.extend(encode(0, pieces=tuple(range(1, PARTS))))

    def encode_more(wanted, *earlier):
        nonlocal encoded
        while len(own) < min(wanted, count):
            own.extend(encode(encoded, *earlier))
            encoded += 1

    def gradient_of(piece, *earlier):
        terms = (own[piece], near[piece], across[piece], near[piece + 4])
        gradients.append(gradient((after(terms[0], *earlier), *terms[1:]), piece))

    encode_more(3)
    near.append(outer(after(own[1], own[2])))
    encode_more(5)
    latest = own[4]
    for step in range(count):
        half = own[step] + after(near[step], latest)
        across.append(inner(half))
        payload = own[step + 2] if step + 2 < count else None
        if step >= 2:
            others = own[step - 2] + after(across[step - 2], half)
            payload = others if payload is None else jnp.where(ends > 0, payload, others)
        else:
            payload = after(payload, near[step])
        near.append(outer(payload))
        latest = payload
        if len(own) < min(step + 7, count):
            encode_more(step + 7, payload)
            latest = own[-1]
        if step >= 4:
            gradient_of(step - 4, payload)
    for piece in range(count - 2, count):
        latest = own[piece] + after(across[piece], latest, near[count])
        near.append(outer(latest))
    for piece in range(count - 4, count):
        gradient_of(piece, latest)
    return gradients


def body(images, coil_maps, kspace, shift_index, phase_offset, group_order):
    vols, per_device, _, _, length = images.shape
    coils = coil_maps.shape[0]
    groups = lax.axis_size("slc")
    rows = round_up(length, ROW_TILE * PARTS)
    places = vols * coils
    lanes = round_up(places * 2 * length, LANE_TILE)
    whole_classes = per_device % groups == 0
    slots = max(1, per_device // groups)
    tables = dft_matrices(length, rows)
    factor = 1.0 / (coils * lax.axis_size("coil") * vols * lax.axis_size("vol"))
    first = (lax.axis_index("slc") * per_device) % groups
    on_line = whole_classes and groups == 4
    in_vmem = pl.BlockSpec(memory_space=pltpu.VMEM)
    in_smem = pl.BlockSpec(memory_space=pltpu.SMEM)
    in_place = pl.BlockSpec(memory_space=pl.ANY)

    def in_hbm(array):
        return pltpu.with_memory_space_constraint(jnp.asarray(array), pltpu.HBM)

    def rows_of_class(group):
        return [slot * groups + group for slot in range(slots)] if whole_classes else None

    def place_of(group):
        if whole_classes:
            return ()
        held = [(group + step - first, per_device) for step in range(2)]
        inside = [(within >= 0) & (within < size) for within, size in held]
        rows_held = [jnp.where(yes, held[i][0], 0) for i, yes in enumerate(inside)]
        return (jnp.stack([inside[0], rows_held[0], rows_held[1]]).astype(jnp.int32),)

    left, gram, adjoint = (in_hbm(table) for table in tables)
    lying = [in_hbm(jnp.swapaxes(array, -3, -2)) for array in (images, coil_maps)]
    order = in_hbm(group_order)
    raw_shapes = [
        jax.ShapeDtypeStruct((count, slots, length, 2, length), jnp.bfloat16)
        for count in (vols, coils)
    ]
    scalar_specs = [] if whole_classes else [in_smem]
    padded_rows = round_up(rows, LANE_TILE)
    slice_semaphores = pltpu.SemaphoreType.DMA((slots, vols + coils))
    *raw, left, phases, ends = pl.pallas_call(
        functools.partial(fetch_kernel, rows_of_class(0)),
        in_specs=scalar_specs + [in_place] * 5,
        out_specs=[in_vmem] * 5,
        out_shape=raw_shapes
        + [
            jax.ShapeDtypeStruct(left.shape, left.dtype),
            jax.ShapeDtypeStruct((padded_rows, 2 * per_device), jnp.float32),
            jax.ShapeDtypeStruct((1, lanes), jnp.float32),
        ],
        scratch_shapes=[
            pltpu.SMEM((per_device,), jnp.int32),
            pltpu.VMEM((per_device, length), jnp.float32),
            pltpu.VMEM((per_device, padded_rows), jnp.float32),
            slice_semaphores,
            pltpu.SemaphoreType.DMA((3,)),
        ],
        compiler_params=pltpu.CompilerParams(vmem_limit_bytes=VMEM_BYTES),
        name="fetch",
    )(*place_of(0), in_hbm(shift_index), in_hbm(phase_offset), *lying, left)

    shifted = []

    def encode(group, *earlier, pieces=tuple(range(PARTS))):
        image, coil_map = (jnp.swapaxes(array, -3, -2) for array in raw)
        has_next = group + 1 < groups and pieces[-1] == PARTS - 1
        held_rows = rows // PARTS * len(pieces)
        place, group_phases = place_of(group), phases
        if not whole_classes:
            group_phases = jnp.take(
                phases, jnp.stack([place[0][1], place[0][1] + per_device]), axis=1
            )
        if earlier:
            image = after(image, *earlier)
        outputs = pl.pallas_call(
            functools.partial(
                encode_kernel,
                slots,
                group,
                pieces,
                rows_of_class(group),
                (rows_of_class(group + 1) or [0]) if has_next else None,
            ),
            in_specs=scalar_specs + [in_vmem] * 5 + [in_place] * 5,
            out_specs=[in_vmem] * (1 + len(pieces) + 2 * has_next),
            out_shape=[jax.ShapeDtypeStruct((slots, held_rows, lanes), jnp.bfloat16)]
            + [jax.ShapeDtypeStruct((rows // PARTS, lanes), jnp.bfloat16)] * len(pieces)
            + raw_shapes * has_next,
            scratch_shapes=[
                pltpu.VMEM((held_rows, lanes), jnp.float32),
                pltpu.VMEM(gram.shape, jnp.bfloat16),
                pltpu.VMEM(adjoint.shape, jnp.bfloat16),
                pltpu.SMEM((groups,), jnp.int32),
                slice_semaphores,
                pltpu.SemaphoreType.DMA((3,)),
            ],
            compiler_params=pltpu.CompilerParams(vmem_limit_bytes=VMEM_BYTES),
            cost_estimate=pl.CostEstimate(
                flops=places * (slots + 1) * 16 * length**3,
                bytes_accessed=6_000_000,
                transcendentals=0,
            ),
            name="encode",
        )(
            *place,
            group_phases,
            image,
            coil_map,
            left,
            kspace,
            order,
            gram,
            adjoint,
            *lying,
        )
        if has_next:
            raw[:] = outputs[1 + len(pieces) :]
        shifted.extend((outputs[0], index) for index in range(len(pieces)))
        return outputs[1 : 1 + len(pieces)]

    def gradient(terms, piece):
        held, index = shifted[piece]
        return pl.pallas_call(
            functools.partial(gradient_kernel, index, factor, on_line),
            out_shape=jax.ShapeDtypeStruct((slots, rows // PARTS), jnp.float32),
            compiler_params=pltpu.CompilerParams(vmem_limit_bytes=VMEM_BYTES),
            cost_estimate=pl.CostEstimate(
                flops=places * slots * 4 * length**2, bytes_accessed=1_500_000, transcendentals=0
            ),
            name="gradient",
        )(*terms, held)

    if on_line:
        gradients = line_of_four(encode, gradient, groups, ends)
    else:
        reduced = lax.psum([piece for group in range(groups) for piece in encode(group)], "slc")
        gradients = [gradient((piece,), index) for index, piece in enumerate(reduced)]
    by_class = jnp.stack(
        [
            jnp.concatenate(gradients[group * PARTS : (group + 1) * PARTS], axis=1)
            for group in range(groups)
        ],
        axis=1,
    )[:, :, :length]
    if whole_classes:
        local = by_class.reshape(per_device, length)
    else:
        local = lax.dynamic_slice_in_dim(by_class[0], first, per_device, axis=0)
    return sum_over_replicas(local)


def solution(mesh):
    placed = (
        P(("grp", "vol"), "slc", None, None, None),
        P(("grp", "coil"), "slc", None, None, None),
        P(("grp", "vol"), "slc", "coil", None, None, None),
        P("slc"),
        P("slc", None),
        P(),
    )
    return jax.shard_map(
        body, mesh=mesh, in_specs=placed, out_specs=P(("grp", "slc"), None), check_vma=False
    )
```

```python
import functools
import math

import jax
import jax.numpy as jnp
import ml_dtypes
import numpy as np
from jax import lax
from jax.experimental import pallas as pl
from jax.experimental.pallas import tpu as pltpu
from jax.sharding import PartitionSpec as P

MB = 8
ROW_TILE = 16
LANE_TILE = 128
PARTS = 2
VMEM_BYTES = 24 * 1024 * 1024


def round_up(value, multiple):
    return -(-value // multiple) * multiple


def fourier_tables(length):
    positions = np.arange(length, dtype=np.int32)
    product = positions[:, None] * positions[None, :] % length
    radians = np.float32(2.0 * math.pi / length) * product.astype(np.float32)
    factor = np.float32(1.0 / math.sqrt(length))
    return (
        (np.cos(radians) * factor).astype(ml_dtypes.bfloat16),
        (-np.sin(radians) * factor).astype(ml_dtypes.bfloat16),
    )


def dft_matrices(length, rows):
    cos_table, sin_table = fourier_tables(length)
    cosine, sine = cos_table.astype(np.float64), sin_table.astype(np.float64)
    left_re = np.zeros((2 * rows + 8, length), np.float64)
    left_im = np.zeros((2 * rows + 8, length), np.float64)
    left_re[:length], left_re[rows : rows + length] = cosine, sine
    left_im[:length], left_im[rows : rows + length] = -sine, cosine
    gram_re = cosine.T @ cosine + sine.T @ sine
    gram_im = sine.T @ cosine - cosine.T @ sine
    gram = np.stack(
        [np.concatenate([gram_im, -gram_re], 1), np.concatenate([gram_re, gram_im], 1)]
    )
    adjoint = np.stack(
        [np.concatenate([-sine, -cosine], 1), np.concatenate([cosine, -sine], 1)]
    )
    left = np.stack([left_re, left_im])
    return tuple(part.astype(ml_dtypes.bfloat16) for part in (left, gram, adjoint))


def dot(left, right):
    return jnp.dot(left, right, preferred_element_type=jnp.float32)


def at_line_end():
    position = lax.axis_index("slc")
    return (position == 0) | (position == lax.axis_size("slc") - 1)


def start_all(copies):
    for copy in copies:
        copy.start()


def slice_copies(image_ref, map_ref, image_out, map_out, arrived, rows_of):
    vols, coils = image_ref.shape[0], map_ref.shape[0]
    return [
        pltpu.make_async_copy(
            image_ref.at[vol, row], image_out.at[vol, slot], arrived.at[slot, vol]
        )
        for slot, row in enumerate(rows_of)
        for vol in range(vols)
    ] + [
        pltpu.make_async_copy(
            map_ref.at[coil, row], map_out.at[coil, slot], arrived.at[slot, vols + coil]
        )
        for slot, row in enumerate(rows_of)
        for coil in range(coils)
    ]


def fetch_kernel(rows_of, *refs):
    if rows_of is None:
        rows_of, refs = [refs[0][1]], refs[1:]
    shift_ref, offset_ref, image_ref, map_ref, left_ref = refs[:5]
    image_out, map_out, left_out, phase_out, ends_out = refs[5:10]
    shift, offset, angle, arrived, small = refs[10:]
    copies = slice_copies(image_ref, map_ref, image_out, map_out, arrived, rows_of)
    copies.append(pltpu.make_async_copy(left_ref, left_out, small.at[0]))
    early = [
        pltpu.make_async_copy(shift_ref, shift, small.at[1]),
        pltpu.make_async_copy(offset_ref, offset, small.at[2]),
    ]
    start_all(early)
    start_all(copies)
    ends_out[...] = jnp.where(at_line_end(), 1.0, 0.0) * jnp.ones_like(ends_out)
    for copy in early:
        copy.wait()
    per_device, length = offset.shape
    lines = lax.broadcasted_iota(jnp.int32, (1, length), 1) - length // 2
    angle[...] = jnp.zeros_like(angle)
    for row in range(per_device):
        turns = (shift[row] * lines) & (MB - 1)
        angle[row : row + 1, :length] = (
            2.0 * math.pi / MB * turns.astype(jnp.float32) + offset[row : row + 1, :]
        )
    phase_out[:, :per_device] = jnp.cos(angle[...]).T
    phase_out[:, per_device:] = jnp.sin(angle[...]).T
    for copy in copies:
        copy.wait()


def encode_kernel(slots, group, rows_of, next_rows, *refs):
    whole_classes = rows_of is not None
    if not whole_classes:
        place_ref, refs = refs[0], refs[1:]
        next_rows = next_rows and [place_ref[2]]
    phase_ref, image, coil_map, left_ref, kspace_ref = refs[:5]
    order_ref, gram_ref, adjoint_ref, image_ref, map_ref = refs[5:10]
    refs = refs[10:]
    shifted, refs = refs[0], refs[1:]
    out_refs, refs = refs[:PARTS], refs[PARTS:]
    if next_rows:
        next_image, next_map, refs = refs[0], refs[1], refs[2:]
    total, gram, adjoint, order, arrived, small = refs
    vols, coils, length = image.shape[0], coil_map.shape[0], image.shape[-1]
    _, rows, lanes = shifted.shape
    order_copy = pltpu.make_async_copy(order_ref, order, small.at[0])
    gram_copy = pltpu.make_async_copy(gram_ref, gram, small.at[1])
    owner_copies = [pltpu.make_async_copy(adjoint_ref, adjoint, small.at[2])]
    next_copies = []
    if next_rows:
        next_copies = slice_copies(image_ref, map_ref, next_image, next_map, arrived, next_rows)
    start_all([order_copy, gram_copy, *next_copies])

    if lanes > vols * coils * 2 * length:
        last = slice(lanes - LANE_TILE, lanes)
        total[:, last] = jnp.zeros((rows, LANE_TILE), jnp.float32)
        for slot in range(slots):
            shifted[slot, :, last] = jnp.zeros((rows, LANE_TILE), jnp.bfloat16)
    sums = [None] * (vols * coils)
    for slot in range(slots):
        if whole_classes:
            column = rows_of[slot]
            half = phase_ref.shape[1] // 2
            cosine = phase_ref[:rows, column : column + 1]
            sine = phase_ref[:rows, half + column : half + column + 1]
        else:
            cosine, sine = phase_ref[:rows, :1], phase_ref[:rows, 1:]
        for vol in range(vols):
            image_re = image[vol, slot, 0].astype(jnp.float32)
            image_im = image[vol, slot, 1].astype(jnp.float32)
            for coil in range(coils):
                place = vol * coils + coil
                base = place * 2 * length
                map_re = coil_map[coil, slot, 0].astype(jnp.float32)
                map_im = coil_map[coil, slot, 1].astype(jnp.float32)
                coil_re = (map_re * image_re - map_im * image_im).astype(jnp.bfloat16)
                coil_im = (map_re * image_im + map_im * image_re).astype(jnp.bfloat16)
                partly = dot(left_ref[0, : 2 * rows], coil_re) + dot(
                    left_ref[1, : 2 * rows], coil_im
                )
                part_re, part_im = partly[:rows], partly[rows:]
                shift_re = part_re * cosine - part_im * sine
                shift_im = part_re * sine + part_im * cosine
                shifted[slot, :, base : base + length] = shift_re.astype(jnp.bfloat16)
                shifted[slot, :, base + length : base + 2 * length] = shift_im.astype(
                    jnp.bfloat16
                )
                if slot > 0:
                    shift_re, shift_im = sums[place][0] + shift_re, sums[place][1] + shift_im
                sums[place] = (shift_re, shift_im)
        if slot == 0:
            order_copy.wait()
            owner = order[group] == lax.axis_index("slc")

            @pl.when(owner)
            def _():
                start_all(owner_copies)

    gram_copy.wait()
    for place, (sum_re, sum_im) in enumerate(sums):
        mixed = dot(sum_re.astype(jnp.bfloat16), gram[0]) + dot(
            sum_im.astype(jnp.bfloat16), gram[1]
        )
        if not whole_classes:
            mixed = jnp.where(place_ref[0] > 0, mixed, 0.0)
        total[:, place * 2 * length : (place + 1) * 2 * length] = mixed

    @pl.when(owner)
    def _():
        for copy in owner_copies:
            copy.wait()
        for vol in range(vols):
            for coil in range(coils):
                place = vol * coils + coil
                measured = dot(kspace_ref[vol, 0, coil, 0], adjoint[0]) + dot(
                    kspace_ref[vol, 0, coil, 1], adjoint[1]
                )
                total[:length, place * 2 * length : (place + 1) * 2 * length] -= measured

    part = rows // PARTS
    for index, out_ref in enumerate(out_refs):
        out_ref[...] = total[index * part : (index + 1) * part, :].astype(jnp.bfloat16)
    for copy in next_copies:
        copy.wait()


def gradient_kernel(index, factor, on_line, *refs):
    term_refs, shifted_ref, out_ref = refs[:-2], refs[-2], refs[-1]
    slots, rows, lanes = shifted_ref.shape
    part = rows // PARTS
    terms = [ref[...].astype(jnp.float32) for ref in term_refs]
    residual = terms[0]
    if on_line:
        near, across, rest = terms[1:]
        residual += jnp.where(at_line_end(), rest, near + across)
    for slot in range(slots):
        product = residual * shifted_ref[slot, index * part : (index + 1) * part, :].astype(
            jnp.float32
        )
        tiles = [product[:, at : at + LANE_TILE] for at in range(0, lanes, LANE_TILE)]
        folded = functools.reduce(lambda a, b: a + b, tiles)
        out_ref[slot : slot + 1, :] = factor * jnp.sum(folded.T, axis=0, keepdims=True)


def after(value, *earlier):
    return lax.optimization_barrier((value, *earlier))[0]


def sum_over_replicas(value):
    axes = ("coil", "vol")
    if any(lax.axis_size(axis) != 2 for axis in axes):
        return lax.psum(value, axes)
    swapped = [
        lax.ppermute(value, axes, [(index, index ^ mask) for index in range(4)])
        for mask in (1, 2, 3)
    ]
    return (value + swapped[0]) + (swapped[1] + swapped[2])


def line_of_four(encode, gradient, groups, ends):
    cores = lax.axis_size("vol")
    count = groups * PARTS
    outer_pairs = [(0, 1), (1, 0), (2, 3), (3, 2)]
    inner_pairs = [
        (source * cores + core, target * cores + (core ^ 1 if swap and cores % 2 == 0 else core))
        for source, target, swap in ((0, 0, True), (1, 2, False), (2, 1, False), (3, 3, True))
        for core in range(cores)
    ]

    def outer(value):
        return lax.ppermute(value, "slc", outer_pairs)

    def inner(value):
        return lax.ppermute(value, ("slc", "vol"), inner_pairs)

    own = [*encode(0)]
    near, across, gradients, encoded = [outer(own[0])], [], [], 1

    def encode_more(wanted, *earlier):
        nonlocal encoded
        while len(own) < min(wanted, count):
            own.extend(encode(encoded, *earlier))
            encoded += 1

    def gradient_of(piece, *earlier):
        terms = (own[piece], near[piece], across[piece], near[piece + 4])
        gradients.append(gradient((after(terms[0], *earlier), *terms[1:]), piece))

    encode_more(3)
    near.append(outer(after(own[1], own[2])))
    encode_more(5)
    latest = own[4]
    for step in range(count):
        half = own[step] + after(near[step], latest)
        across.append(inner(half))
        payload = own[step + 2] if step + 2 < count else None
        if step >= 2:
            others = own[step - 2] + after(across[step - 2], half)
            payload = others if payload is None else jnp.where(ends > 0, payload, others)
        else:
            payload = after(payload, near[step])
        near.append(outer(payload))
        latest = payload
        if len(own) < min(step + 5, count):
            encode_more(step + 5, payload)
            latest = own[-1]
        if step >= 4:
            gradient_of(step - 4, payload)
    for piece in range(count - 2, count):
        latest = own[piece] + after(across[piece], latest, near[count])
        near.append(outer(latest))
    for piece in range(count - 4, count):
        gradient_of(piece, latest)
    return gradients


def body(images, coil_maps, kspace, shift_index, phase_offset, group_order):
    vols, per_device, _, _, length = images.shape
    coils = coil_maps.shape[0]
    groups = lax.axis_size("slc")
    rows = round_up(length, ROW_TILE * PARTS)
    places = vols * coils
    lanes = round_up(places * 2 * length, LANE_TILE)
    whole_classes = per_device % groups == 0
    slots = max(1, per_device // groups)
    tables = dft_matrices(length, rows)
    factor = 1.0 / (coils * lax.axis_size("coil") * vols * lax.axis_size("vol"))
    first = (lax.axis_index("slc") * per_device) % groups
    on_line = whole_classes and groups == 4
    in_vmem = pl.BlockSpec(memory_space=pltpu.VMEM)
    in_smem = pl.BlockSpec(memory_space=pltpu.SMEM)
    in_place = pl.BlockSpec(memory_space=pl.ANY)

    def in_hbm(array):
        return pltpu.with_memory_space_constraint(jnp.asarray(array), pltpu.HBM)

    def rows_of_class(group):
        return [slot * groups + group for slot in range(slots)] if whole_classes else None

    def place_of(group):
        if whole_classes:
            return ()
        held = [(group + step - first, per_device) for step in range(2)]
        inside = [(within >= 0) & (within < size) for within, size in held]
        rows_held = [jnp.where(yes, held[i][0], 0) for i, yes in enumerate(inside)]
        return (jnp.stack([inside[0], rows_held[0], rows_held[1]]).astype(jnp.int32),)

    left, gram, adjoint = (in_hbm(table) for table in tables)
    lying = [in_hbm(jnp.swapaxes(array, -3, -2)) for array in (images, coil_maps)]
    order = in_hbm(group_order)
    raw_shapes = [
        jax.ShapeDtypeStruct((count, slots, length, 2, length), jnp.bfloat16)
        for count in (vols, coils)
    ]
    scalar_specs = [] if whole_classes else [in_smem]
    padded_rows = round_up(rows, LANE_TILE)
    slice_semaphores = pltpu.SemaphoreType.DMA((slots, vols + coils))
    *raw, left, phases, ends = pl.pallas_call(
        functools.partial(fetch_kernel, rows_of_class(0)),
        in_specs=scalar_specs + [in_place] * 5,
        out_specs=[in_vmem] * 5,
        out_shape=raw_shapes
        + [
            jax.ShapeDtypeStruct(left.shape, left.dtype),
            jax.ShapeDtypeStruct((padded_rows, 2 * per_device), jnp.float32),
            jax.ShapeDtypeStruct((1, lanes), jnp.float32),
        ],
        scratch_shapes=[
            pltpu.SMEM((per_device,), jnp.int32),
            pltpu.VMEM((per_device, length), jnp.float32),
            pltpu.VMEM((per_device, padded_rows), jnp.float32),
            slice_semaphores,
            pltpu.SemaphoreType.DMA((3,)),
        ],
        compiler_params=pltpu.CompilerParams(vmem_limit_bytes=VMEM_BYTES),
        name="fetch",
    )(*place_of(0), in_hbm(shift_index), in_hbm(phase_offset), *lying, left)

    shifted = []

    def encode(group, *earlier):
        image, coil_map = (jnp.swapaxes(array, -3, -2) for array in raw)
        has_next = group + 1 < groups
        place, group_phases = place_of(group), phases
        if not whole_classes:
            group_phases = jnp.take(
                phases, jnp.stack([place[0][1], place[0][1] + per_device]), axis=1
            )
        if earlier:
            image = after(image, *earlier)
        outputs = pl.pallas_call(
            functools.partial(
                encode_kernel,
                slots,
                group,
                rows_of_class(group),
                (rows_of_class(group + 1) or [0]) if has_next else None,
            ),
            in_specs=scalar_specs + [in_vmem] * 5 + [in_place] * 5,
            out_specs=[in_vmem] * (1 + PARTS + 2 * has_next),
            out_shape=[jax.ShapeDtypeStruct((slots, rows, lanes), jnp.bfloat16)]
            + [jax.ShapeDtypeStruct((rows // PARTS, lanes), jnp.bfloat16)] * PARTS
            + raw_shapes * has_next,
            scratch_shapes=[
                pltpu.VMEM((rows, lanes), jnp.float32),
                pltpu.VMEM(gram.shape, jnp.bfloat16),
                pltpu.VMEM(adjoint.shape, jnp.bfloat16),
                pltpu.SMEM((groups,), jnp.int32),
                slice_semaphores,
                pltpu.SemaphoreType.DMA((3,)),
            ],
            compiler_params=pltpu.CompilerParams(vmem_limit_bytes=VMEM_BYTES),
            cost_estimate=pl.CostEstimate(
                flops=places * (slots + 1) * 16 * length**3,
                bytes_accessed=6_000_000,
                transcendentals=0,
            ),
            name="encode",
        )(
            *place,
            group_phases,
            image,
            coil_map,
            left,
            kspace,
            order,
            gram,
            adjoint,
            *lying,
        )
        raw[:] = outputs[1 + PARTS :]
        shifted.append(outputs[0])
        return outputs[1 : 1 + PARTS]

    def gradient(terms, piece):
        group, index = divmod(piece, PARTS)
        return pl.pallas_call(
            functools.partial(gradient_kernel, index, factor, on_line),
            out_shape=jax.ShapeDtypeStruct((slots, rows // PARTS), jnp.float32),
            compiler_params=pltpu.CompilerParams(vmem_limit_bytes=VMEM_BYTES),
            cost_estimate=pl.CostEstimate(
                flops=places * slots * 4 * length**2, bytes_accessed=1_500_000, transcendentals=0
            ),
            name="gradient",
        )(*terms, shifted[group])

    if on_line:
        gradients = line_of_four(encode, gradient, groups, ends)
    else:
        reduced = lax.psum([piece for group in range(groups) for piece in encode(group)], "slc")
        gradients = [gradient((piece,), index) for index, piece in enumerate(reduced)]
    by_class = jnp.stack(
        [
            jnp.concatenate(gradients[group * PARTS : (group + 1) * PARTS], axis=1)
            for group in range(groups)
        ],
        axis=1,
    )[:, :, :length]
    if whole_classes:
        local = by_class.reshape(per_device, length)
    else:
        local = lax.dynamic_slice_in_dim(by_class[0], first, per_device, axis=0)
    return sum_over_replicas(local)


def solution(mesh):
    placed = (
        P(("grp", "vol"), "slc", None, None, None),
        P(("grp", "coil"), "slc", None, None, None),
        P(("grp", "vol"), "slc", "coil", None, None, None),
        P("slc"),
        P("slc", None),
        P(),
    )
    return jax.shard_map(
        body, mesh=mesh, in_specs=placed, out_specs=P(("grp", "slc"), None), check_vma=False
    )
```

```python
import functools
import math

import jax
import jax.numpy as jnp
import ml_dtypes
import numpy as np
from jax import lax
from jax.experimental import pallas as pl
from jax.experimental.pallas import tpu as pltpu
from jax.sharding import PartitionSpec as P

MB = 8
ROW_TILE = 16
LANE_TILE = 128
PARTS = 2
VMEM_BYTES = 24 * 1024 * 1024


def round_up(value, multiple):
    return -(-value // multiple) * multiple


def fourier_tables(length):
    positions = np.arange(length, dtype=np.int32)
    product = positions[:, None] * positions[None, :] % length
    radians = np.float32(2.0 * math.pi / length) * product.astype(np.float32)
    factor = np.float32(1.0 / math.sqrt(length))
    return (
        (np.cos(radians) * factor).astype(ml_dtypes.bfloat16),
        (-np.sin(radians) * factor).astype(ml_dtypes.bfloat16),
    )


def dft_matrices(length, rows):
    cos_table, sin_table = fourier_tables(length)
    cosine, sine = cos_table.astype(np.float64), sin_table.astype(np.float64)
    left_re = np.zeros((2 * rows + 8, length), np.float64)
    left_im = np.zeros((2 * rows + 8, length), np.float64)
    left_re[:length], left_re[rows : rows + length] = cosine, sine
    left_im[:length], left_im[rows : rows + length] = -sine, cosine
    gram_re = cosine.T @ cosine + sine.T @ sine
    gram_im = sine.T @ cosine - cosine.T @ sine
    gram = np.stack(
        [np.concatenate([gram_im, -gram_re], 1), np.concatenate([gram_re, gram_im], 1)]
    )
    adjoint = np.stack(
        [np.concatenate([-sine, -cosine], 1), np.concatenate([cosine, -sine], 1)]
    )
    left = np.stack([left_re, left_im])
    return tuple(part.astype(ml_dtypes.bfloat16) for part in (left, gram, adjoint))


def dot(left, right):
    return jnp.dot(left, right, preferred_element_type=jnp.float32)


def at_line_end():
    position = lax.axis_index("slc")
    return (position == 0) | (position == lax.axis_size("slc") - 1)


def start_all(copies):
    for copy in copies:
        copy.start()


def slice_copies(image_ref, map_ref, image_out, map_out, arrived, rows_of):
    vols, coils = image_ref.shape[0], map_ref.shape[0]
    return [
        pltpu.make_async_copy(
            image_ref.at[vol, row], image_out.at[vol, slot], arrived.at[slot, vol]
        )
        for slot, row in enumerate(rows_of)
        for vol in range(vols)
    ] + [
        pltpu.make_async_copy(
            map_ref.at[coil, row], map_out.at[coil, slot], arrived.at[slot, vols + coil]
        )
        for slot, row in enumerate(rows_of)
        for coil in range(coils)
    ]


def fetch_kernel(rows_of, *refs):
    if rows_of is None:
        rows_of, refs = [refs[0][1]], refs[1:]
    shift_ref, offset_ref, image_ref, map_ref, left_ref = refs[:5]
    image_out, map_out, left_out, phase_out, ends_out = refs[5:10]
    shift, offset, angle, arrived, small = refs[10:]
    copies = slice_copies(image_ref, map_ref, image_out, map_out, arrived, rows_of)
    copies.append(pltpu.make_async_copy(left_ref, left_out, small.at[0]))
    early = [
        pltpu.make_async_copy(shift_ref, shift, small.at[1]),
        pltpu.make_async_copy(offset_ref, offset, small.at[2]),
    ]
    start_all(early)
    start_all(copies)
    ends_out[...] = jnp.where(at_line_end(), 1.0, 0.0) * jnp.ones_like(ends_out)
    for copy in early:
        copy.wait()
    per_device, length = offset.shape
    lines = lax.broadcasted_iota(jnp.int32, (1, length), 1) - length // 2
    angle[...] = jnp.zeros_like(angle)
    for row in range(per_device):
        turns = (shift[row] * lines) & (MB - 1)
        angle[row : row + 1, :length] = (
            2.0 * math.pi / MB * turns.astype(jnp.float32) + offset[row : row + 1, :]
        )
    phase_out[:, :per_device] = jnp.cos(angle[...]).T
    phase_out[:, per_device:] = jnp.sin(angle[...]).T
    for copy in copies:
        copy.wait()


def encode_kernel(slots, group, rows_of, next_rows, *refs):
    whole_classes = rows_of is not None
    if not whole_classes:
        place_ref, refs = refs[0], refs[1:]
        next_rows = next_rows and [place_ref[2]]
    phase_ref, image, coil_map, left_ref, kspace_ref = refs[:5]
    order_ref, gram_ref, adjoint_ref, image_ref, map_ref = refs[5:10]
    refs = refs[10:]
    shifted, refs = refs[0], refs[1:]
    out_refs, refs = refs[:PARTS], refs[PARTS:]
    if next_rows:
        next_image, next_map, refs = refs[0], refs[1], refs[2:]
    total, gram, adjoint, order, arrived, small = refs
    vols, coils, length = image.shape[0], coil_map.shape[0], image.shape[-1]
    _, rows, lanes = shifted.shape
    order_copy = pltpu.make_async_copy(order_ref, order, small.at[0])
    gram_copy = pltpu.make_async_copy(gram_ref, gram, small.at[1])
    owner_copies = [pltpu.make_async_copy(adjoint_ref, adjoint, small.at[2])]
    next_copies = []
    if next_rows:
        next_copies = slice_copies(image_ref, map_ref, next_image, next_map, arrived, next_rows)
    start_all([order_copy, gram_copy, *next_copies])

    if lanes > vols * coils * 2 * length:
        last = slice(lanes - LANE_TILE, lanes)
        total[:, last] = jnp.zeros((rows, LANE_TILE), jnp.float32)
        for slot in range(slots):
            shifted[slot, :, last] = jnp.zeros((rows, LANE_TILE), jnp.bfloat16)
    sums = [None] * (vols * coils)
    for slot in range(slots):
        if whole_classes:
            column = rows_of[slot]
            half = phase_ref.shape[1] // 2
            cosine = phase_ref[:rows, column : column + 1]
            sine = phase_ref[:rows, half + column : half + column + 1]
        else:
            cosine, sine = phase_ref[:rows, :1], phase_ref[:rows, 1:]
        for vol in range(vols):
            image_re = image[vol, slot, 0].astype(jnp.float32)
            image_im = image[vol, slot, 1].astype(jnp.float32)
            for coil in range(coils):
                place = vol * coils + coil
                base = place * 2 * length
                map_re = coil_map[coil, slot, 0].astype(jnp.float32)
                map_im = coil_map[coil, slot, 1].astype(jnp.float32)
                coil_re = (map_re * image_re - map_im * image_im).astype(jnp.bfloat16)
                coil_im = (map_re * image_im + map_im * image_re).astype(jnp.bfloat16)
                partly = dot(left_ref[0, : 2 * rows], coil_re) + dot(
                    left_ref[1, : 2 * rows], coil_im
                )
                part_re, part_im = partly[:rows], partly[rows:]
                shift_re = part_re * cosine - part_im * sine
                shift_im = part_re * sine + part_im * cosine
                shifted[slot, :, base : base + length] = shift_re.astype(jnp.bfloat16)
                shifted[slot, :, base + length : base + 2 * length] = shift_im.astype(
                    jnp.bfloat16
                )
                if slot > 0:
                    shift_re, shift_im = sums[place][0] + shift_re, sums[place][1] + shift_im
                sums[place] = (shift_re, shift_im)
        if slot == 0:
            order_copy.wait()
            owner = order[group] == lax.axis_index("slc")

            @pl.when(owner)
            def _():
                start_all(owner_copies)

    gram_copy.wait()
    for place, (sum_re, sum_im) in enumerate(sums):
        mixed = dot(sum_re.astype(jnp.bfloat16), gram[0]) + dot(
            sum_im.astype(jnp.bfloat16), gram[1]
        )
        if not whole_classes:
            mixed = jnp.where(place_ref[0] > 0, mixed, 0.0)
        total[:, place * 2 * length : (place + 1) * 2 * length] = mixed

    @pl.when(owner)
    def _():
        for copy in owner_copies:
            copy.wait()
        for vol in range(vols):
            for coil in range(coils):
                place = vol * coils + coil
                measured = dot(kspace_ref[vol, 0, coil, 0], adjoint[0]) + dot(
                    kspace_ref[vol, 0, coil, 1], adjoint[1]
                )
                total[:length, place * 2 * length : (place + 1) * 2 * length] -= measured

    part = rows // PARTS
    for index, out_ref in enumerate(out_refs):
        out_ref[...] = total[index * part : (index + 1) * part, :].astype(jnp.bfloat16)
    for copy in next_copies:
        copy.wait()


def gradient_kernel(index, factor, on_line, *refs):
    term_refs, shifted_ref, out_ref = refs[:-2], refs[-2], refs[-1]
    slots, rows, lanes = shifted_ref.shape
    part = rows // PARTS
    terms = [ref[...].astype(jnp.float32) for ref in term_refs]
    residual = terms[0]
    if on_line:
        near, across, rest = terms[1:]
        residual += jnp.where(at_line_end(), rest, near + across)
    for slot in range(slots):
        product = residual * shifted_ref[slot, index * part : (index + 1) * part, :].astype(
            jnp.float32
        )
        tiles = [product[:, at : at + LANE_TILE] for at in range(0, lanes, LANE_TILE)]
        folded = functools.reduce(lambda a, b: a + b, tiles)
        out_ref[slot : slot + 1, :] = factor * jnp.sum(folded.T, axis=0, keepdims=True)


def after(value, *earlier):
    return lax.optimization_barrier((value, *earlier))[0]


def sum_over_replicas(value):
    axes = ("coil", "vol")
    if any(lax.axis_size(axis) != 2 for axis in axes):
        return lax.psum(value, axes)
    swapped = [
        lax.ppermute(value, axes, [(index, index ^ mask) for index in range(4)])
        for mask in (1, 2, 3)
    ]
    return (value + swapped[0]) + (swapped[1] + swapped[2])


def line_of_four(encode, gradient, groups, ends):
    cores = lax.axis_size("vol")
    count = groups * PARTS
    outer_pairs = [(0, 1), (1, 0), (2, 3), (3, 2)]
    inner_pairs = [
        (source * cores + core, target * cores + (core ^ 1 if swap and cores % 2 == 0 else core))
        for source, target, swap in ((0, 0, True), (1, 2, False), (2, 1, False), (3, 3, True))
        for core in range(cores)
    ]

    def outer(value):
        return lax.ppermute(value, "slc", outer_pairs)

    def inner(value):
        return lax.ppermute(value, ("slc", "vol"), inner_pairs)

    own = [*encode(0)]
    near, across, gradients, encoded = [outer(own[0])], [], [], 1

    def encode_more(wanted, *earlier):
        nonlocal encoded
        while len(own) < min(wanted, count):
            own.extend(encode(encoded, *earlier))
            encoded += 1

    def gradient_of(piece, *earlier):
        terms = (own[piece], near[piece], across[piece], near[piece + 3])
        gradients.append(gradient((after(terms[0], *earlier), *terms[1:]), piece))

    encode_more(3)
    near.append(outer(after(own[1], own[2])))
    encode_more(5)
    latest = own[4]
    for step in range(count):
        half = own[step] + after(near[step], latest)
        across.append(inner(half))
        payload = own[step + 2] if step + 2 < count else None
        if step >= 1:
            others = own[step - 1] + after(across[step - 1], half)
            payload = others if payload is None else jnp.where(ends > 0, payload, others)
        else:
            payload = after(payload, near[step])
        near.append(outer(payload))
        latest = payload
        if len(own) < min(step + 7, count):
            encode_more(step + 7, payload)
            latest = own[-1]
        if step >= 3:
            gradient_of(step - 3, payload)
    last = own[count - 1] + after(across[count - 1], latest, near[count])
    near.append(outer(last))
    for piece in range(count - 3, count):
        gradient_of(piece, last)
    return gradients


def body(images, coil_maps, kspace, shift_index, phase_offset, group_order):
    vols, per_device, _, _, length = images.shape
    coils = coil_maps.shape[0]
    groups = lax.axis_size("slc")
    rows = round_up(length, ROW_TILE * PARTS)
    places = vols * coils
    lanes = round_up(places * 2 * length, LANE_TILE)
    whole_classes = per_device % groups == 0
    slots = max(1, per_device // groups)
    tables = dft_matrices(length, rows)
    factor = 1.0 / (coils * lax.axis_size("coil") * vols * lax.axis_size("vol"))
    first = (lax.axis_index("slc") * per_device) % groups
    on_line = whole_classes and groups == 4
    in_vmem = pl.BlockSpec(memory_space=pltpu.VMEM)
    in_smem = pl.BlockSpec(memory_space=pltpu.SMEM)
    in_place = pl.BlockSpec(memory_space=pl.ANY)

    def in_hbm(array):
        return pltpu.with_memory_space_constraint(jnp.asarray(array), pltpu.HBM)

    def rows_of_class(group):
        return [slot * groups + group for slot in range(slots)] if whole_classes else None

    def place_of(group):
        if whole_classes:
            return ()
        held = [(group + step - first, per_device) for step in range(2)]
        inside = [(within >= 0) & (within < size) for within, size in held]
        rows_held = [jnp.where(yes, held[i][0], 0) for i, yes in enumerate(inside)]
        return (jnp.stack([inside[0], rows_held[0], rows_held[1]]).astype(jnp.int32),)

    left, gram, adjoint = (in_hbm(table) for table in tables)
    lying = [in_hbm(jnp.swapaxes(array, -3, -2)) for array in (images, coil_maps)]
    order = in_hbm(group_order)
    raw_shapes = [
        jax.ShapeDtypeStruct((count, slots, length, 2, length), jnp.bfloat16)
        for count in (vols, coils)
    ]
    scalar_specs = [] if whole_classes else [in_smem]
    padded_rows = round_up(rows, LANE_TILE)
    slice_semaphores = pltpu.SemaphoreType.DMA((slots, vols + coils))
    *raw, left, phases, ends = pl.pallas_call(
        functools.partial(fetch_kernel, rows_of_class(0)),
        in_specs=scalar_specs + [in_place] * 5,
        out_specs=[in_vmem] * 5,
        out_shape=raw_shapes
        + [
            jax.ShapeDtypeStruct(left.shape, left.dtype),
            jax.ShapeDtypeStruct((padded_rows, 2 * per_device), jnp.float32),
            jax.ShapeDtypeStruct((1, lanes), jnp.float32),
        ],
        scratch_shapes=[
            pltpu.SMEM((per_device,), jnp.int32),
            pltpu.VMEM((per_device, length), jnp.float32),
            pltpu.VMEM((per_device, padded_rows), jnp.float32),
            slice_semaphores,
            pltpu.SemaphoreType.DMA((3,)),
        ],
        compiler_params=pltpu.CompilerParams(vmem_limit_bytes=VMEM_BYTES),
        name="fetch",
    )(*place_of(0), in_hbm(shift_index), in_hbm(phase_offset), *lying, left)

    shifted = []

    def encode(group, *earlier):
        image, coil_map = (jnp.swapaxes(array, -3, -2) for array in raw)
        has_next = group + 1 < groups
        place, group_phases = place_of(group), phases
        if not whole_classes:
            group_phases = jnp.take(
                phases, jnp.stack([place[0][1], place[0][1] + per_device]), axis=1
            )
        if earlier:
            image = after(image, *earlier)
        outputs = pl.pallas_call(
            functools.partial(
                encode_kernel,
                slots,
                group,
                rows_of_class(group),
                (rows_of_class(group + 1) or [0]) if has_next else None,
            ),
            in_specs=scalar_specs + [in_vmem] * 5 + [in_place] * 5,
            out_specs=[in_vmem] * (1 + PARTS + 2 * has_next),
            out_shape=[jax.ShapeDtypeStruct((slots, rows, lanes), jnp.bfloat16)]
            + [jax.ShapeDtypeStruct((rows // PARTS, lanes), jnp.bfloat16)] * PARTS
            + raw_shapes * has_next,
            scratch_shapes=[
                pltpu.VMEM((rows, lanes), jnp.float32),
                pltpu.VMEM(gram.shape, jnp.bfloat16),
                pltpu.VMEM(adjoint.shape, jnp.bfloat16),
                pltpu.SMEM((groups,), jnp.int32),
                slice_semaphores,
                pltpu.SemaphoreType.DMA((3,)),
            ],
            compiler_params=pltpu.CompilerParams(vmem_limit_bytes=VMEM_BYTES),
            cost_estimate=pl.CostEstimate(
                flops=places * (slots + 1) * 16 * length**3,
                bytes_accessed=6_000_000,
                transcendentals=0,
            ),
            name="encode",
        )(
            *place,
            group_phases,
            image,
            coil_map,
            left,
            kspace,
            order,
            gram,
            adjoint,
            *lying,
        )
        raw[:] = outputs[1 + PARTS :]
        shifted.append(outputs[0])
        return outputs[1 : 1 + PARTS]

    def gradient(terms, piece):
        group, index = divmod(piece, PARTS)
        return pl.pallas_call(
            functools.partial(gradient_kernel, index, factor, on_line),
            out_shape=jax.ShapeDtypeStruct((slots, rows // PARTS), jnp.float32),
            compiler_params=pltpu.CompilerParams(vmem_limit_bytes=VMEM_BYTES),
            cost_estimate=pl.CostEstimate(
                flops=places * slots * 4 * length**2, bytes_accessed=1_500_000, transcendentals=0
            ),
            name="gradient",
        )(*terms, shifted[group])

    if on_line:
        gradients = line_of_four(encode, gradient, groups, ends)
    else:
        reduced = lax.psum([piece for group in range(groups) for piece in encode(group)], "slc")
        gradients = [gradient((piece,), index) for index, piece in enumerate(reduced)]
    by_class = jnp.stack(
        [
            jnp.concatenate(gradients[group * PARTS : (group + 1) * PARTS], axis=1)
            for group in range(groups)
        ],
        axis=1,
    )[:, :, :length]
    if whole_classes:
        local = by_class.reshape(per_device, length)
    else:
        local = lax.dynamic_slice_in_dim(by_class[0], first, per_device, axis=0)
    return sum_over_replicas(local)


def solution(mesh):
    placed = (
        P(("grp", "vol"), "slc", None, None, None),
        P(("grp", "coil"), "slc", None, None, None),
        P(("grp", "vol"), "slc", "coil", None, None, None),
        P("slc"),
        P("slc", None),
        P(),
    )
    return jax.shard_map(
        body, mesh=mesh, in_specs=placed, out_specs=P(("grp", "slc"), None), check_vma=False
    )
```

```python
import functools
import math

import jax
import jax.numpy as jnp
import ml_dtypes
import numpy as np
from jax import lax
from jax.experimental import pallas as pl
from jax.experimental.pallas import tpu as pltpu
from jax.sharding import PartitionSpec as P

MB = 8
ROW_TILE = 16
LANE_TILE = 128
PARTS = 2
VMEM_BYTES = 24 * 1024 * 1024


def round_up(value, multiple):
    return -(-value // multiple) * multiple


def fourier_tables(length):
    positions = np.arange(length, dtype=np.int32)
    product = positions[:, None] * positions[None, :] % length
    radians = np.float32(2.0 * math.pi / length) * product.astype(np.float32)
    factor = np.float32(1.0 / math.sqrt(length))
    return (
        (np.cos(radians) * factor).astype(ml_dtypes.bfloat16),
        (-np.sin(radians) * factor).astype(ml_dtypes.bfloat16),
    )


def dft_matrices(length, rows):
    cos_table, sin_table = fourier_tables(length)
    cosine, sine = cos_table.astype(np.float64), sin_table.astype(np.float64)
    left_re = np.zeros((2 * rows + 8, length), np.float64)
    left_im = np.zeros((2 * rows + 8, length), np.float64)
    left_re[:length], left_re[rows : rows + length] = cosine, sine
    left_im[:length], left_im[rows : rows + length] = -sine, cosine
    gram_re = cosine.T @ cosine + sine.T @ sine
    gram_im = sine.T @ cosine - cosine.T @ sine
    gram = np.stack(
        [np.concatenate([gram_im, -gram_re], 1), np.concatenate([gram_re, gram_im], 1)]
    )
    adjoint = np.stack(
        [np.concatenate([-sine, -cosine], 1), np.concatenate([cosine, -sine], 1)]
    )
    left = np.stack([left_re, left_im])
    return tuple(part.astype(ml_dtypes.bfloat16) for part in (left, gram, adjoint))


def dot(left, right):
    return jnp.dot(left, right, preferred_element_type=jnp.float32)


def at_line_end():
    position = lax.axis_index("slc")
    return (position == 0) | (position == lax.axis_size("slc") - 1)


def start_all(copies):
    for copy in copies:
        copy.start()


def slice_copies(image_ref, map_ref, image_out, map_out, arrived, rows_of):
    vols, coils = image_ref.shape[0], map_ref.shape[0]
    return [
        pltpu.make_async_copy(
            image_ref.at[vol, row], image_out.at[vol, slot], arrived.at[slot, vol]
        )
        for slot, row in enumerate(rows_of)
        for vol in range(vols)
    ] + [
        pltpu.make_async_copy(
            map_ref.at[coil, row], map_out.at[coil, slot], arrived.at[slot, vols + coil]
        )
        for slot, row in enumerate(rows_of)
        for coil in range(coils)
    ]


def fetch_kernel(rows_of, *refs):
    if rows_of is None:
        rows_of, refs = [refs[0][1]], refs[1:]
    shift_ref, offset_ref, image_ref, map_ref, left_ref = refs[:5]
    image_out, map_out, left_out, phase_out, ends_out = refs[5:10]
    shift, offset, angle, arrived, small = refs[10:]
    copies = slice_copies(image_ref, map_ref, image_out, map_out, arrived, rows_of)
    copies.append(pltpu.make_async_copy(left_ref, left_out, small.at[0]))
    early = [
        pltpu.make_async_copy(shift_ref, shift, small.at[1]),
        pltpu.make_async_copy(offset_ref, offset, small.at[2]),
    ]
    start_all(early)
    start_all(copies)
    ends_out[...] = jnp.where(at_line_end(), 1.0, 0.0) * jnp.ones_like(ends_out)
    for copy in early:
        copy.wait()
    per_device, length = offset.shape
    lines = lax.broadcasted_iota(jnp.int32, (1, length), 1) - length // 2
    angle[...] = jnp.zeros_like(angle)
    for row in range(per_device):
        turns = (shift[row] * lines) & (MB - 1)
        angle[row : row + 1, :length] = (
            2.0 * math.pi / MB * turns.astype(jnp.float32) + offset[row : row + 1, :]
        )
    phase_out[:, :per_device] = jnp.cos(angle[...]).T
    phase_out[:, per_device:] = jnp.sin(angle[...]).T
    for copy in copies:
        copy.wait()


def encode_kernel(slots, group, rows_of, next_rows, *refs):
    whole_classes = rows_of is not None
    if not whole_classes:
        place_ref, refs = refs[0], refs[1:]
        next_rows = next_rows and [place_ref[2]]
    phase_ref, image, coil_map, left_ref, kspace_ref = refs[:5]
    order_ref, gram_ref, adjoint_ref, image_ref, map_ref = refs[5:10]
    refs = refs[10:]
    shifted, refs = refs[0], refs[1:]
    out_refs, refs = refs[:PARTS], refs[PARTS:]
    if next_rows:
        next_image, next_map, refs = refs[0], refs[1], refs[2:]
    total, gram, adjoint, order, arrived, small = refs
    vols, coils, length = image.shape[0], coil_map.shape[0], image.shape[-1]
    _, rows, lanes = shifted.shape
    order_copy = pltpu.make_async_copy(order_ref, order, small.at[0])
    gram_copy = pltpu.make_async_copy(gram_ref, gram, small.at[1])
    owner_copies = [pltpu.make_async_copy(adjoint_ref, adjoint, small.at[2])]
    next_copies = []
    if next_rows:
        next_copies = slice_copies(image_ref, map_ref, next_image, next_map, arrived, next_rows)
    start_all([order_copy, gram_copy, *owner_copies, *next_copies])

    if lanes > vols * coils * 2 * length:
        last = slice(lanes - LANE_TILE, lanes)
        total[:, last] = jnp.zeros((rows, LANE_TILE), jnp.float32)
        for slot in range(slots):
            shifted[slot, :, last] = jnp.zeros((rows, LANE_TILE), jnp.bfloat16)
    sums = [None] * (vols * coils)
    for slot in range(slots):
        if whole_classes:
            column = rows_of[slot]
            half = phase_ref.shape[1] // 2
            cosine = phase_ref[:rows, column : column + 1]
            sine = phase_ref[:rows, half + column : half + column + 1]
        else:
            cosine, sine = phase_ref[:rows, :1], phase_ref[:rows, 1:]
        for vol in range(vols):
            image_re = image[vol, slot, 0].astype(jnp.float32)
            image_im = image[vol, slot, 1].astype(jnp.float32)
            for coil in range(coils):
                place = vol * coils + coil
                base = place * 2 * length
                map_re = coil_map[coil, slot, 0].astype(jnp.float32)
                map_im = coil_map[coil, slot, 1].astype(jnp.float32)
                coil_re = (map_re * image_re - map_im * image_im).astype(jnp.bfloat16)
                coil_im = (map_re * image_im + map_im * image_re).astype(jnp.bfloat16)
                partly = dot(left_ref[0, : 2 * rows], coil_re) + dot(
                    left_ref[1, : 2 * rows], coil_im
                )
                part_re, part_im = partly[:rows], partly[rows:]
                shift_re = part_re * cosine - part_im * sine
                shift_im = part_re * sine + part_im * cosine
                shifted[slot, :, base : base + length] = shift_re.astype(jnp.bfloat16)
                shifted[slot, :, base + length : base + 2 * length] = shift_im.astype(
                    jnp.bfloat16
                )
                if slot > 0:
                    shift_re, shift_im = sums[place][0] + shift_re, sums[place][1] + shift_im
                sums[place] = (shift_re, shift_im)

    gram_copy.wait()
    for place, (sum_re, sum_im) in enumerate(sums):
        mixed = dot(sum_re.astype(jnp.bfloat16), gram[0]) + dot(
            sum_im.astype(jnp.bfloat16), gram[1]
        )
        if not whole_classes:
            mixed = jnp.where(place_ref[0] > 0, mixed, 0.0)
        total[:, place * 2 * length : (place + 1) * 2 * length] = mixed

    for copy in (order_copy, *owner_copies):
        copy.wait()

    @pl.when(order[group] == lax.axis_index("slc"))
    def _():
        for vol in range(vols):
            for coil in range(coils):
                place = vol * coils + coil
                measured = dot(kspace_ref[vol, 0, coil, 0], adjoint[0]) + dot(
                    kspace_ref[vol, 0, coil, 1], adjoint[1]
                )
                total[:length, place * 2 * length : (place + 1) * 2 * length] -= measured

    part = rows // PARTS
    for index, out_ref in enumerate(out_refs):
        out_ref[...] = total[index * part : (index + 1) * part, :].astype(jnp.bfloat16)
    for copy in next_copies:
        copy.wait()


def gradient_kernel(index, factor, on_line, *refs):
    term_refs, shifted_ref, out_ref = refs[:-2], refs[-2], refs[-1]
    slots, rows, lanes = shifted_ref.shape
    part = rows // PARTS
    terms = [ref[...].astype(jnp.float32) for ref in term_refs]
    residual = terms[0]
    if on_line:
        near, across, rest = terms[1:]
        residual += jnp.where(at_line_end(), rest, near + across)
    for slot in range(slots):
        product = residual * shifted_ref[slot, index * part : (index + 1) * part, :].astype(
            jnp.float32
        )
        tiles = [product[:, at : at + LANE_TILE] for at in range(0, lanes, LANE_TILE)]
        folded = functools.reduce(lambda a, b: a + b, tiles)
        out_ref[slot : slot + 1, :] = factor * jnp.sum(folded.T, axis=0, keepdims=True)


def after(value, *earlier):
    return lax.optimization_barrier((value, *earlier))[0]


def sum_over_replicas(value):
    axes = ("coil", "vol")
    if any(lax.axis_size(axis) != 2 for axis in axes):
        return lax.psum(value, axes)
    swapped = [
        lax.ppermute(value, axes, [(index, index ^ mask) for index in range(4)])
        for mask in (1, 2, 3)
    ]
    return (value + swapped[0]) + (swapped[1] + swapped[2])


def line_of_four(encode, gradient, groups, ends):
    cores = lax.axis_size("vol")
    count = groups * PARTS
    outer_pairs = [(0, 1), (1, 0), (2, 3), (3, 2)]
    inner_pairs = [
        (source * cores + core, target * cores + (core ^ 1 if swap and cores % 2 == 0 else core))
        for source, target, swap in ((0, 0, True), (1, 2, False), (2, 1, False), (3, 3, True))
        for core in range(cores)
    ]

    def outer(value):
        return lax.ppermute(value, "slc", outer_pairs)

    def inner(value):
        return lax.ppermute(value, ("slc", "vol"), inner_pairs)

    own = [*encode(0)]
    near, across, gradients, encoded = [outer(own[0])], [], [], 1

    def encode_more(wanted, *earlier):
        nonlocal encoded
        while len(own) < min(wanted, count):
            own.extend(encode(encoded, *earlier))
            encoded += 1

    def gradient_of(piece, *earlier):
        terms = (own[piece], near[piece], across[piece], near[piece + 3])
        gradients.append(gradient((after(terms[0], *earlier), *terms[1:]), piece))

    encode_more(3)
    near.append(outer(after(own[1], own[2])))
    encode_more(5)
    latest = own[4]
    for step in range(count):
        half = own[step] + after(near[step], latest)
        across.append(inner(half))
        payload = own[step + 2] if step + 2 < count else None
        if step >= 1:
            others = own[step - 1] + after(across[step - 1], half)
            payload = others if payload is None else jnp.where(ends > 0, payload, others)
        else:
            payload = after(payload, near[step])
        near.append(outer(payload))
        latest = payload
        if len(own) < min(step + 7, count):
            encode_more(step + 7, payload)
            latest = own[-1]
        if step >= 3:
            gradient_of(step - 3, payload)
    last = own[count - 1] + after(across[count - 1], latest, near[count])
    near.append(outer(last))
    for piece in range(count - 3, count):
        gradient_of(piece, last)
    return gradients


def body(images, coil_maps, kspace, shift_index, phase_offset, group_order):
    vols, per_device, _, _, length = images.shape
    coils = coil_maps.shape[0]
    groups = lax.axis_size("slc")
    rows = round_up(length, ROW_TILE * PARTS)
    places = vols * coils
    lanes = round_up(places * 2 * length, LANE_TILE)
    whole_classes = per_device % groups == 0
    slots = max(1, per_device // groups)
    tables = dft_matrices(length, rows)
    factor = 1.0 / (coils * lax.axis_size("coil") * vols * lax.axis_size("vol"))
    first = (lax.axis_index("slc") * per_device) % groups
    on_line = whole_classes and groups == 4
    in_vmem = pl.BlockSpec(memory_space=pltpu.VMEM)
    in_smem = pl.BlockSpec(memory_space=pltpu.SMEM)
    in_place = pl.BlockSpec(memory_space=pl.ANY)

    def in_hbm(array):
        return pltpu.with_memory_space_constraint(jnp.asarray(array), pltpu.HBM)

    def rows_of_class(group):
        return [slot * groups + group for slot in range(slots)] if whole_classes else None

    def place_of(group):
        if whole_classes:
            return ()
        held = [(group + step - first, per_device) for step in range(2)]
        inside = [(within >= 0) & (within < size) for within, size in held]
        rows_held = [jnp.where(yes, held[i][0], 0) for i, yes in enumerate(inside)]
        return (jnp.stack([inside[0], rows_held[0], rows_held[1]]).astype(jnp.int32),)

    left, gram, adjoint = (in_hbm(table) for table in tables)
    lying = [in_hbm(jnp.swapaxes(array, -3, -2)) for array in (images, coil_maps)]
    order = in_hbm(group_order)
    raw_shapes = [
        jax.ShapeDtypeStruct((count, slots, length, 2, length), jnp.bfloat16)
        for count in (vols, coils)
    ]
    scalar_specs = [] if whole_classes else [in_smem]
    padded_rows = round_up(rows, LANE_TILE)
    slice_semaphores = pltpu.SemaphoreType.DMA((slots, vols + coils))
    *raw, left, phases, ends = pl.pallas_call(
        functools.partial(fetch_kernel, rows_of_class(0)),
        in_specs=scalar_specs + [in_place] * 5,
        out_specs=[in_vmem] * 5,
        out_shape=raw_shapes
        + [
            jax.ShapeDtypeStruct(left.shape, left.dtype),
            jax.ShapeDtypeStruct((padded_rows, 2 * per_device), jnp.float32),
            jax.ShapeDtypeStruct((1, lanes), jnp.float32),
        ],
        scratch_shapes=[
            pltpu.SMEM((per_device,), jnp.int32),
            pltpu.VMEM((per_device, length), jnp.float32),
            pltpu.VMEM((per_device, padded_rows), jnp.float32),
            slice_semaphores,
            pltpu.SemaphoreType.DMA((3,)),
        ],
        compiler_params=pltpu.CompilerParams(vmem_limit_bytes=VMEM_BYTES),
        name="fetch",
    )(*place_of(0), in_hbm(shift_index), in_hbm(phase_offset), *lying, left)

    shifted = []

    def encode(group, *earlier):
        image, coil_map = (jnp.swapaxes(array, -3, -2) for array in raw)
        has_next = group + 1 < groups
        place, group_phases = place_of(group), phases
        if not whole_classes:
            group_phases = jnp.take(
                phases, jnp.stack([place[0][1], place[0][1] + per_device]), axis=1
            )
        if earlier:
            image = after(image, *earlier)
        outputs = pl.pallas_call(
            functools.partial(
                encode_kernel,
                slots,
                group,
                rows_of_class(group),
                (rows_of_class(group + 1) or [0]) if has_next else None,
            ),
            in_specs=scalar_specs + [in_vmem] * 5 + [in_place] * 5,
            out_specs=[in_vmem] * (1 + PARTS + 2 * has_next),
            out_shape=[jax.ShapeDtypeStruct((slots, rows, lanes), jnp.bfloat16)]
            + [jax.ShapeDtypeStruct((rows // PARTS, lanes), jnp.bfloat16)] * PARTS
            + raw_shapes * has_next,
            scratch_shapes=[
                pltpu.VMEM((rows, lanes), jnp.float32),
                pltpu.VMEM(gram.shape, jnp.bfloat16),
                pltpu.VMEM(adjoint.shape, jnp.bfloat16),
                pltpu.SMEM((groups,), jnp.int32),
                slice_semaphores,
                pltpu.SemaphoreType.DMA((3,)),
            ],
            compiler_params=pltpu.CompilerParams(vmem_limit_bytes=VMEM_BYTES),
            cost_estimate=pl.CostEstimate(
                flops=places * (slots + 1) * 16 * length**3,
                bytes_accessed=6_000_000,
                transcendentals=0,
            ),
            name="encode",
        )(
            *place,
            group_phases,
            image,
            coil_map,
            left,
            kspace,
            order,
            gram,
            adjoint,
            *lying,
        )
        raw[:] = outputs[1 + PARTS :]
        shifted.append(outputs[0])
        return outputs[1 : 1 + PARTS]

    def gradient(terms, piece):
        group, index = divmod(piece, PARTS)
        return pl.pallas_call(
            functools.partial(gradient_kernel, index, factor, on_line),
            out_shape=jax.ShapeDtypeStruct((slots, rows // PARTS), jnp.float32),
            compiler_params=pltpu.CompilerParams(vmem_limit_bytes=VMEM_BYTES),
            cost_estimate=pl.CostEstimate(
                flops=places * slots * 4 * length**2, bytes_accessed=1_500_000, transcendentals=0
            ),
            name="gradient",
        )(*terms, shifted[group])

    if on_line:
        gradients = line_of_four(encode, gradient, groups, ends)
    else:
        reduced = lax.psum([piece for group in range(groups) for piece in encode(group)], "slc")
        gradients = [gradient((piece,), index) for index, piece in enumerate(reduced)]
    by_class = jnp.stack(
        [
            jnp.concatenate(gradients[group * PARTS : (group + 1) * PARTS], axis=1)
            for group in range(groups)
        ],
        axis=1,
    )[:, :, :length]
    if whole_classes:
        local = by_class.reshape(per_device, length)
    else:
        local = lax.dynamic_slice_in_dim(by_class[0], first, per_device, axis=0)
    return sum_over_replicas(local)


def solution(mesh):
    placed = (
        P(("grp", "vol"), "slc", None, None, None),
        P(("grp", "coil"), "slc", None, None, None),
        P(("grp", "vol"), "slc", "coil", None, None, None),
        P("slc"),
        P("slc", None),
        P(),
    )
    return jax.shard_map(
        body, mesh=mesh, in_specs=placed, out_specs=P(("grp", "slc"), None), check_vma=False
    )
```
